32 devices in a mesh: sensor: 4 (over x, core), space: 8 (over z, y).
Axes of the slice: x: 2, y: 2, z: 4, core: 2. Of those that a mesh axis runs over, the one named last changes fastest.
Arguments:
- forward_map: bfloat16 [16, 2, 1024, 2048], P(None, None, 'sensor', 'space'), may hold values from -1 to 1
- observed: float32 [16, 2, 1024, 128], P(None, None, 'sensor'), may hold values from -6 to 6
- noise_var: float32 [1024], P('sensor'), may hold values from 0.3 to 1.5
- prior_rows: bfloat16 [2048, 512], P('space'), may hold values from -2 to 14, as said below
- prior_scale: float32 [16], replicated, may hold values from 0.6 to 1.2
Outputs:
- multiplier: float32 [16, 2, 1024, 128], P(None, None, 'sensor')
- posterior: float32 [16, 2048, 2, 128], P('sensor', 'space')
The draws below stay inside these ranges and needn't reach their ends.
Inputs may be any that keep to these rules, and one draw needn't show every extreme that they name: `prior_rows`: each block of 512 rows is a symmetric matrix.
All inputs are finite; a program needn't handle non-finite values.
Results may differ from the reference program's by a relative error of at most 0.03.
Values may be sent and summed in bfloat16 or wider, within the bound.
No kernel may reach another device: no remote copies, remote signals or barrier semaphores. Data moves between devices by JAX's collectives and lax.ppermute only.
A program may use at most 64 MiB of HBM per device.

```python
import math
import jax
import jax.numpy as jnp
from jax import lax

NF = 16
S_DEV = 256
SCEN = 128
PBLK = 512
ITERS = 2
C_DEV = 256
SENSORS = 1024
CELLS = 2048
NB = 4
N_SENSOR = 4
N_SPACE = 8


def draw_prior_rows(key, part):
    raw = jax.random.normal(key, (NB, PBLK, PBLK), jnp.float32)
    symmetric = (raw + jnp.swapaxes(raw, 1, 2)) * (0.5 / math.sqrt(PBLK))
    identity = jnp.eye(PBLK, dtype=jnp.float32)
    blocks = 1.5 * identity[None, :, :] + symmetric
    blocks = jnp.clip(blocks, -2.0, 14.0)
    return blocks.reshape(NB * PBLK, PBLK).astype(jnp.bfloat16)


def draw_forward_map(key, part):
    ranks = jax.random.permutation(jax.random.fold_in(key, 11), SENSORS)
    fraction = ranks.astype(jnp.float32) / float(max(SENSORS - 1, 1))
    sensor_gain = math.sqrt(0.1) * jnp.exp(0.5 * math.log(20.0) * fraction)
    entry_scale = 1.0 / math.sqrt(2.0 * CELLS)

    def one_frequency(freq_index):
        freq_key = jax.random.fold_in(key, freq_index)
        values = jnp.clip(jax.random.normal(freq_key, (2, SENSORS, CELLS), jnp.float32), -4.0, 4.0)
        return (values * sensor_gain[None, :, None] * entry_scale).astype(jnp.bfloat16)
    return lax.map(one_frequency, jnp.arange(NF, dtype=jnp.int32))


def block_scale(stream_key, shape, shards, smallest, top_value):
    factor_of = 1.0
    for dim, blocks in shards:
        draws = jax.random.uniform(jax.random.fold_in(jax.random.fold_in(stream_key, 6), dim), (blocks,), jnp.float32, smallest / len(shards), top_value / len(shards))
        factor_of = factor_of * jnp.repeat(jnp.exp(draws), shape[dim] // blocks).reshape((-1,) + (1,) * (len(shape) - 1 - dim))
    return factor_of


def scatter_about(rng, dims, spread, bound, cuts=(), held_as=jnp.bfloat16):
    result = jax.random.normal(rng, dims, jnp.float32) * spread
    if len(cuts) > 0:
        result = block_scale(rng, dims, cuts, -0.22, 0.18) * result
    return jnp.clip(result, min=-bound, max=bound).astype(held_as)


def setup_inputs(seed: int = 0) -> dict:
    key_list = jax.random.split(jax.random.key(seed), 6)
    return {
        "forward_map": draw_forward_map(jax.random.fold_in(key_list[5], 71), 0),
        "observed": scatter_about(key_list[1], (NF, 2, SENSORS, SCEN), 1.0, 6.0, ((2, 4),), jnp.float32),
        "noise_var": jnp.clip(jnp.exp(math.log(1.5) - 1.60943787 * jax.random.uniform(key_list[2], (SENSORS,), jnp.float32) ** block_scale(key_list[2], (SENSORS,), ((0, 4),), -0.2, 0.2)), 0.3, 1.5),
        "prior_rows": draw_prior_rows(jax.random.fold_in(key_list[5], 71), 0),
        "prior_scale": jnp.clip(jnp.exp(jax.random.uniform(key_list[4], (NF,), jnp.float32, math.log(0.6), math.log(1.2))), 0.6, 1.2),
    }


relax_step = 0.25


def stack_sides(dual_b):
    real_part = dual_b[..., 0, :, :]
    imag_part = dual_b[..., 1, :, :]
    upper = jnp.concatenate([real_part, imag_part], -1)
    lower = jnp.concatenate([imag_part, -real_part], -1)
    return jnp.concatenate([upper, lower], -2)


def to_data(products, half, scenarios):
    upper = products[..., :half, :]
    lower = products[..., half:, :]
    real_part = upper[..., :scenarios] - lower[..., scenarios:]
    imag_part = upper[..., scenarios:] + lower[..., :scenarios]
    return jnp.stack([real_part, imag_part], -3)


def adjoint_full(forward_map, multiplier):
    dual_b = multiplier.astype(jnp.bfloat16)
    running = jnp.zeros((NF, CELLS, 2 * SCEN), jnp.float32)
    for sensor_group in range(N_SENSOR):
        first_row = sensor_group * S_DEV
        map_block = forward_map[:, :, first_row:first_row + S_DEV, :].reshape(NF, 2 * S_DEV, CELLS).astype(jnp.float32)
        right_sides = stack_sides(dual_b[:, :, first_row:first_row + S_DEV, :]).astype(jnp.float32)
        partial_sum = jnp.einsum("fkc,fkr->fcr", map_block, right_sides)
        running = running + partial_sum.astype(jnp.bfloat16).astype(jnp.float32)
    return running


def prior_full(adjoint_sum, prior_rows, prior_scale):
    rounded = adjoint_sum.astype(jnp.bfloat16).astype(jnp.float32).reshape(NF, NB, PBLK, 2 * SCEN)
    blocks = prior_rows.astype(jnp.float32).reshape(NB, PBLK, PBLK)
    prior_term = jnp.einsum("bij,fbjr->fbir", blocks, rounded) * prior_scale[:, None, None, None]
    return prior_term.reshape(NF, CELLS, 2 * SCEN)


def forward_full(forward_map, source_b):
    flat = forward_map.reshape(NF, 2 * SENSORS, CELLS)

    def add_group(group_index, running):
        offset = (group_index * C_DEV).astype(jnp.int32)
        map_piece = lax.dynamic_slice_in_dim(flat, offset, C_DEV, 2).astype(jnp.float32)
        source_piece = lax.dynamic_slice_in_dim(source_b, offset, C_DEV, 1).astype(jnp.float32)
        partial_sum = to_data(jnp.einsum("fkc,fcr->fkr", map_piece, source_piece), SENSORS, SCEN)
        return running + partial_sum.astype(jnp.bfloat16).astype(jnp.float32)

    start_value = jnp.zeros((NF, 2, SENSORS, SCEN), jnp.float32)
    return lax.fori_loop(0, N_SPACE, add_group, start_value)


def reference(forward_map, observed, noise_var, prior_rows, prior_scale):
    multiplier = relax_step * observed
    for iteration in range(ITERS):
        adjoint_sum = adjoint_full(forward_map, multiplier)
        prior_term = prior_full(adjoint_sum, prior_rows, prior_scale)
        predicted = forward_full(forward_map, prior_term.astype(jnp.bfloat16))
        multiplier = multiplier + relax_step * (observed - predicted - noise_var[:, None] * multiplier)
    adjoint_sum = adjoint_full(forward_map, multiplier)
    prior_term = prior_full(adjoint_sum, prior_rows, prior_scale)
    return multiplier, prior_term.reshape(NF, CELLS, 2, SCEN)
```

```python
import functools

import jax
import jax.numpy as jnp
from jax import lax
from jax.experimental import pallas as pl
from jax.experimental.pallas import tpu as pltpu
from jax.sharding import Mesh, PartitionSpec as P

ITERS = 2
relax_step = 0.25
LANES = 128
VMEM_LIMIT = 48 * 2**20


def turned(z):
    return jnp.concatenate([z[:, LANES:], -z[:, :LANES]], 1)


def turned_back(v):
    return jnp.concatenate([-v[:, LANES:], v[:, :LANES]], 1)


def dot(a, b):
    return jnp.dot(a, b, preferred_element_type=jnp.float32)


def dot_t(a, b):
    return lax.dot_general(a, b, (((0,), (0,)), ((), ())), preferred_element_type=jnp.float32)


class Rows:
    def __init__(self, sensors, cells, groups, quads, prior_width):
        sizes = {
            "map": 2 * sensors,
            "obs": sensors // quads,
            "prior": cells // groups * (prior_width // cells),
            "noise": 16,
        }
        self.size, self.at, total = sizes, {}, 0
        for name in sorted(sizes, key=lambda n: -sizes[n]):
            self.at[name] = total
            total += sizes[name]
        self.total = total

    def span(self, name):
        return slice(self.at[name], self.at[name] + self.size[name])


def pack_kernel(rows, place_ref, map_ref, obs_ref, prior_ref, noise_ref, out_ref):
    out_ref[0, rows.span("map"), :] = map_ref[0]
    obs = obs_ref[0].astype(jnp.bfloat16)
    out_ref[0, rows.span("obs"), :LANES] = obs[0]
    out_ref[0, rows.span("obs"), LANES:] = obs[1]
    share, width = prior_ref.shape
    cells = out_ref.shape[2]
    for part in range(width // cells):
        first = rows.at["prior"] + part * share
        out_ref[0, first:first + share, :] = prior_ref[:, part * cells:(part + 1) * cells]
    noise = noise_ref[...]
    high = noise.astype(jnp.bfloat16)
    low = (noise - high.astype(jnp.float32)).astype(jnp.bfloat16)
    out_ref[0, rows.span("noise"), :] = jnp.concatenate(
        [jnp.broadcast_to(high, (8, cells)), jnp.broadcast_to(low, (8, cells))], 0
    )


def pack(rows, forward_map, observed, noise_var, prior_rows, place, groups, quads):
    frequencies, halves, sensors, cells = forward_map.shape
    return pl.pallas_call(
        functools.partial(pack_kernel, rows),
        grid_spec=pltpu.PrefetchScalarGridSpec(
            num_scalar_prefetch=1,
            grid=(frequencies,),
            in_specs=[
                pl.BlockSpec((1, halves * sensors, cells), lambda f, place: (f, 0, 0)),
                pl.BlockSpec((1, halves, sensors // quads, LANES), lambda f, place: (f, 0, place[1], 0)),
                pl.BlockSpec((cells // groups, prior_rows.shape[1]), lambda f, place: (place[0], 0)),
                pl.BlockSpec((1, sensors), lambda f, place: (0, 0)),
            ],
            out_specs=pl.BlockSpec((1, rows.total, cells), lambda f, place: (f, 0, 0)),
        ),
        out_shape=jax.ShapeDtypeStruct((frequencies, rows.total, cells), jnp.bfloat16),
    )(place, forward_map.reshape(frequencies, halves * sensors, cells), observed, prior_rows, noise_var.reshape(1, sensors))


def step_kernel(stage, n_pred, sensors, scale_ref, map_ref, prior_ref, obs_ref, noise_ref, *rest):
    groups, per_block = map_ref.shape[:2]
    cells = map_ref.shape[3]
    quads = obs_ref.shape[1]
    share = prior_ref.shape[2] // per_block
    last = stage == ITERS
    preds, rest = rest[:n_pred], rest[n_pred:]
    held_ref = None
    if stage > 1:
        held_ref, rest = rest[0], rest[1:]
    if last:
        dual_ref, post_ref, z_ref = rest
    elif stage > 0:
        out_ref, next_ref, z_ref, total_ref = rest
    else:
        out_ref, z_ref, total_ref = rest
    block = pl.program_id(0)

    @pl.when(block == 0)
    def _():
        for g in range(groups):
            span = slice(g * sensors, (g + 1) * sensors)
            obs = jnp.concatenate([obs_ref[g, q] for q in range(quads)], 0).astype(jnp.float32)
            now = relax_step * obs if stage < 2 else held_ref[span, :]
            if stage > 0:
                both = noise_ref[g, 0].astype(jnp.float32)
                noise_row = both[0:1, :] + both[8:9, :]
                row = lax.broadcasted_iota(jnp.int32, (sensors, sensors), 0)
                col = lax.broadcasted_iota(jnp.int32, (sensors, sensors), 1)
                noise = jnp.sum(jnp.where(row == col, noise_row, 0.0), 1, keepdims=True)
                predicted = sum(p[span, :].astype(jnp.float32) for p in preds)
                now = now + relax_step * (obs - predicted - noise * now)
                if last:
                    dual_ref[span, :] = now.astype(jnp.bfloat16)
                elif stage > 0:
                    next_ref[span, :] = now
            z = now.astype(jnp.bfloat16)
            z_ref[0, span, :] = z
            z_ref[1, span, :] = turned(z)

    parts = []
    for q in range(per_block):
        u = jnp.zeros((cells, 2 * LANES), jnp.float32)
        for g in range(groups):
            span = slice(g * sensors, (g + 1) * sensors)
            u += dot_t(map_ref[g, q, :sensors, :], z_ref[0, span, :])
            u += dot_t(map_ref[g, q, sensors:, :], z_ref[1, span, :])
        parts.append(u.astype(jnp.bfloat16))
    ub = jnp.concatenate(parts, 0)
    scale = scale_ref[0]
    for q in range(per_block):
        row_blocks = [
            jnp.concatenate([prior_ref[g, q, p * share:(p + 1) * share, :] for p in range(per_block)], 1)
            for g in range(groups)
        ]
        term = dot(jnp.concatenate(row_blocks, 0), ub) * scale
        v = term.astype(jnp.bfloat16)
        if last:
            post_ref[q] = v
            continue
        w = turned_back(v)
        for g in range(groups):
            span = slice(g * sensors, (g + 1) * sensors)
            add = dot(map_ref[g, q, :sensors, :], v) + dot(map_ref[g, q, sensors:, :], w)
            if q == 0:
                total_ref[span, :] = jnp.where(block == 0, add, total_ref[span, :] + add)
            else:
                total_ref[span, :] += add
    if not last:

        @pl.when(block == pl.num_programs(0) - 1)
        def _():
            out_ref[...] = total_ref[...].astype(jnp.bfloat16)


def step(stage, rows, held, preds, multiplier, scale, sensors, per_block):
    groups, quads, _, cells = held.shape
    width = 2 * LANES
    whole = groups * sensors
    blocks = quads // per_block
    last = stage == ITERS

    def piece(name, inner):
        place = rows.at[name] // rows.size[name]
        if inner:
            return pl.BlockSpec((groups, per_block, rows.size[name], cells), lambda b: (0, b, place, 0))
        return pl.BlockSpec((groups, quads, rows.size[name], cells), lambda b: (0, 0, place, 0))

    fixed = pl.BlockSpec((whole, width), lambda b: (0, 0))
    operands = [scale, held, held, held, held] + list(preds)
    in_specs = [
        pl.BlockSpec(memory_space=pltpu.SMEM),
        piece("map", True),
        piece("prior", True),
        piece("obs", False),
        piece("noise", False),
    ] + [fixed] * len(preds)
    if stage > 1:
        operands.append(multiplier)
        in_specs.append(fixed)
    scratch = [pltpu.VMEM((2, whole, width), jnp.bfloat16)]
    narrow = jax.ShapeDtypeStruct((whole, width), jnp.bfloat16)
    if last:
        out_shape = [narrow, jax.ShapeDtypeStruct((quads, cells, width), jnp.bfloat16)]
        out_specs = [fixed, pl.BlockSpec((per_block, cells, width), lambda b: (b, 0, 0))]
    else:
        out_shape, out_specs = [narrow], [fixed]
        if stage > 0:
            out_shape.append(jax.ShapeDtypeStruct((whole, width), jnp.float32))
            out_specs.append(fixed)
        scratch.append(pltpu.VMEM((whole, width), jnp.float32))
    return pl.pallas_call(
        functools.partial(step_kernel, stage, len(preds), sensors),
        grid=(blocks,),
        in_specs=in_specs,
        out_specs=out_specs,
        out_shape=out_shape,
        scratch_shapes=scratch,
        compiler_params=pltpu.CompilerParams(vmem_limit_bytes=VMEM_LIMIT),
    )(*operands)


def on_device(forward_map, observed, noise_var, prior_rows, prior_scale):
    frequencies, halves, sensors, cells = forward_map.shape
    groups, quads, sides = (lax.axis_size(a) for a in ("sensor", "quad", "side"))
    per_block = prior_rows.shape[1] // cells
    g, q = lax.axis_index("sensor"), lax.axis_index("quad")
    rows = Rows(sensors, cells, groups, quads, prior_rows.shape[1])
    place = jnp.stack([g, q]).astype(jnp.int32)
    scale = lax.dynamic_slice_in_dim(prior_scale, g * quads + q, 1, 0)

    packed = pack(rows, forward_map, observed, noise_var, prior_rows, place, groups, quads)
    held = lax.all_to_all(packed, ("sensor", "quad"), split_axis=0, concat_axis=0, tiled=True)
    held = held.reshape(groups, quads, rows.total, cells)

    def over_sides(partial):
        if sides == 2:
            return [partial, lax.ppermute(partial, "side", [(0, 1), (1, 0)])]
        return [lax.psum(partial, "side")]

    run = functools.partial(step, rows=rows, held=held, scale=scale, sensors=sensors, per_block=per_block)
    preds, multiplier = [], None
    for stage in range(ITERS):
        outs = run(stage, preds=preds, multiplier=multiplier)
        preds = over_sides(outs[0])
        if stage > 0:
            multiplier = outs[1]
    dual, post = run(ITERS, preds=preds, multiplier=multiplier)

    post = lax.all_to_all(post, "quad", split_axis=0, concat_axis=0, tiled=True)
    posterior = post.astype(jnp.float32).reshape(quads, cells, 2, LANES)
    dual = jnp.broadcast_to(dual.reshape(groups, 1, sensors, 2 * LANES), (groups, quads, sensors, 2 * LANES))
    dual = lax.all_to_all(
        dual.reshape(frequencies, sensors, 2 * LANES), ("sensor", "quad"), split_axis=0, concat_axis=0, tiled=True
    )
    dual_out = jnp.stack([dual[:, :, :LANES], dual[:, :, LANES:]], 1).astype(jnp.float32)
    return dual_out, posterior


def solution(mesh):
    groups, space = mesh.devices.shape

    def run(forward_map, observed, noise_var, prior_rows, prior_scale):
        quads = forward_map.shape[0] // groups
        split = Mesh(mesh.devices.reshape(groups, space // quads, quads), ("sensor", "side", "quad"))
        return jax.shard_map(
            on_device,
            mesh=split,
            in_specs=(
                P(None, None, "sensor", ("side", "quad")),
                P(None, None, "sensor", None),
                P("sensor"),
                P(("side", "quad"), None),
                P(),
            ),
            out_specs=(P(None, None, "sensor", None), P("sensor", ("side", "quad"), None, None)),
            check_vma=False,
        )(forward_map, observed, noise_var, prior_rows, prior_scale)

    return run
```

```python
import functools

import jax
import jax.numpy as jnp
from jax import lax
from jax.experimental import pallas as pl
from jax.experimental.pallas import tpu as pltpu
from jax.sharding import Mesh, PartitionSpec as P

ITERS = 2
relax_step = 0.25
STREAMS = 2
LANES = 128
HALF = LANES // 2
VMEM_LIMIT = 32 * 2**20
VMEM = pl.BlockSpec(memory_space=pltpu.VMEM)
SMEM = pl.BlockSpec(memory_space=pltpu.SMEM)
ANY = pl.BlockSpec(memory_space=pl.ANY)
bf16, f32 = jnp.bfloat16, jnp.float32


def shape(dims, dtype):
    return jax.ShapeDtypeStruct(dims, dtype)


def call(kernel, in_specs, out_shape, scratch=(), flops=0, moved=0):
    return pl.pallas_call(
        kernel,
        in_specs=in_specs,
        out_specs=[VMEM] * len(out_shape),
        out_shape=out_shape,
        scratch_shapes=list(scratch),
        cost_estimate=pl.CostEstimate(flops=flops, bytes_accessed=moved, transcendentals=0),
        compiler_params=pltpu.CompilerParams(vmem_limit_bytes=VMEM_LIMIT),
    )


def swap(x, axes, distance):
    count = lax.axis_size(axes)
    return lax.ppermute(x, axes, [(i, i ^ distance) for i in range(count)])


def dot(a, b):
    return jnp.dot(a, b, preferred_element_type=f32)


def dot_t(a, b):
    return lax.dot_general(a, b, (((0,), (0,)), ((), ())), preferred_element_type=f32)


def data_kernel(groups, quads, place_ref, obs_ref, noise_ref, *refs):
    outs, (held, sems) = refs[:groups], refs[groups:]
    sensors = obs_ref.shape[2]
    copies = []
    for d in range(groups):
        freq = (place_ref[0] ^ d) * quads + place_ref[1]
        copies.append(pltpu.make_async_copy(obs_ref.at[freq], held.at[d], sems.at[d]))
        copies[-1].start()
    noise = noise_ref[...]
    high = noise.astype(bf16)
    low = (noise - high.astype(f32)).astype(bf16)
    tail = jnp.concatenate([jnp.broadcast_to(high, (8, sensors)), jnp.broadcast_to(low, (8, sensors))], 0)
    for d in range(groups):
        copies[d].wait()
        re, im = held[d, 0], held[d, 1]
        for s in range(STREAMS):
            part = slice(s * HALF, (s + 1) * HALF)
            outs[d][:sensors, s * LANES:(s + 1) * LANES] = jnp.concatenate([re[:, part], im[:, part]], 1).astype(bf16)
        outs[d][sensors:, :] = tail


def gather_kernel(groups, quads, place_ref, own_ref, *refs):
    halves, other, data = refs[:quads - 1], refs[quads - 1:2 * quads - 2], refs[2 * quads - 2:2 * quads - 2 + groups]
    prior_ref, noise_ref, *streams = refs[2 * quads - 2 + groups:]
    me, quad = place_ref[0], place_ref[1]
    core = me & 1
    sensors = streams[0].shape[1]
    prior_ref[quad] = own_ref[...]
    rows = own_ref.shape[0] // 2
    mine = pl.ds(pl.multiple_of(core * rows, rows), rows)
    theirs = pl.ds(pl.multiple_of((1 - core) * rows, rows), rows)
    for d in range(1, quads):
        prior_ref[quad ^ d, mine, :] = halves[d - 1][...]
        prior_ref[quad ^ d, theirs, :] = other[d - 1][...]
    row = lax.broadcasted_iota(jnp.int32, (sensors, sensors), 0)
    col = lax.broadcasted_iota(jnp.int32, (sensors, sensors), 1)
    for d in range(groups):
        for s in range(STREAMS):
            streams[s][me ^ d] = data[d][:sensors, s * LANES:(s + 1) * LANES]
        both = data[d][sensors:, :].astype(f32)
        noise_row = both[0:1, :] + both[8:9, :]
        noise = jnp.sum(jnp.where(row == col, noise_row, 0.0), 1, keepdims=True)
        noise_ref[me ^ d] = jnp.broadcast_to(noise, (sensors, LANES))


def step_kernel(stage, n_pred, per_block, place_ref, scale_ref, map_ref, prior_ref, obs_ref, noise_ref, *rest):
    groups, quads, double, cells = map_ref.shape
    sensors = double // 2
    last = stage == ITERS
    preds, rest = rest[:n_pred], rest[n_pred:]
    if stage > 1:
        held_ref, rest = rest[0], rest[1:]
    if last:
        keep_ref, give_ref, post_ref, z_ref, dual_ref = rest
    elif stage > 0:
        out_ref, next_ref, z_ref = rest
    else:
        out_ref, z_ref = rest

    for g in range(groups):
        obs = obs_ref[g].astype(f32)
        now = relax_step * obs if stage < 2 else held_ref[g]
        if stage > 0:
            predicted = sum(p[g].astype(f32) for p in preds)
            now = now + relax_step * (obs - predicted - noise_ref[g] * now)
            if not last:
                next_ref[g] = now
        z = now.astype(bf16)
        z_ref[g, :sensors, :] = z
        z_ref[g, sensors:, :] = jnp.concatenate([z[:, HALF:], -z[:, :HALF]], 1)
        if last:
            dual_ref[g] = z
    if last:
        core = place_ref[0] & 1
        for pair in range(groups // 2):
            keep_ref[pair] = dual_ref[2 * pair + core]
            give_ref[pair] = dual_ref[2 * pair + 1 - core]

    scale = scale_ref[0]
    sources = []
    for block in range(quads // per_block):
        parts = []
        for q in range(block * per_block, (block + 1) * per_block):
            u = jnp.zeros((cells, LANES), f32)
            for g in range(groups):
                u += dot_t(map_ref[g, q], z_ref[g])
            parts.append(u.astype(bf16))
        ub = jnp.concatenate(parts, 0)
        for q in range(block * per_block, (block + 1) * per_block):
            v = (dot(prior_ref[q], ub) * scale).astype(bf16)
            if last:
                post_ref[q] = v
            else:
                sources.append((v, jnp.concatenate([-v[:, HALF:], v[:, :HALF]], 1)))
    if not last:
        for g in range(groups):
            total = jnp.zeros((sensors, LANES), f32)
            for q, (v, w) in enumerate(sources):
                total += dot(map_ref[g, q, :sensors, :], v) + dot(map_ref[g, q, sensors:, :], w)
            out_ref[g] = total.astype(bf16)


def send_kernel(groups, quads, place_ref, keep_ref, got_ref, post_ref, *outs):
    sensors = keep_ref.shape[1]
    pair, quad = place_ref[0] // 2, place_ref[1]
    for e in range(groups // 2):
        for d in range(quads if e == 0 else 1):
            out = outs[d] if e == 0 else outs[quads + e - 1]
            out[:sensors] = keep_ref[pair ^ e]
            out[sensors:2 * sensors] = got_ref[pair ^ e]
            if e == 0:
                out[2 * sensors:] = post_ref[quad ^ d]


def end_kernel(groups, quads, place_ref, *refs):
    count = groups // 2 * quads
    first, second, (dual_ref, post_ref) = refs[:count], refs[count:2 * count], refs[2 * count:]
    sensors = dual_ref.shape[2]
    cells = post_ref.shape[1] // 2
    me, quad = place_ref[0], place_ref[1]
    for e in range(groups // 2):
        for d in range(quads):
            a, b = first[e * quads + d], second[e * quads + d]
            for sibling in range(2):
                freq = (me ^ (2 * e + sibling)) * quads + (quad ^ d)
                span = slice(sibling * sensors, (sibling + 1) * sensors)
                x, y = a[span, :].astype(f32), b[span, :].astype(f32)
                dual_ref[freq, 0] = jnp.concatenate([x[:, :HALF], y[:, :HALF]], 1)
                dual_ref[freq, 1] = jnp.concatenate([x[:, HALF:], y[:, HALF:]], 1)
            if e == 0:
                x, y = a[2 * sensors:, :].astype(f32), b[2 * sensors:, :].astype(f32)
                post_ref[quad ^ d, pl.ds(0, cells, stride=2), :] = jnp.concatenate([x[:, :HALF], y[:, :HALF]], 1)
                post_ref[quad ^ d, pl.ds(1, cells, stride=2), :] = jnp.concatenate([x[:, HALF:], y[:, HALF:]], 1)


def spread(count):
    order = []
    for d in sorted(range(1, count), key=lambda d: -bin(d).count("1")):
        for x in (d, count - 1 - d):
            if x and x not in order:
                order.append(x)
    return order


def on_device(forward_map, observed, noise_var, prior_rows, prior_scale):
    frequencies, halves, sensors, cells = forward_map.shape
    groups, quads, sides = (lax.axis_size(a) for a in ("sensor", "quad", "side"))
    width = prior_rows.shape[1]
    per_block = width // cells
    me, quad = lax.axis_index("sensor"), lax.axis_index("quad")
    place = jnp.stack([me, quad]).astype(jnp.int32)
    scale = lax.dynamic_slice_in_dim(prior_scale, me * quads + quad, 1, 0)
    both = ("sensor", "quad")

    held = lax.all_to_all(
        forward_map.reshape(frequencies, halves * sensors, cells), both, split_axis=0, concat_axis=0, tiled=True
    ).reshape(groups, quads, halves * sensors, cells)

    data = call(
        functools.partial(data_kernel, groups, quads),
        [SMEM, ANY, VMEM],
        [shape((sensors + 16, STREAMS * LANES), bf16)] * groups,
        [pltpu.VMEM((groups, halves, sensors, LANES), f32), pltpu.SemaphoreType.DMA((groups,))],
        moved=groups * sensors * LANES * 12,
    )(place, observed, noise_var.reshape(1, sensors))
    data = [data[0]] + [swap(data[d], "sensor", d) for d in range(1, groups)]
    own_half = lax.dynamic_slice_in_dim(prior_rows, (me % 2) * (cells // 2), cells // 2, 0)
    came = [swap(own_half, "quad", d) for d in range(1, quads)]
    other = [swap(x, "sensor", 1) for x in came]
    prior, noise, *streams = call(
        functools.partial(gather_kernel, groups, quads),
        [SMEM] + [VMEM] * (1 + 2 * (quads - 1) + groups),
        [shape((quads, cells, width), bf16), shape((groups, sensors, LANES), f32)]
        + [shape((groups, sensors, LANES), bf16)] * STREAMS,
        moved=8 * 2**20,
    )(place, prior_rows, *came, *other, *data)

    def over_sides(partial):
        if sides == 2:
            return [partial, swap(partial, "side", 1)]
        return [lax.psum(partial, "side")]

    wide, narrow = shape((groups, sensors, LANES), f32), shape((groups, sensors, LANES), bf16)
    pairs = shape((groups // 2, sensors, LANES), bf16)

    def step(stage, obs, preds, multiplier):
        operands = [place, scale, held, prior, obs, noise] + preds + ([multiplier] if stage > 1 else [])
        out = [pairs, pairs, shape((quads, cells, LANES), bf16)] if stage == ITERS else [narrow] + [wide] * (stage > 0)
        scratch = [pltpu.VMEM((groups, halves * sensors, LANES), bf16)]
        if stage == ITERS:
            scratch.append(pltpu.VMEM((groups, sensors, LANES), bf16))
        return call(
            functools.partial(step_kernel, stage, len(preds), per_block),
            [SMEM, SMEM] + [VMEM] * (len(operands) - 2),
            out,
            scratch,
            flops=2 * 2**30,
            moved=8 * 2**20,
        )(*operands)

    preds, multiplier = [[]] * STREAMS, [None] * STREAMS
    for stage in range(ITERS):
        for s in range(STREAMS):
            outs = step(stage, streams[s], preds[s], multiplier[s])
            preds = preds[:s] + [over_sides(outs[0])] + preds[s + 1:]
            if stage > 0:
                multiplier[s] = outs[1]

    arrived = []
    for s in range(STREAMS):
        keep, give, post = step(ITERS, streams[s], preds[s], multiplier[s])
        messages = call(
            functools.partial(send_kernel, groups, quads),
            [SMEM] + [VMEM] * 3,
            [shape((2 * sensors + cells, LANES), bf16)] * quads
            + [shape((2 * sensors, LANES), bf16)] * (groups // 2 - 1),
            moved=4 * 2**20,
        )(place, keep, swap(give, "sensor", 1), post)
        got = {0: messages[0]}
        for distance in spread(groups // 2 * quads):
            e, d = divmod(distance, quads)
            out = messages[d] if e == 0 else messages[quads + e - 1]
            got[distance] = swap(out, both, 2 * e * quads + d)
        arrived += [got[i] for i in range(groups // 2 * quads)]
    dual, posterior = call(
        functools.partial(end_kernel, groups, quads),
        [SMEM] + [VMEM] * len(arrived),
        [shape((frequencies, halves, sensors, LANES), f32), shape((quads, cells * 2, LANES), f32)],
        moved=8 * 2**20,
    )(place, *arrived)
    return dual, posterior.reshape(quads, cells, 2, LANES)


def solution(mesh):
    groups, space = mesh.devices.shape

    def run(forward_map, observed, noise_var, prior_rows, prior_scale):
        quads = forward_map.shape[0] // groups
        split = Mesh(mesh.devices.reshape(groups, space // quads, quads), ("sensor", "side", "quad"))
        return jax.shard_map(
            on_device,
            mesh=split,
            in_specs=(
                P(None, None, "sensor", ("side", "quad")),
                P(None, None, "sensor", None),
                P("sensor"),
                P(("side", "quad"), None),
                P(),
            ),
            out_specs=(P(None, None, "sensor", None), P("sensor", ("side", "quad"), None, None)),
            check_vma=False,
        )(forward_map, observed, noise_var, prior_rows, prior_scale)

    return run
```

```python
import functools

import jax
import jax.numpy as jnp
from jax import lax
from jax.experimental import pallas as pl
from jax.experimental.pallas import tpu as pltpu
from jax.sharding import Mesh, PartitionSpec as P

ITERS = 2
relax_step = 0.25
CORES = 2
LANES = 128
HALF = LANES // CORES
BATCHES = ((0, 1),)
VMEM_LIMIT = 32 * 2**20
VMEM = pl.BlockSpec(memory_space=pltpu.VMEM)
SMEM = pl.BlockSpec(memory_space=pltpu.SMEM)
ANY = pl.BlockSpec(memory_space=pl.ANY)
bf16, f32 = jnp.bfloat16, jnp.float32


def shape(dims, dtype):
    return jax.ShapeDtypeStruct(dims, dtype)


def call(kernel, in_specs, out_shape, scratch=(), out_specs=None, flops=0, moved=0):
    return pl.pallas_call(
        kernel,
        in_specs=in_specs,
        out_specs=out_specs or [VMEM] * len(out_shape),
        out_shape=out_shape,
        scratch_shapes=list(scratch),
        cost_estimate=pl.CostEstimate(flops=flops, bytes_accessed=moved, transcendentals=0),
        compiler_params=pltpu.CompilerParams(vmem_limit_bytes=VMEM_LIMIT),
    )


def dot(a, b):
    return jnp.dot(a, b, preferred_element_type=f32)


def dot_nt(a, b):
    return lax.dot_general(a, b, (((1,), (1,)), ((), ())), preferred_element_type=f32)


class Plan:
    def __init__(self, groups, quads, sensors, cells, width):
        self.groups, self.quads, self.sensors, self.cells, self.width = groups, quads, sensors, cells, width
        self.pairs = groups // CORES
        self.chips = self.pairs * quads
        self.per_block = width // cells
        self.map_rows = 2 * sensors
        self.share = cells // CORES

    def extra(self, batch, d):
        e, dq = divmod(d, self.quads)
        if batch > 0:
            return 0
        if dq == 0:
            return CORES * self.sensors + 16
        return self.share * self.per_block if e == 0 else 0

    def rows(self, batch, d):
        return len(BATCHES[batch]) * self.map_rows + self.extra(batch, d)

    def order(self):
        order = []
        for d in sorted(range(1, self.chips), key=lambda d: -bin(d).count("1")):
            for x in (d, self.chips - 1 - d):
                if x and x not in order:
                    order.append(x)
        return order


def pack_kernel(plan, batch, place_ref, map_ref, obs_ref, prior_ref, noise_ref, *refs):
    outs, (held, lines, sems) = refs[:plan.chips], refs[plan.chips:]
    pair, quad, core = place_ref[0], place_ref[1], place_ref[2]
    chip = pair * plan.quads + quad
    copies = []
    first, count = BATCHES[batch][0], len(BATCHES[batch])
    for d in range(plan.chips):
        freq = CORES * (chip ^ d) + first
        for j in range(count):
            to = outs[d].at[pl.ds(j * plan.map_rows, plan.map_rows)]
            copies.append(pltpu.make_async_copy(map_ref.at[freq + j], to, sems.at[d, j]))
            copies[-1].start()
    if batch == 0:
        at = count * plan.map_rows
        noise = noise_ref[...]
        high = noise.astype(bf16)
        low = (noise - high.astype(f32)).astype(bf16)
        wide = (8, plan.sensors)
        tail = jnp.concatenate([jnp.broadcast_to(high, wide), jnp.broadcast_to(low, wide)], 0)
        loads = []
        for e in range(plan.pairs):
            freq = CORES * (chip ^ (e * plan.quads))
            loads.append(pltpu.make_async_copy(obs_ref.at[pl.ds(freq, CORES)], held.at[e], sems.at[plan.chips, e]))
            loads[-1].start()
        half = prior_ref[pl.ds(pl.multiple_of(core * plan.share, plan.share), plan.share), :]
        for k in range(plan.per_block):
            lines[0, k * plan.share:(k + 1) * plan.share, :] = half[:, k * plan.cells:(k + 1) * plan.cells]
        stores = []
        for dq in range(1, plan.quads):
            size = plan.share * plan.per_block
            to = outs[dq].at[pl.ds(at, size)]
            stores.append(pltpu.make_async_copy(lines.at[0, pl.ds(0, size)], to, sems.at[plan.chips + 1, dq]))
            stores[-1].start()
        for e in range(plan.pairs):
            loads[e].wait()
            slot = 1 + e
            for j in range(CORES):
                re, im = held[e, j, 0], held[e, j, 1]
                for s in range(CORES):
                    part = slice(s * HALF, (s + 1) * HALF)
                    lines[slot, j * plan.sensors:(j + 1) * plan.sensors, s * LANES:(s + 1) * LANES] = (
                        jnp.concatenate([re[:, part], im[:, part]], 1).astype(bf16)
                    )
            size = plan.extra(0, 0)
            lines[slot, size - 16:size, :] = tail
            to = outs[e * plan.quads].at[pl.ds(at, size)]
            stores.append(pltpu.make_async_copy(lines.at[slot, pl.ds(0, size)], to, sems.at[plan.chips + 2, e]))
            stores[-1].start()
        for copy in stores:
            copy.wait()
    for copy in copies:
        copy.wait()


def gather_kernel(plan, place_ref, own_ref, *refs):
    mine, theirs = refs[:plan.chips], refs[plan.chips:2 * plan.chips]
    prior_ref, noise_ref, *streams = refs[2 * plan.chips:]
    quad, core = place_ref[1], place_ref[2]
    at = len(BATCHES[0]) * plan.map_rows
    share, cells, sensors = plan.share, plan.cells, plan.sensors
    for k in range(plan.per_block):
        column = k ^ (quad & (plan.per_block - 1))
        to = slice(k * cells, (k + 1) * cells)
        prior_ref[0, :, to] = own_ref[:, pl.ds(pl.multiple_of(column * cells, cells), cells)]
        for dq in range(1, plan.quads):
            span = pl.ds(pl.multiple_of(at + column * share, share), share)
            for part, ref in ((core, mine[dq]), (1 - core, theirs[dq])):
                prior_ref[dq, pl.ds(pl.multiple_of(part * share, share), share), to] = ref[span, :]
    row = lax.broadcasted_iota(jnp.int32, (sensors, sensors), 0)
    col = lax.broadcasted_iota(jnp.int32, (sensors, sensors), 1)
    lanes = pl.ds(pl.multiple_of(core * LANES, LANES), LANES)
    for e in range(plan.pairs):
        for s, refs_s in enumerate((mine, theirs)):
            ref, r = refs_s[e * plan.quads], CORES * e + s
            for j in range(CORES):
                streams[j][r] = ref[at + j * sensors:at + (j + 1) * sensors, lanes]
            both = ref[at + CORES * sensors:, :].astype(f32)
            noise_row = both[0:1, :] + both[8:9, :]
            noise = jnp.sum(jnp.where(row == col, noise_row, 0.0), 1, keepdims=True)
            noise_ref[r] = jnp.broadcast_to(noise, (sensors, LANES))


def sides(z):
    return jnp.concatenate([z, jnp.concatenate([z[:, HALF:], -z[:, :HALF]], 1)], 0).T


def source(plan, chunk, sides_ref, prior_ref, scale):
    out = []
    for block in range(plan.quads // plan.per_block):
        quads = range(block * plan.per_block, (block + 1) * plan.per_block)
        parts = []
        for dq in quads:
            u = jnp.zeros((LANES, plan.cells), f32)
            for r in range(plan.groups):
                u += dot(sides_ref[r], chunk(r, dq)[...])
            parts.append(u.astype(bf16))
        ub = jnp.concatenate(parts, 1)
        out += [(dot_nt(prior_ref[dq], ub) * scale).astype(bf16) for dq in quads]
    return out


def chunks(plan, refs, start):
    rows = pl.ds(start, plan.map_rows)
    return lambda r, dq: refs[(r % CORES) * plan.chips + r // CORES * plan.quads + dq].at[rows]


def step_kernel(plan, stage, start, n_pred, scale_ref, prior_ref, obs_ref, noise_ref, *refs):
    chunk, refs = chunks(plan, refs, start), refs[2 * plan.chips:]
    preds, refs = refs[:n_pred], refs[n_pred:]
    if stage > 0:
        next_ref, refs = refs[0], refs[1:]
    outs, sides_ref = refs[:-1], refs[-1]
    for r in range(plan.groups):
        obs = obs_ref[r].astype(f32)
        now = relax_step * obs
        if stage > 0:
            predicted = sum(p[r].astype(f32) for p in preds)
            now = now + relax_step * (obs - predicted - noise_ref[r] * now)
            next_ref[r] = now
        sides_ref[r] = sides(now.astype(bf16))
    sources = source(plan, chunk, sides_ref, prior_ref, scale_ref[0])
    turned = [jnp.concatenate([-v[:, HALF:], v[:, :HALF]], 1) for v in sources]
    for r in reversed(range(plan.groups)):
        total = jnp.zeros((plan.sensors, LANES), f32)
        for dq in range(plan.quads):
            block = chunk(r, dq)
            total += dot(block[:plan.sensors, :], sources[dq]) + dot(block[plan.sensors:, :], turned[dq])
        if len(outs) == 1:
            outs[0][r] = total.astype(bf16)
        else:
            outs[r // CORES][r % CORES] = total.astype(bf16)


def last_kernel(plan, e, n_pred, noise_ref, *refs):
    obs, held, refs = refs[:CORES], refs[CORES:2 * CORES], refs[2 * CORES:]
    preds, (keep_ref, give_ref) = refs[:CORES * n_pred], refs[CORES * n_pred:]
    for j in range(CORES):
        for s, out in ((1, give_ref), (0, keep_ref)):
            r = CORES * e + s
            now = held[j][r]
            predicted = sum(p[s].astype(f32) for p in preds[j * n_pred:(j + 1) * n_pred])
            now = now + relax_step * (obs[j][r].astype(f32) - predicted - noise_ref[r] * now)
            out[j] = now.astype(bf16)


def merge(flag, mine, theirs):
    low, high = jnp.where(flag, theirs, mine), jnp.where(flag, mine, theirs)
    re = jnp.concatenate([low[:, :HALF], high[:, :HALF]], 1)
    im = jnp.concatenate([low[:, HALF:], high[:, HALF:]], 1)
    return re, im


def send_kernel(place_ref, keep_ref, got_ref, out_ref):
    for j in range(CORES):
        re, im = merge(place_ref[2] == 1, keep_ref[j].astype(f32), got_ref[j].astype(f32))
        out_ref[j, :, :LANES] = re.astype(bf16)
        out_ref[j, :, LANES:] = im.astype(bf16)


def post_kernel(plan, starts, place_ref, scale_ref, prior_ref, *refs):
    maps, refs = refs[:2 * plan.chips * len(BATCHES)], refs[2 * plan.chips * len(BATCHES):]
    keeps, gives, refs = refs[:plan.pairs], refs[plan.pairs:2 * plan.pairs], refs[2 * plan.pairs:]
    outs, (sides_ref, held_ref) = refs[:plan.quads], refs[plan.quads:]
    quad, core = place_ref[1], place_ref[2]
    for j in range(CORES):
        batch, start = starts[j]
        chunk = chunks(plan, maps[2 * plan.chips * batch:], start)
        for r in range(plan.groups):
            sides_ref[r] = sides((gives if r % CORES else keeps)[r // CORES][j])
        for dq, v in enumerate(source(plan, chunk, sides_ref, prior_ref, scale_ref[j])):
            held_ref[dq, j] = v
    wide = plan.quads // CORES
    for flip in range(CORES):
        for step in range(wide):
            to = (core ^ flip) * wide + ((quad & (wide - 1)) ^ step)
            outs[flip * wide + step][...] = held_ref[to ^ quad]


def post_route(groups, quads, flip, step):
    wide, route = quads // CORES, []
    for g in range(groups):
        for q in range(quads):
            core = g % CORES
            to_quad = (core ^ flip) * wide + ((q % wide) ^ step)
            route.append((g * quads + q, (g - core + q // wide) * quads + to_quad))
    return route


def end_kernel(plan, place_ref, *refs):
    duals, posts = refs[:plan.chips], refs[plan.chips:plan.chips + plan.quads]
    dual_ref, post_ref = refs[plan.chips + plan.quads:]
    pair, quad = place_ref[0], place_ref[1]
    chip = pair * plan.quads + quad
    for d in range(plan.chips):
        for j in range(CORES):
            freq = CORES * (chip ^ d) + j
            dual_ref[freq, 0] = duals[d][j, :, :LANES].astype(f32)
            dual_ref[freq, 1] = duals[d][j, :, LANES:].astype(f32)
    wide = plan.quads // CORES
    for step in range(wide):
        for j in range(CORES):
            re, im = merge(quad // wide == 1, posts[step][j].astype(f32), posts[wide + step][j].astype(f32))
            freq = CORES * ((quad & (wide - 1)) ^ step) + j
            post_ref[freq, pl.ds(0, plan.cells, stride=2), :] = re
            post_ref[freq, pl.ds(1, plan.cells, stride=2), :] = im


def on_device(forward_map, observed, noise_var, prior_rows, prior_scale):
    frequencies, halves, sensors, cells = forward_map.shape
    groups, quads, count = (lax.axis_size(a) for a in ("sensor", "quad", "side"))
    plan = Plan(groups, quads, sensors, cells, prior_rows.shape[1])
    me, quad = lax.axis_index("sensor"), lax.axis_index("quad")
    pair, core = me // CORES, me % CORES
    place = jnp.stack([pair, quad, core]).astype(jnp.int32)
    scales = lax.dynamic_slice_in_dim(prior_scale, CORES * (pair * quads + quad), CORES, 0)
    both = ("sensor", "quad")

    def swap(x, axes, distance):
        return lax.ppermute(x, axes, [(i, i ^ distance) for i in range(lax.axis_size(axes))])

    def to_chip(x, d):
        e, dq = divmod(d, quads)
        return swap(x, both, CORES * e * quads + dq)

    def to_sibling(x):
        return swap(x, "sensor", 1)

    flat = forward_map.reshape(frequencies, halves * sensors, cells)
    maps = []
    for batch in range(len(BATCHES)):
        line = max(plan.extra(0, d) for d in range(plan.chips))
        messages = call(
            functools.partial(pack_kernel, plan, batch),
            [SMEM, ANY, ANY, VMEM, VMEM],
            [shape((plan.rows(batch, d), cells), bf16) for d in range(plan.chips)],
            [
                pltpu.VMEM((plan.pairs, CORES, halves, sensors, LANES), f32),
                pltpu.VMEM((1 + plan.pairs, line, cells), bf16),
                pltpu.SemaphoreType.DMA((plan.chips + 3, max(plan.chips, quads, CORES))),
            ],
            [ANY] * plan.chips,
            moved=10 * 2**20,
        )(place, flat, observed, prior_rows, noise_var.reshape(1, sensors))
        mine = [messages[0]] + [None] * (plan.chips - 1)
        for d in plan.order():
            mine[d] = to_chip(messages[d], d)
        maps.append(mine + [to_sibling(x) for x in mine])
    starts = {}
    for batch, held in enumerate(BATCHES):
        for i, j in enumerate(held):
            starts[j] = (batch, i * plan.map_rows)

    prior, noise, *streams = call(
        functools.partial(gather_kernel, plan),
        [SMEM] + [VMEM] * (1 + 2 * plan.chips),
        [shape((quads, cells, plan.width), bf16), shape((groups, sensors, LANES), f32)]
        + [shape((groups, sensors, LANES), bf16)] * CORES,
        moved=4 * 2**20,
    )(place, prior_rows, *maps[0])

    def over_sides(partial):
        if count == 2:
            return [partial, swap(partial, "side", 1)]
        return [lax.psum(partial, "side")]

    wide, narrow = shape((groups, sensors, LANES), f32), shape((groups, sensors, LANES), bf16)
    couple = shape((CORES, sensors, LANES), bf16)
    sides_scratch = pltpu.VMEM((groups, LANES, halves * sensors), bf16)

    def step(stage, j, preds):
        batch, start = starts[j]
        operands = [scales[j:j + 1], prior, streams[j], noise] + maps[batch] + preds
        return call(
            functools.partial(step_kernel, plan, stage, start, len(preds)),
            [SMEM] + [VMEM] * (len(operands) - 1),
            [narrow] if stage == 0 else [wide] + [couple] * plan.pairs,
            [sides_scratch],
            flops=2**31,
            moved=8 * 2**20,
        )(*operands)

    first = [over_sides(step(0, j, [])[0]) for j in range(CORES)]
    multiplier, partials = [], []
    for j in range(CORES):
        held, *parts = step(1, j, first[j])
        multiplier.append(held)
        partials.append(parts)
    keeps, gives = [None] * plan.pairs, [None] * plan.pairs
    duals = [None] * plan.chips
    for e in reversed(range(plan.pairs)):
        preds = [over_sides(partials[j][e]) for j in range(CORES)]
        preds = preds[0] + preds[1]
        keeps[e], gives[e] = call(
            functools.partial(last_kernel, plan, e, len(preds) // CORES),
            [VMEM] * (1 + 2 * CORES + len(preds)),
            [couple, couple],
            moved=2 * 2**20,
        )(noise, *streams, *multiplier, *preds)
        message = call(
            send_kernel,
            [SMEM, VMEM, VMEM],
            [shape((CORES, sensors, 2 * LANES), bf16)],
            moved=2**20,
        )(place, keeps[e], to_sibling(gives[e]))[0]
        for dq in reversed(range(quads)):
            d = e * quads + dq
            duals[d] = to_chip(message, d) if d else message

    posts = call(
        functools.partial(post_kernel, plan, starts),
        [SMEM, SMEM] + [VMEM] * (1 + sum(len(m) for m in maps) + 2 * plan.pairs),
        [shape((CORES, cells, LANES), bf16)] * quads,
        [sides_scratch, pltpu.VMEM((quads, CORES, cells, LANES), bf16)],
        flops=2**31,
        moved=16 * 2**20,
    )(place, scales, prior, *[x for m in maps for x in m], *keeps, *gives)
    half = quads // CORES
    posts = [lax.ppermute(posts[i], both, post_route(groups, quads, *divmod(i, half))) for i in range(quads)]
    dual, posterior = call(
        functools.partial(end_kernel, plan),
        [SMEM] + [VMEM] * (plan.chips + quads),
        [shape((frequencies, halves, sensors, LANES), f32), shape((quads, cells * 2, LANES), f32)],
        moved=8 * 2**20,
    )(place, *duals, *posts)
    return dual, posterior.reshape(quads, cells, 2, LANES)


def solution(mesh):
    groups, space = mesh.devices.shape

    def run(forward_map, observed, noise_var, prior_rows, prior_scale):
        quads = forward_map.shape[0] // groups
        split = Mesh(mesh.devices.reshape(groups, space // quads, quads), ("sensor", "side", "quad"))
        return jax.shard_map(
            on_device,
            mesh=split,
            in_specs=(
                P(None, None, "sensor", ("side", "quad")),
                P(None, None, "sensor", None),
                P("sensor"),
                P(("side", "quad"), None),
                P(),
            ),
            out_specs=(P(None, None, "sensor", None), P("sensor", ("side", "quad"), None, None)),
            check_vma=False,
        )(forward_map, observed, noise_var, prior_rows, prior_scale)

    return run
```

```python
import functools

import jax
import jax.numpy as jnp
from jax import lax
from jax.experimental import pallas as pl
from jax.experimental.pallas import tpu as pltpu
from jax.sharding import Mesh, PartitionSpec as P

ITERS = 2
relax_step = 0.25
CORES = 2
LANES = 128
HALF = LANES // CORES
BATCHES = ((0,), (1,))
VMEM_LIMIT = 16 * 2**20
VMEM = pl.BlockSpec(memory_space=pltpu.VMEM)
SMEM = pl.BlockSpec(memory_space=pltpu.SMEM)
ANY = pl.BlockSpec(memory_space=pl.ANY)
HBM = pl.BlockSpec(memory_space=pltpu.HBM)
bf16, f32 = jnp.bfloat16, jnp.float32


def shape(dims, dtype):
    return jax.ShapeDtypeStruct(dims, dtype)


def call(kernel, in_specs, out_shape, scratch=(), out_specs=None, flops=0, moved=0, aliases=None):
    return pl.pallas_call(
        kernel,
        input_output_aliases=aliases or {},
        in_specs=in_specs,
        out_specs=out_specs or [VMEM] * len(out_shape),
        out_shape=out_shape,
        scratch_shapes=list(scratch),
        cost_estimate=pl.CostEstimate(flops=flops, bytes_accessed=moved, transcendentals=0),
        compiler_params=pltpu.CompilerParams(vmem_limit_bytes=VMEM_LIMIT),
    )


def dot(a, b):
    return jnp.dot(a, b, preferred_element_type=f32)


def dot_nt(a, b):
    return lax.dot_general(a, b, (((1,), (1,)), ((), ())), preferred_element_type=f32)


class Plan:
    def __init__(self, groups, quads, sensors, cells, width):
        self.groups, self.quads, self.sensors, self.cells, self.width = groups, quads, sensors, cells, width
        self.pairs = groups // CORES
        self.chips = self.pairs * quads
        self.per_block = width // cells
        self.map_rows = 2 * sensors
        self.share = cells // CORES

    def extra(self, batch, d):
        e, dq = divmod(d, self.quads)
        if batch > 0:
            return 0
        if dq == 0:
            return CORES * self.sensors + 16
        return self.share * self.per_block if e == 0 else 0

    def rows(self, batch, d):
        return len(BATCHES[batch]) * self.map_rows + self.extra(batch, d)

    def order(self):
        far, order = self.chips - 1, []
        for d in sorted(range(1, far), key=lambda d: -bin(d).count("1")):
            for x in (d, far - d):
                if x not in order:
                    order.append(x)
        return order[:2] + [far] + order[2:]


def pack_kernel(plan, batch, place_ref, map_ref, obs_ref, prior_ref, noise_ref, *refs):
    refs = refs[batch:]
    outs, (held, lines, sems) = refs[:plan.chips], refs[plan.chips:]
    pair, quad, core = place_ref[0], place_ref[1], place_ref[2]
    chip = pair * plan.quads + quad
    copies = []
    first, count = BATCHES[batch][0], len(BATCHES[batch])
    for d in range(plan.chips):
        freq = CORES * (chip ^ d) + first
        for j in range(count):
            to = outs[d].at[pl.ds(j * plan.map_rows, plan.map_rows)]
            copies.append(pltpu.make_async_copy(map_ref.at[freq + j], to, sems.at[d, j]))
            copies[-1].start()
    if batch == 0:
        at = count * plan.map_rows
        noise = noise_ref[...]
        high = noise.astype(bf16)
        low = (noise - high.astype(f32)).astype(bf16)
        wide = (8, plan.sensors)
        tail = jnp.concatenate([jnp.broadcast_to(high, wide), jnp.broadcast_to(low, wide)], 0)
        loads = []
        for e in range(plan.pairs):
            freq = CORES * (chip ^ (e * plan.quads))
            loads.append(pltpu.make_async_copy(obs_ref.at[pl.ds(freq, CORES)], held.at[e], sems.at[plan.chips, e]))
            loads[-1].start()
        half = prior_ref[pl.ds(pl.multiple_of(core * plan.share, plan.share), plan.share), :]
        for k in range(plan.per_block):
            lines[0, k * plan.share:(k + 1) * plan.share, :] = half[:, k * plan.cells:(k + 1) * plan.cells]
        stores = []
        for dq in range(1, plan.quads):
            size = plan.share * plan.per_block
            to = outs[dq].at[pl.ds(at, size)]
            stores.append(pltpu.make_async_copy(lines.at[0, pl.ds(0, size)], to, sems.at[plan.chips + 1, dq]))
            stores[-1].start()
        for e in range(plan.pairs):
            loads[e].wait()
            slot = 1 + e
            for j in range(CORES):
                re, im = held[e, j, 0], held[e, j, 1]
                for s in range(CORES):
                    part = slice(s * HALF, (s + 1) * HALF)
                    lines[slot, j * plan.sensors:(j + 1) * plan.sensors, s * LANES:(s + 1) * LANES] = (
                        jnp.concatenate([re[:, part], im[:, part]], 1).astype(bf16)
                    )
            size = plan.extra(0, 0)
            lines[slot, size - 16:size, :] = tail
            to = outs[e * plan.quads].at[pl.ds(at, size)]
            stores.append(pltpu.make_async_copy(lines.at[slot, pl.ds(0, size)], to, sems.at[plan.chips + 2, e]))
            stores[-1].start()
        for copy in stores:
            copy.wait()
    for copy in copies:
        copy.wait()


def gather_kernel(plan, place_ref, own_ref, *refs):
    mine, theirs = refs[:plan.chips], refs[plan.chips:2 * plan.chips]
    prior_ref, noise_ref, *streams = refs[2 * plan.chips:]
    quad, core = place_ref[1], place_ref[2]
    at = len(BATCHES[0]) * plan.map_rows
    share, cells, sensors = plan.share, plan.cells, plan.sensors
    for k in range(plan.per_block):
        column = k ^ (quad & (plan.per_block - 1))
        to = slice(k * cells, (k + 1) * cells)
        prior_ref[0, :, to] = own_ref[:, pl.ds(pl.multiple_of(column * cells, cells), cells)]
        for dq in range(1, plan.quads):
            span = pl.ds(pl.multiple_of(at + column * share, share), share)
            for part, ref in ((core, mine[dq]), (1 - core, theirs[dq])):
                prior_ref[dq, pl.ds(pl.multiple_of(part * share, share), share), to] = ref[span, :]
    row = lax.broadcasted_iota(jnp.int32, (sensors, sensors), 0)
    col = lax.broadcasted_iota(jnp.int32, (sensors, sensors), 1)
    lanes = pl.ds(pl.multiple_of(core * LANES, LANES), LANES)
    for e in range(plan.pairs):
        for s, refs_s in enumerate((mine, theirs)):
            ref, r = refs_s[e * plan.quads], CORES * e + s
            for j in range(CORES):
                streams[j][r] = ref[at + j * sensors:at + (j + 1) * sensors, lanes]
            both = ref[at + CORES * sensors:, :].astype(f32)
            noise_row = both[0:1, :] + both[8:9, :]
            noise = jnp.sum(jnp.where(row == col, noise_row, 0.0), 1, keepdims=True)
            noise_ref[r] = jnp.broadcast_to(noise, (sensors, LANES))


def sides(z):
    return jnp.concatenate([z, jnp.concatenate([z[:, HALF:], -z[:, :HALF]], 1)], 0).T


def source(plan, chunk, sides_ref, prior_ref, scale):
    out = []
    for block in range(plan.quads // plan.per_block):
        quads = range(block * plan.per_block, (block + 1) * plan.per_block)
        parts = []
        for dq in quads:
            u = jnp.zeros((LANES, plan.cells), f32)
            for r in range(plan.groups):
                u += dot(sides_ref[r], chunk(r, dq)[...])
            parts.append(u.astype(bf16))
        ub = jnp.concatenate(parts, 1)
        out += [(dot_nt(prior_ref[dq], ub) * scale).astype(bf16) for dq in quads]
    return out


def chunks(plan, refs, start):
    rows = pl.ds(start, plan.map_rows)
    return lambda r, dq: refs[(r % CORES) * plan.chips + r // CORES * plan.quads + dq].at[rows]


def step_kernel(plan, stage, start, n_pred, scale_ref, prior_ref, obs_ref, noise_ref, *refs):
    chunk, refs = chunks(plan, refs, start), refs[2 * plan.chips:]
    preds, refs = refs[:n_pred], refs[n_pred:]
    if stage > 0:
        next_ref, refs = refs[0], refs[1:]
    out_ref, sides_ref = refs
    for r in range(plan.groups):
        obs = obs_ref[r].astype(f32)
        now = relax_step * obs
        if stage > 0:
            predicted = sum(p[r].astype(f32) for p in preds)
            now = now + relax_step * (obs - predicted - noise_ref[r] * now)
            next_ref[r] = now
        sides_ref[r] = sides(now.astype(bf16))
    sources = source(plan, chunk, sides_ref, prior_ref, scale_ref[0])
    turned = [jnp.concatenate([-v[:, HALF:], v[:, :HALF]], 1) for v in sources]
    for r in range(plan.groups):
        total = jnp.zeros((plan.sensors, LANES), f32)
        for dq in range(plan.quads):
            block = chunk(r, dq)
            total += dot(block[:plan.sensors, :], sources[dq]) + dot(block[plan.sensors:, :], turned[dq])
        out_ref[r] = total.astype(bf16)


def last_kernel(plan, n_pred, place_ref, noise_ref, obs_ref, held_ref, *refs):
    preds, (final_ref, out_ref) = refs[:n_pred], refs[n_pred:]
    first = CORES * place_ref[0] + place_ref[2]
    for r in range(plan.groups):
        now = held_ref[r]
        predicted = sum(p[r].astype(f32) for p in preds)
        now = now + relax_step * (obs_ref[r].astype(f32) - predicted - noise_ref[r] * now)
        now = now.astype(bf16)
        final_ref[r] = now
        for q in range(plan.quads):
            out_ref[first ^ r, q] = now


def post_kernel(plan, start, place_ref, scale_ref, prior_ref, final_ref, *refs):
    chunk, refs = chunks(plan, refs, start), refs[2 * plan.chips:]
    outs, (sides_ref, held_ref) = refs[:plan.quads], refs[plan.quads:]
    quad, core = place_ref[1], place_ref[2]
    for r in range(plan.groups):
        sides_ref[r] = sides(final_ref[r])
    for dq, v in enumerate(source(plan, chunk, sides_ref, prior_ref, scale_ref[0])):
        held_ref[dq] = v
    wide = plan.quads // CORES
    for flip in range(CORES):
        for step in range(wide):
            to = (core ^ flip) * wide + ((quad & (wide - 1)) ^ step)
            outs[flip * wide + step][...] = held_ref[to ^ quad]


def post_route(quads, flip, step):
    wide, route = quads // CORES, []
    for core in range(CORES):
        for q in range(quads):
            to_quad = (core ^ flip) * wide + ((q % wide) ^ step)
            route.append((core * quads + q, q // wide * quads + to_quad))
    return route


def end_kernel(plan, j, place_ref, dual_ref, *refs):
    posts, refs = refs[:plan.quads], refs[plan.quads + 2 * j:]
    dual_out, post_out, wide_ref, post_ref, sems = refs
    quad = place_ref[1]
    sends = []
    for chip in range(plan.chips):
        x, q = divmod(chip, plan.quads)
        low, high = dual_ref[x, 0, q].astype(f32), dual_ref[x, 1, q].astype(f32)
        wide_ref[chip, 0] = jnp.concatenate([low[:, :HALF], high[:, :HALF]], 1)
        wide_ref[chip, 1] = jnp.concatenate([low[:, HALF:], high[:, HALF:]], 1)
        sends.append(pltpu.make_async_copy(wide_ref.at[chip], dual_out.at[CORES * chip + j], sems.at[chip]))
        sends[-1].start()
    half = plan.quads // CORES
    flip = quad // half == 1
    for step in range(half):
        mine, theirs = posts[step][...].astype(f32), posts[half + step][...].astype(f32)
        low, high = jnp.where(flip, theirs, mine), jnp.where(flip, mine, theirs)
        post_ref[step, pl.ds(0, plan.cells, stride=2), :] = jnp.concatenate([low[:, :HALF], high[:, :HALF]], 1)
        post_ref[step, pl.ds(1, plan.cells, stride=2), :] = jnp.concatenate([low[:, HALF:], high[:, HALF:]], 1)
        freq = CORES * ((quad & (half - 1)) ^ step) + j
        sends.append(pltpu.make_async_copy(post_ref.at[step], post_out.at[freq], sems.at[plan.chips + step]))
        sends[-1].start()
    for copy in sends:
        copy.wait()


def on_device(forward_map, observed, noise_var, prior_rows, prior_scale):
    frequencies, halves, sensors, cells = forward_map.shape
    pairs, quads, count = (lax.axis_size(a) for a in ("pair", "quad", "side"))
    groups = pairs * CORES
    plan = Plan(groups, quads, sensors, cells, prior_rows.shape[1])
    pair, core, quad = (lax.axis_index(a) for a in ("pair", "core", "quad"))
    place = jnp.stack([pair, quad, core]).astype(jnp.int32)
    scales = lax.dynamic_slice_in_dim(prior_scale, CORES * (pair * quads + quad), CORES, 0)

    def swap(x, axes, distance):
        return lax.ppermute(x, axes, [(i, i ^ distance) for i in range(lax.axis_size(axes))])

    flat = forward_map.reshape(frequencies, halves * sensors, cells)
    line = max(plan.extra(0, d) for d in range(plan.chips))
    order, starts, maps = plan.order(), {}, []
    for batch, held in enumerate(BATCHES):
        for i, j in enumerate(held):
            starts[j] = (batch, i * plan.map_rows)
        operands = [place, flat, observed, prior_rows, noise_var.reshape(1, sensors)]
        messages = call(
            functools.partial(pack_kernel, plan, batch),
            [SMEM, HBM, HBM, VMEM, VMEM] + [ANY] * batch,
            [shape((plan.rows(batch, d), cells), bf16) for d in range(plan.chips)],
            [
                pltpu.VMEM((plan.pairs, CORES, halves, sensors, LANES), f32),
                pltpu.VMEM((1 + plan.pairs, line, cells), bf16),
                pltpu.SemaphoreType.DMA((plan.chips + 3, max(plan.chips, quads, CORES))),
            ],
            [ANY] * plan.chips,
            moved=10 * 2**20,
        )(*operands, *[maps[i][order[2]] for i in range(batch)])
        mine = [messages[0]] + [None] * (plan.chips - 1)
        for d in order:
            mine[d] = swap(messages[d], ("pair", "quad"), d)
        maps.append(mine + [swap(x, "core", 1) for x in mine])

    prior, noise, *streams = call(
        functools.partial(gather_kernel, plan),
        [SMEM] + [VMEM] * (1 + 2 * plan.chips),
        [shape((quads, cells, plan.width), bf16), shape((groups, sensors, LANES), f32)]
        + [shape((groups, sensors, LANES), bf16)] * CORES,
        moved=4 * 2**20,
    )(place, prior_rows, *maps[0])

    def over_sides(partial):
        if count == 2:
            return [partial, swap(partial, "side", 1)]
        return [lax.psum(partial, "side")]

    wide, narrow = shape((groups, sensors, LANES), f32), shape((groups, sensors, LANES), bf16)
    sides_scratch = pltpu.VMEM((groups, LANES, halves * sensors), bf16)

    def step(stage, j, preds):
        batch, start = starts[j]
        operands = [scales[j:j + 1], prior, streams[j], noise] + maps[batch] + preds
        return call(
            functools.partial(step_kernel, plan, stage, start, len(preds)),
            [SMEM] + [VMEM] * (len(operands) - 1),
            [narrow] if stage == 0 else [wide, narrow],
            [sides_scratch],
            flops=2**31,
            moved=8 * 2**20,
        )(*operands)

    outputs = []
    for j in range(CORES):
        batch, start = starts[j]
        preds = over_sides(step(0, j, [])[0])
        held, partial = step(1, j, preds)
        preds = over_sides(partial)
        final, dual = call(
            functools.partial(last_kernel, plan, len(preds)),
            [SMEM] + [VMEM] * (3 + len(preds)),
            [narrow, shape((groups, quads, sensors, LANES), bf16)],
            moved=2 * 2**20,
        )(place, noise, streams[j], held, *preds)
        dual = lax.all_to_all(
            dual.reshape(groups * quads, sensors, LANES), ("pair", "core", "quad"), split_axis=0, concat_axis=0, tiled=True
        ).reshape(pairs, CORES, quads, sensors, LANES)
        posts = call(
            functools.partial(post_kernel, plan, start),
            [SMEM, SMEM] + [VMEM] * (2 + 2 * plan.chips),
            [shape((cells, LANES), bf16)] * quads,
            [sides_scratch, pltpu.VMEM((quads, cells, LANES), bf16)],
            flops=2**31,
            moved=16 * 2**20,
        )(place, scales[j:j + 1], prior, final, *maps[batch])
        half = quads // CORES
        posts = [lax.ppermute(posts[i], ("core", "quad"), post_route(quads, *divmod(i, half))) for i in range(quads)]
        operands = [place, dual] + posts + outputs
        outputs = call(
            functools.partial(end_kernel, plan, j),
            [SMEM] + [VMEM] * (1 + quads) + [ANY] * len(outputs),
            [shape((frequencies, halves, sensors, LANES), f32), shape((quads, cells * 2, LANES), f32)],
            [
                pltpu.VMEM((plan.chips, halves, sensors, LANES), f32),
                pltpu.VMEM((half, cells * 2, LANES), f32),
                pltpu.SemaphoreType.DMA((plan.chips + half,)),
            ],
            [ANY, ANY],
            moved=8 * 2**20,
            aliases={len(operands) - 2: 0, len(operands) - 1: 1} if j else None,
        )(*operands)
        outputs = list(outputs)
    dual, posterior = outputs
    return dual, posterior.reshape(quads, cells, 2, LANES)


def solution(mesh):
    groups, space = mesh.devices.shape

    def run(forward_map, observed, noise_var, prior_rows, prior_scale):
        quads = forward_map.shape[0] // groups
        split = Mesh(
            mesh.devices.reshape(groups // CORES, CORES, space // quads, quads), ("pair", "core", "side", "quad")
        )
        return jax.shard_map(
            on_device,
            mesh=split,
            in_specs=(
                P(None, None, ("pair", "core"), ("side", "quad")),
                P(None, None, ("pair", "core"), None),
                P(("pair", "core")),
                P(("side", "quad"), None),
                P(),
            ),
            out_specs=(P(None, None, ("pair", "core"), None), P(("pair", "core"), ("side", "quad"), None, None)),
            check_vma=False,
        )(forward_map, observed, noise_var, prior_rows, prior_scale)

    return run
```

```python
import functools

import jax
import jax.numpy as jnp
from jax import lax
from jax.experimental import pallas as pl
from jax.experimental.pallas import tpu as pltpu
from jax.sharding import Mesh, PartitionSpec as P

ITERS = 2
relax_step = 0.25
STREAMS = 2
CORES = 2
LANES = 128
HALF = LANES // 2
VMEM_LIMIT = 16 * 2**20
VMEM = pl.BlockSpec(memory_space=pltpu.VMEM)
SMEM = pl.BlockSpec(memory_space=pltpu.SMEM)
ANY = pl.BlockSpec(memory_space=pl.ANY)
bf16, f32 = jnp.bfloat16, jnp.float32


def shape(dims, dtype):
    return jax.ShapeDtypeStruct(dims, dtype)


def call(kernel, in_specs, out_shape, scratch=(), flops=0, moved=0):
    return pl.pallas_call(
        kernel,
        in_specs=in_specs,
        out_specs=[VMEM] * len(out_shape),
        out_shape=out_shape,
        scratch_shapes=list(scratch),
        cost_estimate=pl.CostEstimate(flops=flops, bytes_accessed=moved, transcendentals=0),
        compiler_params=pltpu.CompilerParams(vmem_limit_bytes=VMEM_LIMIT),
    )


def swap(x, axes, distance):
    count = lax.axis_size(axes)
    return lax.ppermute(x, axes, [(i, i ^ distance) for i in range(count)])


def dot(a, b):
    return jnp.dot(a, b, preferred_element_type=f32)


def dot_nt(a, b):
    return lax.dot_general(a, b, (((1,), (1,)), ((), ())), preferred_element_type=f32)


def data_kernel(groups, quads, place_ref, obs_ref, noise_ref, *refs):
    outs, (held, sems) = refs[:groups], refs[groups:]
    sensors = obs_ref.shape[2]
    copies = []
    for d in range(groups):
        freq = ((place_ref[0] * CORES + place_ref[2]) ^ d) * quads + place_ref[1]
        copies.append(pltpu.make_async_copy(obs_ref.at[freq], held.at[d], sems.at[d]))
        copies[-1].start()
    noise = noise_ref[...]
    high = noise.astype(bf16)
    low = (noise - high.astype(f32)).astype(bf16)
    tail = jnp.concatenate([jnp.broadcast_to(high, (8, sensors)), jnp.broadcast_to(low, (8, sensors))], 0)
    for d in range(groups):
        copies[d].wait()
        re, im = held[d, 0], held[d, 1]
        for s in range(STREAMS):
            part = slice(s * HALF, (s + 1) * HALF)
            outs[d][:sensors, s * LANES:(s + 1) * LANES] = jnp.concatenate([re[:, part], im[:, part]], 1).astype(bf16)
        outs[d][sensors:, :] = tail


def gather_kernel(groups, quads, place_ref, own_ref, *refs):
    came, data = refs[:quads - 1], refs[quads - 1:quads - 1 + groups]
    prior_ref, noise_ref, *streams = refs[quads - 1 + groups:]
    me, quad = place_ref[0] * CORES + place_ref[2], place_ref[1]
    sensors, cells = streams[0].shape[1], own_ref.shape[0]
    on, off = (pl.ds(pl.multiple_of(p * cells, cells), cells) for p in (quad & 1, 1 - (quad & 1)))
    for d in range(0, quads, 2):
        rows = own_ref if d == 0 else came[d - 1]
        prior_ref[quad ^ d] = rows[...]
        prior_ref[quad ^ d ^ 1, :, on] = rows[:, off].T
        prior_ref[quad ^ d ^ 1, :, off] = came[d][...]
    row = lax.broadcasted_iota(jnp.int32, (sensors, sensors), 0)
    col = lax.broadcasted_iota(jnp.int32, (sensors, sensors), 1)
    for d in range(groups):
        for s in range(STREAMS):
            streams[s][me ^ d] = data[d][:sensors, s * LANES:(s + 1) * LANES]
        both = data[d][sensors:, :].astype(f32)
        noise_row = both[0:1, :] + both[8:9, :]
        noise = jnp.sum(jnp.where(row == col, noise_row, 0.0), 1, keepdims=True)
        noise_ref[me ^ d] = jnp.broadcast_to(noise, (sensors, LANES))


def source(map_ref, sides_ref, prior_ref, scale):
    groups, quads, _, cells = map_ref.shape
    per_block = prior_ref.shape[2] // cells
    out = []
    for block in range(quads // per_block):
        members = range(block * per_block, (block + 1) * per_block)
        parts = []
        for q in members:
            u = jnp.zeros((sides_ref.shape[1], cells), f32)
            for g in range(groups):
                u += dot(sides_ref[g], map_ref[g, q])
            parts.append(u.astype(bf16))
        ub = jnp.concatenate(parts, 1)
        out += [(dot_nt(prior_ref[q], ub) * scale).astype(bf16) for q in members]
    return out


def sides(z):
    half = z.shape[1] // 2
    return jnp.concatenate([z, jnp.concatenate([z[:, half:], -z[:, :half]], 1)], 0).T


def step_kernel(stage, n_pred, place_ref, scale_ref, map_ref, prior_ref, obs_ref, noise_ref, *refs):
    groups, quads, double, _ = map_ref.shape
    sensors = double // 2
    preds, refs = refs[:n_pred], refs[n_pred:]
    if stage > 0:
        next_ref, refs = refs[0], refs[1:]
    outs, sides_ref = refs[:-1], refs[-1]
    for g in range(groups):
        obs = obs_ref[g].astype(f32)
        now = relax_step * obs
        if stage > 0:
            predicted = sum(p[g].astype(f32) for p in preds)
            now = now + relax_step * (obs - predicted - noise_ref[g] * now)
            next_ref[g] = now
        sides_ref[g] = sides(now.astype(bf16))
    sources = source(map_ref, sides_ref, prior_ref, scale_ref[0])
    turned = [jnp.concatenate([-v[:, HALF:], v[:, :HALF]], 1) for v in sources]
    for e in reversed(range(groups // CORES)):
        for core in range(CORES):
            g = CORES * (place_ref[0] ^ e) + core if stage > 0 else CORES * e + core
            total = jnp.zeros((sensors, LANES), f32)
            for q in range(quads):
                total += dot(map_ref[g, q, :sensors, :], sources[q]) + dot(map_ref[g, q, sensors:, :], turned[q])
            if stage > 0:
                outs[e][core] = total.astype(bf16)
            else:
                outs[0][g] = total.astype(bf16)


def last_kernel(e, n_pred, place_ref, noise_ref, *refs):
    obs, held, refs = refs[:STREAMS], refs[STREAMS:2 * STREAMS], refs[2 * STREAMS:]
    preds, (keep_ref, give_ref) = refs[:STREAMS * n_pred], refs[STREAMS * n_pred:]
    for out, core in ((give_ref, 1 - place_ref[2]), (keep_ref, place_ref[2])):
        g = CORES * (place_ref[0] ^ e) + core
        parts = []
        for s in range(STREAMS):
            now = held[s][g]
            predicted = sum(p[core].astype(f32) for p in preds[s * n_pred:(s + 1) * n_pred])
            parts.append(now + relax_step * (obs[s][g].astype(f32) - predicted - noise_ref[g] * now))
        out[:, :LANES] = jnp.concatenate([p[:, :HALF] for p in parts], 1).astype(bf16)
        out[:, LANES:] = jnp.concatenate([p[:, HALF:] for p in parts], 1).astype(bf16)


def send_kernel(place_ref, keep_ref, got_ref, out_ref):
    out_ref[place_ref[2]] = keep_ref[...]
    out_ref[1 - place_ref[2]] = got_ref[...]


def post_kernel(pairs, place_ref, scale_ref, map_ref, prior_ref, *refs):
    keeps, gives, refs = refs[:pairs], refs[pairs:2 * pairs], refs[2 * pairs + 1:]
    outs, (sides_ref, held_ref) = refs[:-2], refs[-2:]
    for e in range(pairs):
        first = CORES * (place_ref[0] ^ e)
        sides_ref[first + place_ref[2]] = sides(keeps[e][...])
        sides_ref[first + 1 - place_ref[2]] = sides(gives[e][...])
    for q, v in enumerate(source(map_ref, sides_ref, prior_ref, scale_ref[0])):
        held_ref[q] = v
    for d, out in enumerate(outs):
        out[...] = held_ref[place_ref[1] ^ d]


def end_kernel(chips, quads, place_ref, *refs):
    duals, posts, (dual_ref, post_ref) = refs[:chips], refs[chips:chips + quads], refs[chips + quads:]
    pair, quad = place_ref[0], place_ref[1]
    cells = post_ref.shape[1] // 2
    for chip in range(chips):
        e, d = divmod(chip, quads)
        for core in range(CORES):
            freq = (CORES * (pair ^ e) + core) * quads + (quad ^ d)
            dual_ref[freq, 0] = duals[chip][core, :, :LANES].astype(f32)
            dual_ref[freq, 1] = duals[chip][core, :, LANES:].astype(f32)
    for d in range(quads):
        post_ref[quad ^ d, pl.ds(0, cells, stride=2), :] = posts[d][:, :LANES].astype(f32)
        post_ref[quad ^ d, pl.ds(1, cells, stride=2), :] = posts[d][:, LANES:].astype(f32)


def on_device(forward_map, observed, noise_var, prior_rows, prior_scale):
    frequencies, halves, sensors, cells = forward_map.shape
    groups, quads, sides = (lax.axis_size(a) for a in ("sensor", "quad", "side"))
    width = prior_rows.shape[1]
    pairs = groups // CORES
    me, quad = lax.axis_index("sensor"), lax.axis_index("quad")
    place = jnp.stack([me // CORES, quad, me % CORES]).astype(jnp.int32)
    scale = lax.dynamic_slice_in_dim(prior_scale, me * quads + quad, 1, 0)
    both = ("sensor", "quad")

    held = lax.all_to_all(
        forward_map.reshape(frequencies, halves * sensors, cells), both, split_axis=0, concat_axis=0, tiled=True
    ).reshape(groups, quads, halves * sensors, cells)

    data = call(
        functools.partial(data_kernel, groups, quads),
        [SMEM, ANY, VMEM],
        [shape((sensors + 16, STREAMS * LANES), bf16)] * groups,
        [pltpu.VMEM((groups, halves, sensors, LANES), f32), pltpu.SemaphoreType.DMA((groups,))],
        moved=groups * sensors * LANES * 12,
    )(place, observed, noise_var.reshape(1, sensors))
    data = [data[0]] + [swap(data[d], "sensor", d) for d in range(1, groups)]
    diagonal = lax.dynamic_slice_in_dim(prior_rows, quad % 2 * cells, cells, 1)
    came = [swap(diagonal if d % 2 else prior_rows, "quad", d) for d in range(1, quads)]
    prior, noise, *streams = call(
        functools.partial(gather_kernel, groups, quads),
        [SMEM] + [VMEM] * (quads + groups),
        [shape((quads, cells, width), bf16), shape((groups, sensors, LANES), f32)]
        + [shape((groups, sensors, LANES), bf16)] * STREAMS,
        moved=8 * 2**20,
    )(place, prior_rows, *came, *data)

    def over_sides(partial):
        if sides == 2:
            return [partial, swap(partial, "side", 1)]
        return [lax.psum(partial, "side")]

    wide, narrow = shape((groups, sensors, LANES), f32), shape((groups, sensors, LANES), bf16)
    couple, full = shape((CORES, sensors, LANES), bf16), shape((sensors, 2 * LANES), bf16)

    def step(stage, obs, preds):
        operands = [place, scale, held, prior, obs, noise] + preds
        return call(
            functools.partial(step_kernel, stage, len(preds)),
            [SMEM, SMEM] + [VMEM] * (len(operands) - 2),
            [wide] + [couple] * pairs if stage > 0 else [narrow],
            [pltpu.VMEM((groups, LANES, halves * sensors), bf16)],
            flops=2**31,
            moved=8 * 2**20,
        )(*operands)

    first = [over_sides(step(0, streams[s], [])[0]) for s in range(STREAMS)]
    multiplier, partials = [], []
    for s in range(STREAMS):
        out, *parts = step(1, streams[s], first[s])
        multiplier.append(out)
        partials.append(parts)
    keeps, gives, duals = [None] * pairs, [None] * pairs, {}
    for e in reversed(range(pairs)):
        preds = [over_sides(partials[s][e]) for s in range(STREAMS)]
        count = len(preds[0])
        keeps[e], gives[e] = call(
            functools.partial(last_kernel, e, count),
            [SMEM] + [VMEM] * (1 + STREAMS * (2 + count)),
            [full, full],
            moved=2 * 2**20,
        )(place, noise, *streams, *multiplier, *[p for pair in preds for p in pair])
        message = call(
            send_kernel,
            [SMEM, VMEM, VMEM],
            [shape((CORES, sensors, 2 * LANES), bf16)],
            moved=2**20,
        )(place, keeps[e], swap(gives[e], "sensor", 1))[0]
        for d in reversed(range(quads)):
            away = e * quads + d
            duals[away] = swap(message, both, CORES * e * quads + d) if away else message
    post = call(
        functools.partial(post_kernel, pairs),
        [SMEM, SMEM] + [VMEM] * (2 + 2 * pairs) + [ANY],
        [shape((cells, 2 * LANES), bf16)] * quads,
        [pltpu.VMEM((groups, 2 * LANES, halves * sensors), bf16), pltpu.VMEM((quads, cells, 2 * LANES), bf16)],
        flops=2**31,
        moved=8 * 2**20,
    )(place, scale, held, prior, *keeps, *gives, duals[(pairs - 1) * quads])
    post = [post[0]] + [swap(post[d], "quad", d) for d in range(1, quads)]
    dual, posterior = call(
        functools.partial(end_kernel, pairs * quads, quads),
        [SMEM] + [VMEM] * (pairs * quads + quads),
        [shape((frequencies, halves, sensors, LANES), f32), shape((quads, cells * 2, LANES), f32)],
        moved=8 * 2**20,
    )(place, *[duals[i] for i in range(pairs * quads)], *post)
    return dual, posterior.reshape(quads, cells, 2, LANES)


def solution(mesh):
    groups, space = mesh.devices.shape

    def run(forward_map, observed, noise_var, prior_rows, prior_scale):
        quads = forward_map.shape[0] // groups
        split = Mesh(mesh.devices.reshape(groups, space // quads, quads), ("sensor", "side", "quad"))
        return jax.shard_map(
            on_device,
            mesh=split,
            in_specs=(
                P(None, None, "sensor", ("side", "quad")),
                P(None, None, "sensor", None),
                P("sensor"),
                P(("side", "quad"), None),
                P(),
            ),
            out_specs=(P(None, None, "sensor", None), P("sensor", ("side", "quad"), None, None)),
            check_vma=False,
        )(forward_map, observed, noise_var, prior_rows, prior_scale)

    return run
```

```python
import functools

import jax
import jax.numpy as jnp
from jax import lax
from jax.experimental import pallas as pl
from jax.experimental.pallas import tpu as pltpu
from jax.sharding import Mesh, PartitionSpec as P

ITERS = 2
relax_step = 0.25
STREAMS = 2
CORES = 2
LANES = 128
HALF = LANES // 2
VMEM_LIMIT = 16 * 2**20
VMEM = pl.BlockSpec(memory_space=pltpu.VMEM)
SMEM = pl.BlockSpec(memory_space=pltpu.SMEM)
ANY = pl.BlockSpec(memory_space=pl.ANY)
bf16, f32 = jnp.bfloat16, jnp.float32


def shape(dims, dtype):
    return jax.ShapeDtypeStruct(dims, dtype)


def call(kernel, in_specs, out_shape, scratch=(), out_specs=None, flops=0, moved=0):
    return pl.pallas_call(
        kernel,
        in_specs=in_specs,
        out_specs=out_specs or [VMEM] * len(out_shape),
        out_shape=out_shape,
        scratch_shapes=list(scratch),
        cost_estimate=pl.CostEstimate(flops=flops, bytes_accessed=moved, transcendentals=0),
        compiler_params=pltpu.CompilerParams(vmem_limit_bytes=VMEM_LIMIT),
    )


def swap(x, axes, distance):
    count = lax.axis_size(axes)
    return lax.ppermute(x, axes, [(i, i ^ distance) for i in range(count)])


def dot(a, b):
    return jnp.dot(a, b, preferred_element_type=f32)


def dot_nt(a, b):
    return lax.dot_general(a, b, (((1,), (1,)), ((), ())), preferred_element_type=f32)


def data_kernel(groups, quads, place_ref, obs_ref, noise_ref, *refs):
    outs, (held, sems) = refs[:groups], refs[groups:]
    sensors = obs_ref.shape[2]
    copies = []
    for d in range(groups):
        freq = ((place_ref[0] * CORES + place_ref[2]) ^ d) * quads + place_ref[1]
        copies.append(pltpu.make_async_copy(obs_ref.at[freq], held.at[d], sems.at[d]))
        copies[-1].start()
    noise = noise_ref[...]
    high = noise.astype(bf16)
    low = (noise - high.astype(f32)).astype(bf16)
    tail = jnp.concatenate([jnp.broadcast_to(high, (8, sensors)), jnp.broadcast_to(low, (8, sensors))], 0)
    for d in range(groups):
        copies[d].wait()
        re, im = held[d, 0], held[d, 1]
        for s in range(STREAMS):
            part = slice(s * HALF, (s + 1) * HALF)
            outs[d][:sensors, s * LANES:(s + 1) * LANES] = jnp.concatenate([re[:, part], im[:, part]], 1).astype(bf16)
        outs[d][sensors:, :] = tail


def prior_kernel(place_ref, own_ref, after_ref, full_ref, diagonal_ref):
    cells = own_ref.shape[0]
    full_ref[...] = own_ref[...]
    diagonal_ref[...] = own_ref[:, pl.ds(pl.multiple_of((place_ref[1] & 1) * cells, cells), cells)]


def gather_kernel(groups, quads, place_ref, own_ref, *refs):
    came, data = refs[:quads - 1], refs[quads - 1:quads - 1 + groups]
    prior_ref, noise_ref, *streams = refs[quads - 1 + groups:]
    me, quad = place_ref[0] * CORES + place_ref[2], place_ref[1]
    sensors, cells = streams[0].shape[1], own_ref.shape[0]
    on, off = (pl.ds(pl.multiple_of(p * cells, cells), cells) for p in (quad & 1, 1 - (quad & 1)))
    for d in range(0, quads, 2):
        rows = own_ref if d == 0 else came[d - 1]
        prior_ref[quad ^ d] = rows[...]
        prior_ref[quad ^ d ^ 1, :, on] = rows[:, off].T
        prior_ref[quad ^ d ^ 1, :, off] = came[d][...]
    row = lax.broadcasted_iota(jnp.int32, (sensors, sensors), 0)
    col = lax.broadcasted_iota(jnp.int32, (sensors, sensors), 1)
    for d in range(groups):
        for s in range(STREAMS):
            streams[s][me ^ d] = data[d][:sensors, s * LANES:(s + 1) * LANES]
        both = data[d][sensors:, :].astype(f32)
        noise_row = both[0:1, :] + both[8:9, :]
        noise = jnp.sum(jnp.where(row == col, noise_row, 0.0), 1, keepdims=True)
        noise_ref[me ^ d] = jnp.broadcast_to(noise, (sensors, LANES))


def source(map_ref, sides_ref, prior_ref, scale, ready=None):
    groups, quads, _, cells = map_ref.shape
    per_block = prior_ref.shape[2] // cells
    out = []
    for block in range(quads // per_block):
        members = range(block * per_block, (block + 1) * per_block)
        parts = []
        for q in members:
            u = jnp.zeros((sides_ref.shape[1], cells), f32)
            for g in range(groups):
                if ready is not None:
                    ready(g, q)
                u += dot(sides_ref[g], map_ref[g, q])
            parts.append(u.astype(bf16))
        ub = jnp.concatenate(parts, 1)
        out += [(dot_nt(prior_ref[q], ub) * scale).astype(bf16) for q in members]
    return out


def sides(z):
    half = z.shape[1] // 2
    return jnp.concatenate([z, jnp.concatenate([z[:, half:], -z[:, :half]], 1)], 0).T


def step_kernel(stage, load, n_pred, place_ref, scale_ref, map_ref, prior_ref, obs_ref, noise_ref, *refs):
    groups, quads, double, _ = map_ref.shape
    sensors = double // 2
    ready = None
    if load:
        copy_ref, sems, refs = refs[1], refs[3], refs[:1] + refs[2:3]
        copies = {}
        for q in range(quads):
            for g in range(groups):
                copies[g, q] = pltpu.make_async_copy(map_ref.at[g, q], copy_ref.at[g, q], sems.at[g, q])
                copies[g, q].start()
        map_ref, ready = copy_ref, lambda g, q: copies[g, q].wait()
    preds, refs = refs[:n_pred], refs[n_pred:]
    if stage > 0:
        next_ref, refs = refs[0], refs[1:]
    outs, sides_ref = refs[:-1], refs[-1]
    for g in range(groups):
        obs = obs_ref[g].astype(f32)
        now = relax_step * obs
        if stage > 0:
            predicted = sum(p[g].astype(f32) for p in preds)
            now = now + relax_step * (obs - predicted - noise_ref[g] * now)
            next_ref[g] = now
        sides_ref[g] = sides(now.astype(bf16))
    sources = source(map_ref, sides_ref, prior_ref, scale_ref[0], ready)
    turned = [jnp.concatenate([-v[:, HALF:], v[:, :HALF]], 1) for v in sources]
    for e in reversed(range(groups // CORES)):
        for core in range(CORES):
            g = CORES * (place_ref[0] ^ e) + core if stage > 0 else CORES * e + core
            total = jnp.zeros((sensors, LANES), f32)
            for q in range(quads):
                total += dot(map_ref[g, q, :sensors, :], sources[q]) + dot(map_ref[g, q, sensors:, :], turned[q])
            if stage > 0:
                outs[e][core] = total.astype(bf16)
            else:
                outs[0][g] = total.astype(bf16)


def last_kernel(e, n_pred, place_ref, noise_ref, *refs):
    obs, held, refs = refs[:STREAMS], refs[STREAMS:2 * STREAMS], refs[2 * STREAMS:]
    preds, (keep_ref, give_ref) = refs[:STREAMS * n_pred], refs[STREAMS * n_pred:]
    for out, core in ((give_ref, 1 - place_ref[2]), (keep_ref, place_ref[2])):
        g = CORES * (place_ref[0] ^ e) + core
        parts = []
        for s in range(STREAMS):
            now = held[s][g]
            predicted = sum(p[core].astype(f32) for p in preds[s * n_pred:(s + 1) * n_pred])
            parts.append(now + relax_step * (obs[s][g].astype(f32) - predicted - noise_ref[g] * now))
        out[:, :LANES] = jnp.concatenate([p[:, :HALF] for p in parts], 1).astype(bf16)
        out[:, LANES:] = jnp.concatenate([p[:, HALF:] for p in parts], 1).astype(bf16)


def send_kernel(place_ref, keep_ref, got_ref, *refs):
    posts, outs = refs[:len(refs) // 2], refs[len(refs) // 2:]
    for i, out in enumerate(outs):
        out[place_ref[2]] = keep_ref[...]
        out[1 - place_ref[2]] = got_ref[...]
        if posts:
            out[CORES] = posts[i][...]


def post_kernel(pairs, place_ref, scale_ref, map_ref, prior_ref, *refs):
    keeps, gives, refs = refs[:pairs], refs[pairs:2 * pairs], refs[2 * pairs:]
    outs, (sides_ref, held_ref) = refs[:-2], refs[-2:]
    for e in range(pairs):
        first = CORES * (place_ref[0] ^ e)
        sides_ref[first + place_ref[2]] = sides(keeps[e][...])
        sides_ref[first + 1 - place_ref[2]] = sides(gives[e][...])
    for q, v in enumerate(source(map_ref, sides_ref, prior_ref, scale_ref[0])):
        held_ref[q] = v
    for d, out in enumerate(outs):
        out[...] = held_ref[place_ref[1] ^ d]


def end_kernel(chips, quads, place_ref, *refs):
    came, (dual_out, post_out, dual_ref, post_ref, sems) = refs[:chips], refs[chips:]
    pair, quad = place_ref[0], place_ref[1]
    cells = post_ref.shape[1] // 2
    sends = []
    for chip in reversed(range(chips)):
        e, d = divmod(chip, quads)
        for core in range(CORES):
            freq = (CORES * (pair ^ e) + core) * quads + (quad ^ d)
            for part in range(2):
                dual_ref[chip, core, part] = came[chip][core, :, part * LANES:(part + 1) * LANES].astype(f32)
            sends.append(pltpu.make_async_copy(dual_ref.at[chip, core], dual_out.at[freq], sems.at[chip, core]))
            sends[-1].start()
        if e == 0:
            post_ref[d, pl.ds(0, cells, stride=2), :] = came[chip][CORES, :, :LANES].astype(f32)
            post_ref[d, pl.ds(1, cells, stride=2), :] = came[chip][CORES, :, LANES:].astype(f32)
            sends.append(pltpu.make_async_copy(post_ref.at[d], post_out.at[quad ^ d], sems.at[chip, CORES]))
            sends[-1].start()
    for copy in sends:
        copy.wait()


def on_device(forward_map, observed, noise_var, prior_rows, prior_scale):
    frequencies, halves, sensors, cells = forward_map.shape
    groups, quads, sides = (lax.axis_size(a) for a in ("sensor", "quad", "side"))
    width = prior_rows.shape[1]
    pairs = groups // CORES
    me, quad = lax.axis_index("sensor"), lax.axis_index("quad")
    place = jnp.stack([me // CORES, quad, me % CORES]).astype(jnp.int32)
    scale = lax.dynamic_slice_in_dim(prior_scale, me * quads + quad, 1, 0)
    both = ("sensor", "quad")

    held = lax.all_to_all(
        forward_map.reshape(frequencies, halves * sensors, cells), both, split_axis=0, concat_axis=0, tiled=True
    ).reshape(groups, quads, halves * sensors, cells)

    data = call(
        functools.partial(data_kernel, groups, quads),
        [SMEM, ANY, VMEM],
        [shape((sensors + 16, STREAMS * LANES), bf16)] * groups,
        [pltpu.VMEM((groups, halves, sensors, LANES), f32), pltpu.SemaphoreType.DMA((groups,))],
        moved=groups * sensors * LANES * 12,
    )(place, observed, noise_var.reshape(1, sensors))
    data = [data[0]] + [swap(data[d], "sensor", d) for d in range(1, groups)]
    rows, diagonal = call(
        prior_kernel,
        [SMEM, VMEM, ANY],
        [shape((cells, width), bf16), shape((cells, cells), bf16)],
    )(place, prior_rows, data[1])
    came = [swap(diagonal if d % 2 else rows, "quad", d) for d in range(1, quads)]
    prior, noise, *streams = call(
        functools.partial(gather_kernel, groups, quads),
        [SMEM] + [VMEM] * (quads + groups),
        [shape((quads, cells, width), bf16), shape((groups, sensors, LANES), f32)]
        + [shape((groups, sensors, LANES), bf16)] * STREAMS,
        moved=8 * 2**20,
    )(place, prior_rows, *came, *data)

    def over_sides(partial):
        if sides == 2:
            return [partial, swap(partial, "side", 1)]
        return [lax.psum(partial, "side")]

    wide, narrow = shape((groups, sensors, LANES), f32), shape((groups, sensors, LANES), bf16)
    couple, full = shape((CORES, sensors, LANES), bf16), shape((sensors, 2 * LANES), bf16)

    def step(stage, obs, preds, where, load=False):
        operands = [place, scale, where, prior, obs, noise] + preds
        out = [wide] + [couple] * pairs if stage > 0 else [narrow]
        scratch = [pltpu.VMEM((groups, LANES, halves * sensors), bf16)]
        if load:
            out.append(shape(held.shape, bf16))
            scratch.append(pltpu.SemaphoreType.DMA((groups, quads)))
        return call(
            functools.partial(step_kernel, stage, load, len(preds)),
            [SMEM, SMEM, ANY if load else VMEM] + [VMEM] * (len(operands) - 3),
            out,
            scratch,
            flops=2**31,
            moved=8 * 2**20,
        )(*operands)

    partial, near = step(0, streams[0], [], held, True)
    first = [over_sides(partial)]
    first += [over_sides(step(0, streams[s], [], near)[0]) for s in range(1, STREAMS)]
    multiplier, partials = [], []
    for s in range(STREAMS):
        out, *parts = step(1, streams[s], first[s], near)
        multiplier.append(out)
        partials.append(parts)
    keeps, gives, duals = [None] * pairs, [None] * pairs, {}
    for e in reversed(range(pairs)):
        preds = [over_sides(partials[s][e]) for s in range(STREAMS)]
        count = len(preds[0])
        keeps[e], gives[e] = call(
            functools.partial(last_kernel, e, count),
            [SMEM] + [VMEM] * (1 + STREAMS * (2 + count)),
            [full, full],
            moved=2 * 2**20,
        )(place, noise, *streams, *multiplier, *[p for pair in preds for p in pair])
        got = swap(gives[e], "sensor", 1)
        posts = []
        if e == 0:
            posts = call(
                functools.partial(post_kernel, pairs),
                [SMEM, SMEM] + [VMEM] * (2 + 2 * pairs),
                [shape((cells, 2 * LANES), bf16)] * quads,
                [pltpu.VMEM((groups, 2 * LANES, halves * sensors), bf16), pltpu.VMEM((quads, cells, 2 * LANES), bf16)],
                flops=2**31,
                moved=8 * 2**20,
            )(place, scale, near, prior, *keeps, *gives)
        messages = call(
            send_kernel,
            [SMEM] + [VMEM] * (2 + len(posts)),
            [shape((CORES + (e == 0), sensors, 2 * LANES), bf16)] * (len(posts) or 1),
            moved=2**20,
        )(place, keeps[e], got, *posts)
        for d in reversed(range(quads)):
            message = messages[d] if e == 0 else messages[0]
            duals[e * quads + d] = swap(message, both, CORES * e * quads + d) if e + d else message
    dual, posterior = call(
        functools.partial(end_kernel, pairs * quads, quads),
        [SMEM] + [VMEM] * (pairs * quads),
        [shape((frequencies, halves, sensors, LANES), f32), shape((quads, cells * 2, LANES), f32)],
        [
            pltpu.VMEM((pairs * quads, CORES, halves, sensors, LANES), f32),
            pltpu.VMEM((quads, cells * 2, LANES), f32),
            pltpu.SemaphoreType.DMA((pairs * quads, CORES + 1)),
        ],
        [ANY, ANY],
        moved=8 * 2**20,
    )(place, *[duals[i] for i in range(pairs * quads)])
    return dual, posterior.reshape(quads, cells, 2, LANES)


def solution(mesh):
    groups, space = mesh.devices.shape

    def run(forward_map, observed, noise_var, prior_rows, prior_scale):
        quads = forward_map.shape[0] // groups
        split = Mesh(mesh.devices.reshape(groups, space // quads, quads), ("sensor", "side", "quad"))
        return jax.shard_map(
            on_device,
            mesh=split,
            in_specs=(
                P(None, None, "sensor", ("side", "quad")),
                P(None, None, "sensor", None),
                P("sensor"),
                P(("side", "quad"), None),
                P(),
            ),
            out_specs=(P(None, None, "sensor", None), P("sensor", ("side", "quad"), None, None)),
            check_vma=False,
        )(forward_map, observed, noise_var, prior_rows, prior_scale)

    return run
```

```python
import functools

import jax
import jax.numpy as jnp
from jax import lax
from jax.experimental import pallas as pl
from jax.experimental.pallas import tpu as pltpu
from jax.sharding import Mesh, PartitionSpec as P

ITERS = 2
relax_step = 0.25
CORES = 2
LANES = 128
HALF = LANES // CORES
VMEM_LIMIT = 12 * 2**20
WHOLE_VMEM = 56 * 2**20
VMEM = pl.BlockSpec(memory_space=pltpu.VMEM)
SMEM = pl.BlockSpec(memory_space=pltpu.SMEM)
ANY = pl.BlockSpec(memory_space=pl.ANY)
bf16, f32 = jnp.bfloat16, jnp.float32


def shape(dims, dtype):
    return jax.ShapeDtypeStruct(dims, dtype)


def call(kernel, in_specs, out_shape, scratch=(), out_specs=None, flops=0, moved=0, limit=VMEM_LIMIT):
    return pl.pallas_call(
        kernel,
        in_specs=in_specs,
        out_specs=out_specs or [VMEM] * len(out_shape),
        out_shape=out_shape,
        scratch_shapes=list(scratch),
        cost_estimate=pl.CostEstimate(flops=flops, bytes_accessed=moved, transcendentals=0),
        compiler_params=pltpu.CompilerParams(vmem_limit_bytes=limit),
    )


def dot(a, b):
    return jnp.dot(a, b, preferred_element_type=f32)


def dot_nt(a, b):
    return lax.dot_general(a, b, (((1,), (1,)), ((), ())), preferred_element_type=f32)


class Plan:
    def __init__(self, groups, quads, sensors, cells, width):
        self.groups, self.quads, self.sensors, self.cells, self.width = groups, quads, sensors, cells, width
        self.pairs = groups // CORES
        self.chips = self.pairs * quads
        self.per_block = width // cells
        self.map_rows = 2 * sensors
        self.share = cells // CORES

    def extra(self, d):
        e, dq = divmod(d, self.quads)
        if dq == 0:
            return CORES * self.sensors + 16
        return self.share * self.per_block if e == 0 else 0

    def rows(self, d):
        return CORES * self.map_rows + self.extra(d)

    def order(self):
        far, order = self.chips - 1, []
        for d in sorted(range(1, far), key=lambda d: -bin(d).count("1")):
            for x in (d, far - d):
                if x not in order:
                    order.append(x)
        return order[:2] + [far] + order[2:]


def pack_kernel(plan, distances, place_ref, map_ref, obs_ref, prior_ref, noise_ref, *refs):
    refs = refs[-len(distances) - 3:]
    outs, (held, lines, sems) = dict(zip(distances, refs)), refs[len(distances):]
    pair, quad, core = place_ref[0], place_ref[1], place_ref[2]
    at = CORES * plan.map_rows
    data = [d for d in distances if d % plan.quads == 0]
    loads = {}
    for d in data:
        for j in range(CORES):
            freq = (CORES * (pair ^ (d // plan.quads)) + j) * plan.quads + quad
            loads[d, j] = pltpu.make_async_copy(obs_ref.at[freq], held.at[d // plan.quads, j], sems.at[d, j])
            loads[d, j].start()
    copies = []
    for d in distances:
        e, dq = divmod(d, plan.quads)
        for j in range(CORES):
            freq = (CORES * (pair ^ e) + j) * plan.quads + (quad ^ dq)
            to = outs[d].at[pl.ds(j * plan.map_rows, plan.map_rows)]
            copies.append(pltpu.make_async_copy(map_ref.at[freq], to, sems.at[d, CORES + j]))
            copies[-1].start()
    priors = [d for d in distances if 0 < d < plan.quads]
    if priors:
        half = prior_ref[pl.ds(pl.multiple_of(core * plan.share, plan.share), plan.share), :]
        for k in range(plan.per_block):
            lines[0, k * plan.share:(k + 1) * plan.share, :] = half[:, k * plan.cells:(k + 1) * plan.cells]
        size = plan.share * plan.per_block
        for d in priors:
            to = outs[d].at[pl.ds(at, size)]
            copies.append(pltpu.make_async_copy(lines.at[0, pl.ds(0, size)], to, sems.at[d, 2 * CORES]))
            copies[-1].start()
    if data:
        noise = noise_ref[...]
        high = noise.astype(bf16)
        low = (noise - high.astype(f32)).astype(bf16)
        wide = (8, plan.sensors)
        tail = jnp.concatenate([jnp.broadcast_to(high, wide), jnp.broadcast_to(low, wide)], 0)
    for d in data:
        e = d // plan.quads
        for j in range(CORES):
            loads[d, j].wait()
            re, im = held[e, j, 0], held[e, j, 1]
            for s in range(CORES):
                part = slice(s * HALF, (s + 1) * HALF)
                lines[1 + e, j * plan.sensors:(j + 1) * plan.sensors, s * LANES:(s + 1) * LANES] = (
                    jnp.concatenate([re[:, part], im[:, part]], 1).astype(bf16)
                )
        size = plan.extra(d)
        lines[1 + e, size - 16:size, :] = tail
        to = outs[d].at[pl.ds(at, size)]
        copies.append(pltpu.make_async_copy(lines.at[1 + e, pl.ds(0, size)], to, sems.at[d, 2 * CORES]))
        copies[-1].start()
    for copy in copies:
        copy.wait()


def gather_kernel(plan, place_ref, own_ref, *refs):
    mine, theirs = refs[:plan.chips], refs[plan.chips:2 * plan.chips]
    prior_ref, noise_ref, *streams = refs[2 * plan.chips:]
    quad, core = place_ref[1], place_ref[2]
    at = CORES * plan.map_rows
    share, cells, sensors = plan.share, plan.cells, plan.sensors
    for k in range(plan.per_block):
        column = k ^ (quad & (plan.per_block - 1))
        to = slice(k * cells, (k + 1) * cells)
        prior_ref[0, :, to] = own_ref[:, pl.ds(pl.multiple_of(column * cells, cells), cells)]
        for dq in range(1, plan.quads):
            span = pl.ds(pl.multiple_of(at + column * share, share), share)
            for part, ref in ((core, mine[dq]), (1 - core, theirs[dq])):
                prior_ref[dq, pl.ds(pl.multiple_of(part * share, share), share), to] = ref[span, :]
    row = lax.broadcasted_iota(jnp.int32, (sensors, sensors), 0)
    col = lax.broadcasted_iota(jnp.int32, (sensors, sensors), 1)
    lanes = pl.ds(pl.multiple_of(core * LANES, LANES), LANES)
    for e in range(plan.pairs):
        for s, refs_s in enumerate((mine, theirs)):
            ref, r = refs_s[e * plan.quads], CORES * e + s
            for j in range(CORES):
                streams[j][r] = ref[at + j * sensors:at + (j + 1) * sensors, lanes]
            both = ref[at + CORES * sensors:, :].astype(f32)
            noise_row = both[0:1, :] + both[8:9, :]
            noise = jnp.sum(jnp.where(row == col, noise_row, 0.0), 1, keepdims=True)
            noise_ref[r] = jnp.broadcast_to(noise, (sensors, LANES))


def sides(z):
    return jnp.concatenate([z, jnp.concatenate([z[:, HALF:], -z[:, :HALF]], 1)], 0).T


def source(plan, chunk, sides_ref, prior_ref, scale):
    out = []
    for block in range(plan.quads // plan.per_block):
        quads = range(block * plan.per_block, (block + 1) * plan.per_block)
        parts = []
        for dq in quads:
            u = jnp.zeros((LANES, plan.cells), f32)
            for r in range(plan.groups):
                u += dot(sides_ref[r], chunk(r, dq)[...])
            parts.append(u.astype(bf16))
        ub = jnp.concatenate(parts, 1)
        out += [(dot_nt(prior_ref[dq], ub) * scale).astype(bf16) for dq in quads]
    return out


def chunks(plan, refs, start):
    rows = pl.ds(start, plan.map_rows)
    return lambda r, dq: refs[(r % CORES) * plan.chips + r // CORES * plan.quads + dq].at[rows]


def step_kernel(plan, stage, start, n_pred, scale_ref, prior_ref, obs_ref, noise_ref, *refs):
    chunk, refs = chunks(plan, refs, start), refs[2 * plan.chips:]
    preds, refs = refs[:n_pred], refs[n_pred:]
    if stage > 0:
        next_ref, refs = refs[0], refs[1:]
    outs, sides_ref = refs[:-1], refs[-1]
    for r in range(plan.groups):
        obs = obs_ref[r].astype(f32)
        now = relax_step * obs
        if stage > 0:
            predicted = sum(p[r].astype(f32) for p in preds)
            now = now + relax_step * (obs - predicted - noise_ref[r] * now)
            next_ref[r] = now
        sides_ref[r] = sides(now.astype(bf16))
    sources = source(plan, chunk, sides_ref, prior_ref, scale_ref[0])
    turned = [jnp.concatenate([-v[:, HALF:], v[:, :HALF]], 1) for v in sources]
    for r in reversed(range(plan.groups)):
        total = jnp.zeros((plan.sensors, LANES), f32)
        for dq in range(plan.quads):
            block = chunk(r, dq)
            total += dot(block[:plan.sensors, :], sources[dq]) + dot(block[plan.sensors:, :], turned[dq])
        if len(outs) == 1:
            outs[0][r] = total.astype(bf16)
        else:
            outs[r // CORES][r % CORES] = total.astype(bf16)


def last_kernel(plan, e, n_pred, noise_ref, *refs):
    obs, held, refs = refs[:CORES], refs[CORES:2 * CORES], refs[2 * CORES:]
    preds, (keep_ref, give_ref) = refs[:CORES * n_pred], refs[CORES * n_pred:]
    for j in range(CORES):
        for s, out in ((1, give_ref), (0, keep_ref)):
            r = CORES * e + s
            now = held[j][r]
            predicted = sum(p[s].astype(f32) for p in preds[j * n_pred:(j + 1) * n_pred])
            now = now + relax_step * (obs[j][r].astype(f32) - predicted - noise_ref[r] * now)
            out[j] = now.astype(bf16)


def merge(flag, mine, theirs):
    low, high = jnp.where(flag, theirs, mine), jnp.where(flag, mine, theirs)
    re = jnp.concatenate([low[:, :HALF], high[:, :HALF]], 1)
    im = jnp.concatenate([low[:, HALF:], high[:, HALF:]], 1)
    return re, im


def send_kernel(quads, place_ref, keep_ref, got_ref, *refs):
    posts, outs = refs[:-quads], refs[-quads:]
    flag = place_ref[2] == 1
    for d, out in enumerate(outs):
        pieces = [(keep_ref[j], got_ref[j]) for j in range(CORES)]
        if posts:
            pieces.append((posts[0][d], posts[1][d]))
        for i, (mine, theirs) in enumerate(pieces):
            re, im = merge(flag, mine.astype(f32), theirs.astype(f32))
            out[i, :, :LANES] = re.astype(bf16)
            out[i, :, LANES:] = im.astype(bf16)


def post_kernel(plan, place_ref, scale_ref, prior_ref, *refs):
    maps, refs = refs[:2 * plan.chips], refs[2 * plan.chips:]
    keeps, gives, refs = refs[:plan.pairs], refs[plan.pairs:2 * plan.pairs], refs[2 * plan.pairs:]
    mine_ref, give_ref, sides_ref, held_ref = refs
    core = place_ref[2]
    for j in range(CORES):
        chunk = chunks(plan, maps, j * plan.map_rows)
        for r in range(plan.groups):
            sides_ref[r] = sides((gives if r % CORES else keeps)[r // CORES][j])
        for dq, v in enumerate(source(plan, chunk, sides_ref, prior_ref, scale_ref[j])):
            held_ref[j, dq] = v
    mine_ref[...] = held_ref[core]
    give_ref[...] = held_ref[1 - core]


def end_kernel(chips, quads, place_ref, *refs):
    came, (dual_out, post_out, dual_ref, post_ref, sems) = refs[:chips], refs[chips:]
    pair, quad = place_ref[0], place_ref[1]
    cells = post_ref.shape[1] // 2
    sends = []
    for chip in reversed(range(chips)):
        e, d = divmod(chip, quads)
        for j in range(CORES):
            freq = (CORES * (pair ^ e) + j) * quads + (quad ^ d)
            for part in range(2):
                dual_ref[chip, j, part] = came[chip][j, :, part * LANES:(part + 1) * LANES].astype(f32)
            sends.append(pltpu.make_async_copy(dual_ref.at[chip, j], dual_out.at[freq], sems.at[chip, j]))
            sends[-1].start()
        if e == 0:
            post_ref[d, pl.ds(0, cells, stride=2), :] = came[chip][CORES, :, :LANES].astype(f32)
            post_ref[d, pl.ds(1, cells, stride=2), :] = came[chip][CORES, :, LANES:].astype(f32)
            sends.append(pltpu.make_async_copy(post_ref.at[d], post_out.at[quad ^ d], sems.at[chip, CORES]))
            sends[-1].start()
    for copy in sends:
        copy.wait()


def on_device(forward_map, observed, noise_var, prior_rows, prior_scale):
    frequencies, halves, sensors, cells = forward_map.shape
    groups, quads, count = (lax.axis_size(a) for a in ("sensor", "quad", "side"))
    plan = Plan(groups, quads, sensors, cells, prior_rows.shape[1])
    pairs = plan.pairs
    me, quad = lax.axis_index("sensor"), lax.axis_index("quad")
    pair, core = me // CORES, me % CORES
    place = jnp.stack([pair, quad, core]).astype(jnp.int32)
    scales = jnp.stack([prior_scale[(CORES * pair + j) * quads + quad] for j in range(CORES)])
    both = ("sensor", "quad")

    def swap(x, axes, distance):
        return lax.ppermute(x, axes, [(i, i ^ distance) for i in range(lax.axis_size(axes))])

    def to_chip(x, d):
        e, dq = divmod(d, quads)
        return swap(x, both, CORES * e * quads + dq)

    def to_sibling(x):
        return swap(x, "sensor", 1)

    flat = forward_map.reshape(frequencies, halves * sensors, cells)
    line = max(plan.extra(d) for d in range(plan.chips))
    order, mine = plan.order(), [None] * plan.chips
    for distances, after in (([0] + order[:5], None), (order[5:], order[0])):
        messages = call(
            functools.partial(pack_kernel, plan, distances),
            [SMEM, ANY, ANY, VMEM, VMEM] + [ANY] * (after is not None),
            [shape((plan.rows(d), cells), bf16) for d in distances],
            [
                pltpu.VMEM((plan.pairs, CORES, halves, sensors, LANES), f32),
                pltpu.VMEM((1 + plan.pairs, line, cells), bf16),
                pltpu.SemaphoreType.DMA((plan.chips, 2 * CORES + 1)),
            ],
            [ANY] * len(distances),
            moved=2**20,
            limit=WHOLE_VMEM,
        )(place, flat, observed, prior_rows, noise_var.reshape(1, sensors), *([] if after is None else [mine[after]]))
        for d, message in zip(distances, messages):
            mine[d] = to_chip(message, d) if d else message
    maps = mine + [to_sibling(x) for x in mine]

    prior, noise, *streams = call(
        functools.partial(gather_kernel, plan),
        [SMEM] + [VMEM] * (1 + 2 * plan.chips),
        [shape((quads, cells, plan.width), bf16), shape((groups, sensors, LANES), f32)]
        + [shape((groups, sensors, LANES), bf16)] * CORES,
        moved=4 * 2**20,
    )(place, prior_rows, *maps)

    def over_sides(partial):
        if count == 2:
            return [partial, swap(partial, "side", 1)]
        return [lax.psum(partial, "side")]

    wide, narrow = shape((groups, sensors, LANES), f32), shape((groups, sensors, LANES), bf16)
    couple = shape((CORES, sensors, LANES), bf16)
    sides_scratch = pltpu.VMEM((groups, LANES, halves * sensors), bf16)

    def step(stage, j, preds):
        operands = [scales[j:j + 1], prior, streams[j], noise] + maps + preds
        return call(
            functools.partial(step_kernel, plan, stage, j * plan.map_rows, len(preds)),
            [SMEM] + [VMEM] * (len(operands) - 1),
            [narrow] if stage == 0 else [wide] + [couple] * plan.pairs,
            [sides_scratch],
            flops=2**31,
            moved=8 * 2**20,
        )(*operands)

    first = [over_sides(step(0, j, [])[0]) for j in range(CORES)]
    multiplier, partials = [], []
    for j in range(CORES):
        held, *parts = step(1, j, first[j])
        multiplier.append(held)
        partials.append(parts)
    keeps, gives = [None] * plan.pairs, [None] * plan.pairs
    duals = [None] * plan.chips
    for e in reversed(range(plan.pairs)):
        preds = [over_sides(partials[j][e]) for j in range(CORES)]
        preds = preds[0] + preds[1]
        keeps[e], gives[e] = call(
            functools.partial(last_kernel, plan, e, len(preds) // CORES),
            [VMEM] * (1 + 2 * CORES + len(preds)),
            [couple, couple],
            moved=2 * 2**20,
        )(noise, *streams, *multiplier, *preds)
        got, posts = to_sibling(gives[e]), []
        if e == 0:
            cut = shape((quads, cells, LANES), bf16)
            own, other = call(
                functools.partial(post_kernel, plan),
                [SMEM, SMEM] + [VMEM] * (1 + len(maps) + 2 * pairs),
                [cut, cut],
                [sides_scratch, pltpu.VMEM((CORES, quads, cells, LANES), bf16)],
                flops=2**31,
                moved=8 * 2**20,
            )(place, scales, prior, *maps, *keeps, *gives)
            posts = [own, to_sibling(other)]
        kinds = quads if e == 0 else 1
        messages = call(
            functools.partial(send_kernel, kinds),
            [SMEM] + [VMEM] * (2 + len(posts)),
            [shape((CORES + (e == 0), sensors, 2 * LANES), bf16)] * kinds,
            moved=2**20,
        )(place, keeps[e], got, *posts)
        for dq in reversed(range(quads)):
            d = e * quads + dq
            message = messages[dq] if e == 0 else messages[0]
            duals[d] = to_chip(message, d) if d else message
    dual, posterior = call(
        functools.partial(end_kernel, plan.chips, quads),
        [SMEM] + [VMEM] * plan.chips,
        [shape((frequencies, halves, sensors, LANES), f32), shape((quads, cells * 2, LANES), f32)],
        [
            pltpu.VMEM((plan.chips, CORES, halves, sensors, LANES), f32),
            pltpu.VMEM((quads, cells * 2, LANES), f32),
            pltpu.SemaphoreType.DMA((plan.chips, CORES + 1)),
        ],
        [ANY, ANY],
        moved=8 * 2**20,
    )(place, *duals)
    return dual, posterior.reshape(quads, cells, 2, LANES)


def solution(mesh):
    groups, space = mesh.devices.shape

    def run(forward_map, observed, noise_var, prior_rows, prior_scale):
        quads = forward_map.shape[0] // groups
        split = Mesh(mesh.devices.reshape(groups, space // quads, quads), ("sensor", "side", "quad"))
        return jax.shard_map(
            on_device,
            mesh=split,
            in_specs=(
                P(None, None, "sensor", ("side", "quad")),
                P(None, None, "sensor", None),
                P("sensor"),
                P(("side", "quad"), None),
                P(),
            ),
            out_specs=(P(None, None, "sensor", None), P("sensor", ("side", "quad"), None, None)),
            check_vma=False,
        )(forward_map, observed, noise_var, prior_rows, prior_scale)

    return run
```

```python
import functools

import jax
import jax.numpy as jnp
from jax import lax
from jax.experimental import pallas as pl
from jax.experimental.pallas import tpu as pltpu
from jax.sharding import Mesh, PartitionSpec as P

ITERS = 2
relax_step = 0.25
STREAMS = 2
CORES = 2
LANES = 128
HALF = LANES // 2
VMEM_LIMIT = 16 * 2**20
VMEM = pl.BlockSpec(memory_space=pltpu.VMEM)
SMEM = pl.BlockSpec(memory_space=pltpu.SMEM)
ANY = pl.BlockSpec(memory_space=pl.ANY)
bf16, f32 = jnp.bfloat16, jnp.float32


def shape(dims, dtype):
    return jax.ShapeDtypeStruct(dims, dtype)


def call(kernel, in_specs, out_shape, scratch=(), out_specs=None, flops=0, moved=0, aliases=None):
    return pl.pallas_call(
        kernel,
        input_output_aliases=aliases or {},
        in_specs=in_specs,
        out_specs=out_specs or [VMEM] * len(out_shape),
        out_shape=out_shape,
        scratch_shapes=list(scratch),
        cost_estimate=pl.CostEstimate(flops=flops, bytes_accessed=moved, transcendentals=0),
        compiler_params=pltpu.CompilerParams(vmem_limit_bytes=VMEM_LIMIT),
    )


def swap(x, axes, distance):
    count = lax.axis_size(axes)
    return lax.ppermute(x, axes, [(i, i ^ distance) for i in range(count)])


def dot(a, b):
    return jnp.dot(a, b, preferred_element_type=f32)


def dot_nt(a, b):
    return lax.dot_general(a, b, (((1,), (1,)), ((), ())), preferred_element_type=f32)


def data_kernel(groups, quads, place_ref, obs_ref, noise_ref, *refs):
    outs, (held, sems) = refs[:groups], refs[groups:]
    sensors = obs_ref.shape[2]
    copies = []
    for d in range(groups):
        freq = ((place_ref[0] * CORES + place_ref[2]) ^ d) * quads + place_ref[1]
        copies.append(pltpu.make_async_copy(obs_ref.at[freq], held.at[d], sems.at[d]))
        copies[-1].start()
    noise = noise_ref[...]
    high = noise.astype(bf16)
    low = (noise - high.astype(f32)).astype(bf16)
    tail = jnp.concatenate([jnp.broadcast_to(high, (8, sensors)), jnp.broadcast_to(low, (8, sensors))], 0)
    for d in range(groups):
        copies[d].wait()
        re, im = held[d, 0], held[d, 1]
        for s in range(STREAMS):
            part = slice(s * HALF, (s + 1) * HALF)
            outs[d][:sensors, s * LANES:(s + 1) * LANES] = jnp.concatenate([re[:, part], im[:, part]], 1).astype(bf16)
        outs[d][sensors:, :] = tail


def prior_kernel(place_ref, own_ref, after_ref, full_ref, diagonal_ref):
    cells = own_ref.shape[0]
    full_ref[...] = own_ref[...]
    diagonal_ref[...] = own_ref[:, pl.ds(pl.multiple_of((place_ref[1] & 1) * cells, cells), cells)]


def gather_kernel(groups, quads, place_ref, own_ref, *refs):
    came, data = refs[:quads - 1], refs[quads - 1:quads - 1 + groups]
    prior_ref, noise_ref, *streams = refs[quads - 1 + groups:]
    me, quad = place_ref[0] * CORES + place_ref[2], place_ref[1]
    sensors, cells = streams[0].shape[1], own_ref.shape[0]
    on, off = (pl.ds(pl.multiple_of(p * cells, cells), cells) for p in (quad & 1, 1 - (quad & 1)))
    for d in range(0, quads, 2):
        rows = own_ref if d == 0 else came[d - 1]
        prior_ref[quad ^ d] = rows[...]
        prior_ref[quad ^ d ^ 1, :, on] = rows[:, off].T
        prior_ref[quad ^ d ^ 1, :, off] = came[d][...]
    row = lax.broadcasted_iota(jnp.int32, (sensors, sensors), 0)
    col = lax.broadcasted_iota(jnp.int32, (sensors, sensors), 1)
    for d in range(groups):
        for s in range(STREAMS):
            streams[s][me ^ d] = data[d][:sensors, s * LANES:(s + 1) * LANES]
        both = data[d][sensors:, :].astype(f32)
        noise_row = both[0:1, :] + both[8:9, :]
        noise = jnp.sum(jnp.where(row == col, noise_row, 0.0), 1, keepdims=True)
        noise_ref[me ^ d] = jnp.broadcast_to(noise, (sensors, LANES))


def source(map_ref, sides_ref, prior_ref, scale):
    groups, quads, _, cells = map_ref.shape
    per_block = prior_ref.shape[2] // cells
    out = []
    for block in range(quads // per_block):
        members = range(block * per_block, (block + 1) * per_block)
        parts = []
        for q in members:
            u = jnp.zeros((sides_ref.shape[1], cells), f32)
            for g in range(groups):
                u += dot(sides_ref[g], map_ref[g, q])
            parts.append(u.astype(bf16))
        ub = jnp.concatenate(parts, 1)
        out += [(dot_nt(prior_ref[q], ub) * scale).astype(bf16) for q in members]
    return out


def sides(z):
    half = z.shape[1] // 2
    return jnp.concatenate([z, jnp.concatenate([z[:, half:], -z[:, :half]], 1)], 0).T


def bring_kernel(map_ref, out_ref, sem):
    copy = pltpu.make_async_copy(map_ref, out_ref, sem)
    copy.start()
    copy.wait()


def step_kernel(stage, n_pred, place_ref, scale_ref, map_ref, prior_ref, obs_ref, noise_ref, *refs):
    groups, quads, double, _ = map_ref.shape
    sensors = double // 2
    preds, refs = refs[:n_pred], refs[n_pred:]
    if stage > 0:
        next_ref, refs = refs[0], refs[1:]
    outs, sides_ref = refs[:-1], refs[-1]
    for g in range(groups):
        obs = obs_ref[g].astype(f32)
        now = relax_step * obs
        if stage > 0:
            predicted = sum(p[g].astype(f32) for p in preds)
            now = now + relax_step * (obs - predicted - noise_ref[g] * now)
            next_ref[g] = now
        sides_ref[g] = sides(now.astype(bf16))
    sources = source(map_ref, sides_ref, prior_ref, scale_ref[0])
    turned = [jnp.concatenate([-v[:, HALF:], v[:, :HALF]], 1) for v in sources]
    for e in reversed(range(groups // CORES)):
        for core in range(CORES):
            g = CORES * (place_ref[0] ^ e) + core if stage > 0 else CORES * e + core
            total = jnp.zeros((sensors, LANES), f32)
            for q in range(quads):
                total += dot(map_ref[g, q, :sensors, :], sources[q]) + dot(map_ref[g, q, sensors:, :], turned[q])
            if stage > 0:
                outs[e][core] = total.astype(bf16)
            else:
                outs[0][g] = total.astype(bf16)


def last_kernel(e, n_pred, place_ref, noise_ref, *refs):
    obs, held, refs = refs[:STREAMS], refs[STREAMS:2 * STREAMS], refs[2 * STREAMS:]
    preds, (keep_ref, give_ref) = refs[:STREAMS * n_pred], refs[STREAMS * n_pred:]
    for out, core in ((give_ref, 1 - place_ref[2]), (keep_ref, place_ref[2])):
        g = CORES * (place_ref[0] ^ e) + core
        parts = []
        for s in range(STREAMS):
            now = held[s][g]
            predicted = sum(p[core].astype(f32) for p in preds[s * n_pred:(s + 1) * n_pred])
            parts.append(now + relax_step * (obs[s][g].astype(f32) - predicted - noise_ref[g] * now))
        out[:, :LANES] = jnp.concatenate([p[:, :HALF] for p in parts], 1).astype(bf16)
        out[:, LANES:] = jnp.concatenate([p[:, HALF:] for p in parts], 1).astype(bf16)


def send_kernel(place_ref, keep_ref, got_ref, *refs):
    posts, outs = refs[:len(refs) // 2], refs[len(refs) // 2:]
    for i, out in enumerate(outs):
        out[place_ref[2]] = keep_ref[...]
        out[1 - place_ref[2]] = got_ref[...]
        if posts:
            out[CORES] = posts[i][...]


def post_kernel(pairs, place_ref, scale_ref, map_ref, prior_ref, *refs):
    keeps, gives, refs = refs[:pairs], refs[pairs:2 * pairs], refs[2 * pairs + 1:]
    outs, (sides_ref, held_ref) = refs[:-2], refs[-2:]
    for e in range(pairs):
        first = CORES * (place_ref[0] ^ e)
        sides_ref[first + place_ref[2]] = sides(keeps[e][...])
        sides_ref[first + 1 - place_ref[2]] = sides(gives[e][...])
    for q, v in enumerate(source(map_ref, sides_ref, prior_ref, scale_ref[0])):
        held_ref[q] = v
    for d, out in enumerate(outs):
        out[...] = held_ref[place_ref[1] ^ d]


def end_kernel(e, quads, follows, place_ref, *refs):
    came, refs = refs[:quads], refs[quads + follows:]
    dual_out, dual_ref, sems, *post = refs if e else refs[:1] + refs[2:4] + refs[1:2] + refs[4:]
    pair, quad = place_ref[0], place_ref[1]
    sends = []
    for d in reversed(range(quads)):
        for core in range(CORES):
            freq = (CORES * (pair ^ e) + core) * quads + (quad ^ d)
            for part in range(2):
                dual_ref[d, core, part] = came[d][core, :, part * LANES:(part + 1) * LANES].astype(f32)
            sends.append(pltpu.make_async_copy(dual_ref.at[d, core], dual_out.at[freq], sems.at[d, core]))
            sends[-1].start()
        if e == 0:
            post_out, post_ref = post
            cells = post_ref.shape[1] // 2
            post_ref[d, pl.ds(0, cells, stride=2), :] = came[d][CORES, :, :LANES].astype(f32)
            post_ref[d, pl.ds(1, cells, stride=2), :] = came[d][CORES, :, LANES:].astype(f32)
            sends.append(pltpu.make_async_copy(post_ref.at[d], post_out.at[quad ^ d], sems.at[d, CORES]))
            sends[-1].start()
    for copy in sends:
        copy.wait()


def on_device(forward_map, observed, noise_var, prior_rows, prior_scale):
    frequencies, halves, sensors, cells = forward_map.shape
    groups, quads, sides = (lax.axis_size(a) for a in ("sensor", "quad", "side"))
    width = prior_rows.shape[1]
    pairs = groups // CORES
    me, quad = lax.axis_index("sensor"), lax.axis_index("quad")
    place = jnp.stack([me // CORES, quad, me % CORES]).astype(jnp.int32)
    scale = lax.dynamic_slice_in_dim(prior_scale, me * quads + quad, 1, 0)
    both = ("sensor", "quad")

    held = lax.all_to_all(
        forward_map.reshape(frequencies, halves * sensors, cells), both, split_axis=0, concat_axis=0, tiled=True
    ).reshape(groups, quads, halves * sensors, cells)

    data = call(
        functools.partial(data_kernel, groups, quads),
        [SMEM, ANY, VMEM],
        [shape((sensors + 16, STREAMS * LANES), bf16)] * groups,
        [pltpu.VMEM((groups, halves, sensors, LANES), f32), pltpu.SemaphoreType.DMA((groups,))],
        moved=groups * sensors * LANES * 12,
    )(place, observed, noise_var.reshape(1, sensors))
    data = [data[0]] + [swap(data[d], "sensor", d) for d in range(1, groups)]
    rows, diagonal = call(
        prior_kernel,
        [SMEM, VMEM, ANY],
        [shape((cells, width), bf16), shape((cells, cells), bf16)],
    )(place, prior_rows, data[1])
    came = [swap(diagonal if d % 2 else rows, "quad", d) for d in range(1, quads)]
    prior, noise, *streams = call(
        functools.partial(gather_kernel, groups, quads),
        [SMEM] + [VMEM] * (quads + groups),
        [shape((quads, cells, width), bf16), shape((groups, sensors, LANES), f32)]
        + [shape((groups, sensors, LANES), bf16)] * STREAMS,
        moved=8 * 2**20,
    )(place, prior_rows, *came, *data)

    def over_sides(partial):
        if sides == 2:
            return [partial, swap(partial, "side", 1)]
        return [lax.psum(partial, "side")]

    wide, narrow = shape((groups, sensors, LANES), f32), shape((groups, sensors, LANES), bf16)
    couple, full = shape((CORES, sensors, LANES), bf16), shape((sensors, 2 * LANES), bf16)

    near = call(bring_kernel, [ANY], [shape(held.shape, bf16)], [pltpu.SemaphoreType.DMA], moved=8 * 2**20)(held)[0]

    def step(stage, obs, preds):
        operands = [place, scale, near, prior, obs, noise] + preds
        return call(
            functools.partial(step_kernel, stage, len(preds)),
            [SMEM, SMEM] + [VMEM] * (len(operands) - 2),
            [wide] + [couple] * pairs if stage > 0 else [narrow],
            [pltpu.VMEM((groups, LANES, halves * sensors), bf16)],
            flops=2**31,
            moved=8 * 2**20,
        )(*operands)

    first = [over_sides(step(0, streams[s], [])[0]) for s in range(STREAMS)]
    multiplier, partials = [], []
    for s in range(STREAMS):
        out, *parts = step(1, streams[s], first[s])
        multiplier.append(out)
        partials.append(parts)
    keeps, gives, duals = [None] * pairs, [None] * pairs, {}
    for e in reversed(range(pairs)):
        preds = [over_sides(partials[s][e]) for s in range(STREAMS)]
        count = len(preds[0])
        keeps[e], gives[e] = call(
            functools.partial(last_kernel, e, count),
            [SMEM] + [VMEM] * (1 + STREAMS * (2 + count)),
            [full, full],
            moved=2 * 2**20,
        )(place, noise, *streams, *multiplier, *[p for pair in preds for p in pair])
        got = swap(gives[e], "sensor", 1)
        posts = []
        if e == 0:
            posts = call(
                functools.partial(post_kernel, pairs),
                [SMEM, SMEM] + [VMEM] * (2 + 2 * pairs) + [ANY],
                [shape((cells, 2 * LANES), bf16)] * quads,
                [pltpu.VMEM((groups, 2 * LANES, halves * sensors), bf16), pltpu.VMEM((quads, cells, 2 * LANES), bf16)],
                flops=2**31,
                moved=8 * 2**20,
            )(place, scale, near, prior, *keeps, *gives, duals[(pairs - 1) * quads])
        messages = call(
            send_kernel,
            [SMEM] + [VMEM] * (2 + len(posts)),
            [shape((CORES + (e == 0), sensors, 2 * LANES), bf16)] * (len(posts) or 1),
            moved=2**20,
        )(place, keeps[e], got, *posts)
        for d in reversed(range(quads)):
            message = messages[d] if e == 0 else messages[0]
            duals[e * quads + d] = swap(message, both, CORES * e * quads + d) if e + d else message
    dual = None
    for e in reversed(range(pairs)):
        operands = [place] + [duals[e * quads + d] for d in range(quads)] + ([] if dual is None else [dual])
        out = [shape((frequencies, halves, sensors, LANES), f32)]
        scratch = [
            pltpu.VMEM((quads, CORES, halves, sensors, LANES), f32),
            pltpu.SemaphoreType.DMA((quads, CORES + 1)),
        ]
        if e == 0:
            out.append(shape((quads, cells * 2, LANES), f32))
            scratch.append(pltpu.VMEM((quads, cells * 2, LANES), f32))
        dual, *posterior = call(
            functools.partial(end_kernel, e, quads, dual is not None),
            [SMEM] + [VMEM] * quads + [ANY] * (dual is not None),
            out,
            scratch,
            [ANY] * len(out),
            moved=4 * 2**20,
            aliases=None if dual is None else {quads + 1: 0},
        )(*operands)
    return dual, posterior[0].reshape(quads, cells, 2, LANES)


def solution(mesh):
    groups, space = mesh.devices.shape

    def run(forward_map, observed, noise_var, prior_rows, prior_scale):
        quads = forward_map.shape[0] // groups
        split = Mesh(mesh.devices.reshape(groups, space // quads, quads), ("sensor", "side", "quad"))
        return jax.shard_map(
            on_device,
            mesh=split,
            in_specs=(
                P(None, None, "sensor", ("side", "quad")),
                P(None, None, "sensor", None),
                P("sensor"),
                P(("side", "quad"), None),
                P(),
            ),
            out_specs=(P(None, None, "sensor", None), P("sensor", ("side", "quad"), None, None)),
            check_vma=False,
        )(forward_map, observed, noise_var, prior_rows, prior_scale)

    return run
```

```python
import functools

import jax
import jax.numpy as jnp
from jax import lax
from jax.experimental import pallas as pl
from jax.experimental.pallas import tpu as pltpu
from jax.sharding import Mesh, PartitionSpec as P

ITERS = 2
relax_step = 0.25
STREAMS = 2
CORES = 2
LANES = 128
HALF = LANES // 2
VMEM_LIMIT = 16 * 2**20
VMEM = pl.BlockSpec(memory_space=pltpu.VMEM)
SMEM = pl.BlockSpec(memory_space=pltpu.SMEM)
ANY = pl.BlockSpec(memory_space=pl.ANY)
bf16, f32 = jnp.bfloat16, jnp.float32


def shape(dims, dtype):
    return jax.ShapeDtypeStruct(dims, dtype)


def call(kernel, in_specs, out_shape, scratch=(), out_specs=None, flops=0, moved=0, aliases=None):
    return pl.pallas_call(
        kernel,
        input_output_aliases=aliases or {},
        in_specs=in_specs,
        out_specs=out_specs or [VMEM] * len(out_shape),
        out_shape=out_shape,
        scratch_shapes=list(scratch),
        cost_estimate=pl.CostEstimate(flops=flops, bytes_accessed=moved, transcendentals=0),
        compiler_params=pltpu.CompilerParams(vmem_limit_bytes=VMEM_LIMIT),
    )


def swap(x, axes, distance):
    count = lax.axis_size(axes)
    return lax.ppermute(x, axes, [(i, i ^ distance) for i in range(count)])


def dot(a, b):
    return jnp.dot(a, b, preferred_element_type=f32)


def dot_nt(a, b):
    return lax.dot_general(a, b, (((1,), (1,)), ((), ())), preferred_element_type=f32)


def data_kernel(groups, quads, place_ref, obs_ref, noise_ref, *refs):
    outs, (held, sems) = refs[:groups], refs[groups:]
    sensors = obs_ref.shape[2]
    copies = []
    for d in range(groups):
        freq = ((place_ref[0] * CORES + place_ref[2]) ^ d) * quads + place_ref[1]
        copies.append(pltpu.make_async_copy(obs_ref.at[freq], held.at[d], sems.at[d]))
        copies[-1].start()
    noise = noise_ref[...]
    high = noise.astype(bf16)
    low = (noise - high.astype(f32)).astype(bf16)
    tail = jnp.concatenate([jnp.broadcast_to(high, (8, sensors)), jnp.broadcast_to(low, (8, sensors))], 0)
    for d in range(groups):
        copies[d].wait()
        re, im = held[d, 0], held[d, 1]
        for s in range(STREAMS):
            part = slice(s * HALF, (s + 1) * HALF)
            outs[d][:sensors, s * LANES:(s + 1) * LANES] = jnp.concatenate([re[:, part], im[:, part]], 1).astype(bf16)
        outs[d][sensors:, :] = tail


def prior_kernel(place_ref, own_ref, after_ref, full_ref, diagonal_ref):
    cells = own_ref.shape[0]
    full_ref[...] = own_ref[...]
    diagonal_ref[...] = own_ref[:, pl.ds(pl.multiple_of((place_ref[1] & 1) * cells, cells), cells)]


def gather_kernel(groups, quads, place_ref, own_ref, *refs):
    came, data = refs[:quads - 1], refs[quads - 1:quads - 1 + groups]
    prior_ref, noise_ref, *streams = refs[quads - 1 + groups:]
    me, quad = place_ref[0] * CORES + place_ref[2], place_ref[1]
    sensors, cells = streams[0].shape[1], own_ref.shape[0]
    on, off = (pl.ds(pl.multiple_of(p * cells, cells), cells) for p in (quad & 1, 1 - (quad & 1)))
    for d in range(0, quads, 2):
        rows = own_ref if d == 0 else came[d - 1]
        prior_ref[quad ^ d] = rows[...]
        prior_ref[quad ^ d ^ 1, :, on] = rows[:, off].T
        prior_ref[quad ^ d ^ 1, :, off] = came[d][...]
    row = lax.broadcasted_iota(jnp.int32, (sensors, sensors), 0)
    col = lax.broadcasted_iota(jnp.int32, (sensors, sensors), 1)
    for d in range(groups):
        for s in range(STREAMS):
            streams[s][me ^ d] = data[d][:sensors, s * LANES:(s + 1) * LANES]
        both = data[d][sensors:, :].astype(f32)
        noise_row = both[0:1, :] + both[8:9, :]
        noise = jnp.sum(jnp.where(row == col, noise_row, 0.0), 1, keepdims=True)
        noise_ref[me ^ d] = jnp.broadcast_to(noise, (sensors, LANES))


def source(map_ref, sides_ref, prior_ref, scale):
    groups, quads, _, cells = map_ref.shape
    per_block = prior_ref.shape[2] // cells
    out = []
    for block in range(quads // per_block):
        members = range(block * per_block, (block + 1) * per_block)
        parts = []
        for q in members:
            u = jnp.zeros((sides_ref.shape[1], cells), f32)
            for g in range(groups):
                u += dot(sides_ref[g], map_ref[g, q])
            parts.append(u.astype(bf16))
        ub = jnp.concatenate(parts, 1)
        out += [(dot_nt(prior_ref[q], ub) * scale).astype(bf16) for q in members]
    return out


def sides(z):
    half = z.shape[1] // 2
    return jnp.concatenate([z, jnp.concatenate([z[:, half:], -z[:, :half]], 1)], 0).T


def bring_kernel(map_ref, out_ref, sem):
    copy = pltpu.make_async_copy(map_ref, out_ref, sem)
    copy.start()
    copy.wait()


def step_kernel(stage, n_pred, scale_ref, map_ref, prior_ref, obs_ref, noise_ref, *refs):
    groups, quads, double, _ = map_ref.shape
    sensors = double // 2
    preds, refs = refs[:n_pred], refs[n_pred:]
    if stage > 0:
        next_ref, refs = refs[0], refs[1:]
    out_ref, sides_ref = refs
    for g in range(groups):
        obs = obs_ref[g].astype(f32)
        now = relax_step * obs
        if stage > 0:
            predicted = sum(p[g].astype(f32) for p in preds)
            now = now + relax_step * (obs - predicted - noise_ref[g] * now)
            next_ref[g] = now
        sides_ref[g] = sides(now.astype(bf16))
    sources = source(map_ref, sides_ref, prior_ref, scale_ref[0])
    turned = [jnp.concatenate([-v[:, HALF:], v[:, :HALF]], 1) for v in sources]
    for g in range(groups):
        total = jnp.zeros((sensors, LANES), f32)
        for q in range(quads):
            total += dot(map_ref[g, q, :sensors, :], sources[q]) + dot(map_ref[g, q, sensors:, :], turned[q])
        out_ref[g] = total.astype(bf16)


def last_kernel(n_pred, noise_ref, obs_ref, held_ref, *refs):
    preds, (final_ref, out_ref) = refs[:n_pred], refs[n_pred:]
    for g in range(final_ref.shape[0]):
        now = held_ref[g]
        predicted = sum(p[g].astype(f32) for p in preds)
        now = now + relax_step * (obs_ref[g].astype(f32) - predicted - noise_ref[g] * now)
        now = now.astype(bf16)
        final_ref[g] = now
        for q in range(out_ref.shape[1]):
            out_ref[g, q] = now


def join(streams):
    return jnp.concatenate([x[:, :HALF] for x in streams] + [x[:, HALF:] for x in streams], 1)


def post_kernel(place_ref, scale_ref, map_ref, prior_ref, *refs):
    finals, refs = refs[:STREAMS], refs[STREAMS:]
    outs, (sides_ref, held_ref) = refs[:-2], refs[-2:]
    for g in range(map_ref.shape[0]):
        sides_ref[g] = sides(join([x[g] for x in finals]))
    for q, v in enumerate(source(map_ref, sides_ref, prior_ref, scale_ref[0])):
        held_ref[q] = v
    for d, out in enumerate(outs):
        out[...] = held_ref[place_ref[1] ^ d]


def end_kernel(quads, place_ref, *refs):
    came, posts, refs = refs[:STREAMS], refs[STREAMS:STREAMS + quads], refs[STREAMS + quads:]
    dual_out, post_out, dual_ref, post_ref, sems = refs
    quad = place_ref[1]
    cells = post_ref.shape[1] // 2
    sends = []
    for d in range(quads):
        post_ref[d, pl.ds(0, cells, stride=2), :] = posts[d][:, :LANES].astype(f32)
        post_ref[d, pl.ds(1, cells, stride=2), :] = posts[d][:, LANES:].astype(f32)
        sends.append(pltpu.make_async_copy(post_ref.at[d], post_out.at[quad ^ d], sems.at[d]))
        sends[-1].start()
    for freq in range(dual_ref.shape[0]):
        both = join([x[freq].astype(f32) for x in came])
        dual_ref[freq, 0] = both[:, :LANES]
        dual_ref[freq, 1] = both[:, LANES:]
        sends.append(pltpu.make_async_copy(dual_ref.at[freq], dual_out.at[freq], sems.at[quads + freq]))
        sends[-1].start()
    for copy in sends:
        copy.wait()


def on_device(forward_map, observed, noise_var, prior_rows, prior_scale):
    frequencies, halves, sensors, cells = forward_map.shape
    groups, quads, sides = (lax.axis_size(a) for a in ("sensor", "quad", "side"))
    width = prior_rows.shape[1]
    me, quad = lax.axis_index("sensor"), lax.axis_index("quad")
    place = jnp.stack([me // CORES, quad, me % CORES]).astype(jnp.int32)
    scale = lax.dynamic_slice_in_dim(prior_scale, me * quads + quad, 1, 0)
    both = ("sensor", "quad")

    held = lax.all_to_all(
        forward_map.reshape(frequencies, halves * sensors, cells), both, split_axis=0, concat_axis=0, tiled=True
    ).reshape(groups, quads, halves * sensors, cells)

    data = call(
        functools.partial(data_kernel, groups, quads),
        [SMEM, ANY, VMEM],
        [shape((sensors + 16, STREAMS * LANES), bf16)] * groups,
        [pltpu.VMEM((groups, halves, sensors, LANES), f32), pltpu.SemaphoreType.DMA((groups,))],
        moved=groups * sensors * LANES * 12,
    )(place, observed, noise_var.reshape(1, sensors))
    data = [data[0]] + [swap(data[d], "sensor", d) for d in range(1, groups)]
    rows, diagonal = call(
        prior_kernel,
        [SMEM, VMEM, ANY],
        [shape((cells, width), bf16), shape((cells, cells), bf16)],
    )(place, prior_rows, data[1])
    came = [swap(diagonal if d % 2 else rows, "quad", d) for d in range(1, quads)]
    prior, noise, *streams = call(
        functools.partial(gather_kernel, groups, quads),
        [SMEM] + [VMEM] * (quads + groups),
        [shape((quads, cells, width), bf16), shape((groups, sensors, LANES), f32)]
        + [shape((groups, sensors, LANES), bf16)] * STREAMS,
        moved=8 * 2**20,
    )(place, prior_rows, *came, *data)

    def over_sides(partial):
        if sides == 2:
            return [partial, swap(partial, "side", 1)]
        return [lax.psum(partial, "side")]

    wide, narrow = shape((groups, sensors, LANES), f32), shape((groups, sensors, LANES), bf16)

    near = call(bring_kernel, [ANY], [shape(held.shape, bf16)], [pltpu.SemaphoreType.DMA], moved=8 * 2**20)(held)[0]

    def step(stage, obs, preds):
        operands = [scale, near, prior, obs, noise] + preds
        return call(
            functools.partial(step_kernel, stage, len(preds)),
            [SMEM] + [VMEM] * (len(operands) - 1),
            [wide, narrow] if stage > 0 else [narrow],
            [pltpu.VMEM((groups, LANES, halves * sensors), bf16)],
            flops=2**31,
            moved=8 * 2**20,
        )(*operands)

    first = [over_sides(step(0, streams[s], [])[0]) for s in range(STREAMS)]
    finals, duals = [], []
    for s in range(STREAMS):
        held_s, partial = step(1, streams[s], first[s])
        preds = over_sides(partial)
        final, out = call(
            functools.partial(last_kernel, len(preds)),
            [VMEM] * (3 + len(preds)),
            [narrow, shape((groups, quads, sensors, LANES), bf16)],
            moved=2 * 2**20,
        )(noise, streams[s], held_s, *preds)
        finals.append(final)
        out = out.reshape(frequencies, sensors, LANES)
        duals.append(lax.all_to_all(out, both, split_axis=0, concat_axis=0, tiled=True))
    posts = call(
        post_kernel,
        [SMEM, SMEM] + [VMEM] * (2 + STREAMS),
        [shape((cells, 2 * LANES), bf16)] * quads,
        [pltpu.VMEM((groups, 2 * LANES, halves * sensors), bf16), pltpu.VMEM((quads, cells, 2 * LANES), bf16)],
        flops=2**31,
        moved=8 * 2**20,
    )(place, scale, near, prior, *finals)
    posts = [posts[0]] + [swap(posts[d], "quad", d) for d in range(1, quads)]
    dual, posterior = call(
        functools.partial(end_kernel, quads),
        [SMEM] + [VMEM] * (STREAMS + quads),
        [shape((frequencies, halves, sensors, LANES), f32), shape((quads, cells * 2, LANES), f32)],
        [
            pltpu.VMEM((frequencies, halves, sensors, LANES), f32),
            pltpu.VMEM((quads, cells * 2, LANES), f32),
            pltpu.SemaphoreType.DMA((quads + frequencies,)),
        ],
        [ANY, ANY],
        moved=8 * 2**20,
    )(place, *duals, *posts)
    return dual, posterior.reshape(quads, cells, 2, LANES)


def solution(mesh):
    groups, space = mesh.devices.shape

    def run(forward_map, observed, noise_var, prior_rows, prior_scale):
        quads = forward_map.shape[0] // groups
        split = Mesh(mesh.devices.reshape(groups, space // quads, quads), ("sensor", "side", "quad"))
        return jax.shard_map(
            on_device,
            mesh=split,
            in_specs=(
                P(None, None, "sensor", ("side", "quad")),
                P(None, None, "sensor", None),
                P("sensor"),
                P(("side", "quad"), None),
                P(),
            ),
            out_specs=(P(None, None, "sensor", None), P("sensor", ("side", "quad"), None, None)),
            check_vma=False,
        )(forward_map, observed, noise_var, prior_rows, prior_scale)

    return run
```

```python
import functools

import jax
import jax.numpy as jnp
from jax import lax
from jax.experimental import pallas as pl
from jax.experimental.pallas import tpu as pltpu
from jax.sharding import Mesh, PartitionSpec as P

ITERS = 2
relax_step = 0.25
CORES = 2
LANES = 128
HALF = LANES // 2
VMEM_LIMIT = 16 * 2**20
VMEM = pl.BlockSpec(memory_space=pltpu.VMEM)
SMEM = pl.BlockSpec(memory_space=pltpu.SMEM)
ANY = pl.BlockSpec(memory_space=pl.ANY)
bf16, f32 = jnp.bfloat16, jnp.float32


def shape(dims, dtype):
    return jax.ShapeDtypeStruct(dims, dtype)


def call(kernel, in_specs, out_shape, scratch=(), out_specs=None, flops=0, moved=0, aliases=None):
    return pl.pallas_call(
        kernel,
        input_output_aliases=aliases or {},
        in_specs=in_specs,
        out_specs=out_specs or [VMEM] * len(out_shape),
        out_shape=out_shape,
        scratch_shapes=list(scratch),
        cost_estimate=pl.CostEstimate(flops=flops, bytes_accessed=moved, transcendentals=0),
        compiler_params=pltpu.CompilerParams(vmem_limit_bytes=VMEM_LIMIT),
    )


def dot(a, b):
    return jnp.dot(a, b, preferred_element_type=f32)


def dot_nt(a, b):
    return lax.dot_general(a, b, (((1,), (1,)), ((), ())), preferred_element_type=f32)


def data_kernel(groups, quads, place_ref, obs_ref, noise_ref, *refs):
    outs, (held, sems) = refs[:groups], refs[groups:]
    sensors = obs_ref.shape[2]
    loads = []
    for e in range(groups // CORES):
        for j in range(CORES):
            freq = (CORES * (place_ref[0] ^ e) + j) * quads + place_ref[1]
            loads.append(pltpu.make_async_copy(obs_ref.at[freq], held.at[e, j], sems.at[e, j]))
            loads[-1].start()
    noise = noise_ref[...]
    high = noise.astype(bf16)
    low = (noise - high.astype(f32)).astype(bf16)
    tail = jnp.concatenate([jnp.broadcast_to(high, (8, sensors)), jnp.broadcast_to(low, (8, sensors))], 0)
    for load in loads:
        load.wait()
    for d in range(groups):
        e, s = divmod(d, CORES)
        second = (place_ref[2] ^ s) == 1
        for j in range(CORES):
            re, im = held[e, j, 0], held[e, j, 1]
            low_half = jnp.concatenate([re[:, :HALF], im[:, :HALF]], 1)
            high_half = jnp.concatenate([re[:, HALF:], im[:, HALF:]], 1)
            outs[d][:sensors, j * LANES:(j + 1) * LANES] = jnp.where(second, high_half, low_half).astype(bf16)
        outs[d][sensors:, :] = tail


def cut_kernel(place_ref, map_ref, after_ref, out_ref):
    out_ref[...] = map_ref[...]


def prior_kernel(place_ref, own_ref, after_ref, full_ref, diagonal_ref):
    cells = own_ref.shape[0]
    full_ref[...] = own_ref[...]
    diagonal_ref[...] = own_ref[:, pl.ds(pl.multiple_of((place_ref[1] & 1) * cells, cells), cells)]


def gather_kernel(groups, quads, place_ref, own_ref, *refs):
    came, data = refs[:quads - 1], refs[quads - 1:quads - 1 + groups]
    prior_ref, noise_ref, *streams = refs[quads - 1 + groups:]
    quad = place_ref[1]
    sensors, cells = streams[0].shape[1], own_ref.shape[0]
    on, off = (pl.ds(pl.multiple_of(p * cells, cells), cells) for p in (quad & 1, 1 - (quad & 1)))
    for d in range(0, quads, 2):
        rows = own_ref if d == 0 else came[d - 1]
        prior_ref[quad ^ d] = rows[...]
        prior_ref[quad ^ d ^ 1, :, on] = rows[:, off].T
        prior_ref[quad ^ d ^ 1, :, off] = came[d][...]
    row = lax.broadcasted_iota(jnp.int32, (sensors, sensors), 0)
    col = lax.broadcasted_iota(jnp.int32, (sensors, sensors), 1)
    for d in range(groups):
        at = CORES * (place_ref[0] ^ (d // CORES)) + d % CORES
        for s in range(CORES):
            streams[s][at] = data[d][:sensors, s * LANES:(s + 1) * LANES]
        both = data[d][sensors:, :].astype(f32)
        noise_row = both[0:1, :] + both[8:9, :]
        noise = jnp.sum(jnp.where(row == col, noise_row, 0.0), 1, keepdims=True)
        noise_ref[at] = jnp.broadcast_to(noise, (sensors, LANES))


def chunk(maps, r, q):
    return maps[r % CORES][r // CORES, q]


def source(maps, sides_ref, prior_ref, scale):
    pairs, quads, _, cells = maps[0].shape
    per_block = prior_ref.shape[2] // cells
    out = []
    for block in range(quads // per_block):
        members = range(block * per_block, (block + 1) * per_block)
        parts = []
        for q in members:
            u = jnp.zeros((LANES, cells), f32)
            for r in range(pairs * CORES):
                u += dot(sides_ref[r], chunk(maps, r, q))
            parts.append(u.astype(bf16))
        ub = jnp.concatenate(parts, 1)
        out += [(dot_nt(prior_ref[q], ub) * scale).astype(bf16) for q in members]
    return out


def sides(z):
    half = z.shape[1] // 2
    return jnp.concatenate([z, jnp.concatenate([z[:, half:], -z[:, :half]], 1)], 0).T


def bring_kernel(map_ref, out_ref, sem):
    copy = pltpu.make_async_copy(map_ref, out_ref, sem)
    copy.start()
    copy.wait()


def step_kernel(stage, n_pred, scale_ref, mine_ref, theirs_ref, prior_ref, obs_ref, noise_ref, *refs):
    maps = (mine_ref, theirs_ref)
    pairs, quads, double, _ = mine_ref.shape
    sensors = double // 2
    preds, refs = refs[:n_pred], refs[n_pred:]
    if stage > 0:
        next_ref, refs = refs[0], refs[1:]
    out_ref, sides_ref = refs
    for r in range(pairs * CORES):
        obs = obs_ref[r].astype(f32)
        now = relax_step * obs
        if stage > 0:
            predicted = sum(p[r].astype(f32) for p in preds)
            now = now + relax_step * (obs - predicted - noise_ref[r] * now)
            next_ref[r] = now
        sides_ref[r] = sides(now.astype(bf16))
    sources = source(maps, sides_ref, prior_ref, scale_ref[0])
    turned = [jnp.concatenate([-v[:, HALF:], v[:, :HALF]], 1) for v in sources]
    for r in range(pairs * CORES):
        total = jnp.zeros((sensors, LANES), f32)
        for q in range(quads):
            rows = chunk(maps, r, q)
            total += dot(rows[:sensors], sources[q]) + dot(rows[sensors:], turned[q])
        out_ref[r] = total.astype(bf16)


def last_kernel(n_pred, place_ref, noise_ref, obs_ref, held_ref, *refs):
    preds, (final_ref, out_ref) = refs[:n_pred], refs[n_pred:]
    for r in range(final_ref.shape[0]):
        now = held_ref[r]
        predicted = sum(p[r].astype(f32) for p in preds)
        now = now + relax_step * (obs_ref[r].astype(f32) - predicted - noise_ref[r] * now)
        now = now.astype(bf16)
        final_ref[r] = now
        for q in range(out_ref.shape[1]):
            out_ref[r // CORES * CORES + (place_ref[2] ^ (r % CORES)), q] = now


def join(streams):
    return jnp.concatenate([x[:, :HALF] for x in streams] + [x[:, HALF:] for x in streams], 1)


def post_kernel(scale_ref, mine_ref, theirs_ref, prior_ref, final_ref, out_ref, sides_ref):
    for r in range(final_ref.shape[0]):
        sides_ref[r] = sides(final_ref[r])
    for q, v in enumerate(source((mine_ref, theirs_ref), sides_ref, prior_ref, scale_ref[0])):
        out_ref[q] = v


def part_kernel(place_ref, first_ref, second_ref, mine_ref, give_ref):
    flag = place_ref[2] == 1
    first, second = first_ref[...].astype(f32), second_ref[...].astype(f32)
    mine_ref[...] = jnp.where(flag, second, first).astype(bf16)
    give_ref[...] = jnp.where(flag, first, second).astype(bf16)


def merge_kernel(place_ref, mine_ref, got_ref, *outs):
    flag = place_ref[2] == 1
    for d, out in enumerate(outs):
        mine, got = mine_ref[place_ref[1] ^ d].astype(f32), got_ref[place_ref[1] ^ d].astype(f32)
        out[...] = join([jnp.where(flag, got, mine), jnp.where(flag, mine, got)]).astype(bf16)


def end_kernel(pairs, quads, place_ref, *refs):
    came, posts, refs = refs[:CORES], refs[CORES:CORES + quads], refs[CORES + quads:]
    dual_out, post_out, dual_ref, post_ref, sems = refs
    quad = place_ref[1]
    cells = post_ref.shape[1] // 2
    sends = []
    for d in range(quads):
        post_ref[d, pl.ds(0, cells, stride=2), :] = posts[d][:, :LANES].astype(f32)
        post_ref[d, pl.ds(1, cells, stride=2), :] = posts[d][:, LANES:].astype(f32)
        sends.append(pltpu.make_async_copy(post_ref.at[d], post_out.at[quad ^ d], sems.at[d]))
        sends[-1].start()
    for j in range(CORES):
        for pair in range(pairs):
            for q in range(quads):
                freq = (CORES * pair + j) * quads + q
                both = join([came[j][pair, core, q].astype(f32) for core in range(CORES)])
                dual_ref[freq, 0] = both[:, :LANES]
                dual_ref[freq, 1] = both[:, LANES:]
                sends.append(pltpu.make_async_copy(dual_ref.at[freq], dual_out.at[freq], sems.at[quads + freq]))
                sends[-1].start()
    for copy in sends:
        copy.wait()


def on_device(forward_map, observed, noise_var, prior_rows, prior_scale):
    frequencies, halves, sensors, cells = forward_map.shape
    pairs, quads, count = (lax.axis_size(a) for a in ("pair", "quad", "side"))
    groups, width = pairs * CORES, prior_rows.shape[1]
    pair, core, quad = (lax.axis_index(a) for a in ("pair", "core", "quad"))
    place = jnp.stack([pair, quad, core]).astype(jnp.int32)

    def swap(x, axes, distance):
        return lax.ppermute(x, axes, [(i, i ^ distance) for i in range(lax.axis_size(axes))])

    def to_chips(x):
        return lax.all_to_all(x, ("pair", "quad"), split_axis=0, concat_axis=0, tiled=True)

    whole = forward_map.reshape(pairs, CORES, quads, halves * sensors, cells)
    arrived = [to_chips(whole[:, 0].reshape(pairs * quads, halves * sensors, cells))]

    data = call(
        functools.partial(data_kernel, groups, quads),
        [SMEM, ANY, VMEM],
        [shape((sensors + 16, CORES * LANES), bf16)] * groups,
        [pltpu.VMEM((pairs, CORES, halves, sensors, LANES), f32), pltpu.SemaphoreType.DMA((pairs, CORES))],
        moved=groups * sensors * LANES * 12,
    )(place, observed, noise_var.reshape(1, sensors))
    data = [data[0]] + [swap(data[d], ("pair", "core"), d) for d in range(1, groups)]
    rows, diagonal = call(
        prior_kernel,
        [SMEM, VMEM, ANY],
        [shape((cells, width), bf16), shape((cells, cells), bf16)],
    )(place, prior_rows, data[1])
    came = [swap(diagonal if d % 2 else rows, "quad", d) for d in range(1, quads)]
    prior, noise, *streams = call(
        functools.partial(gather_kernel, groups, quads),
        [SMEM] + [VMEM] * (quads + groups),
        [shape((quads, cells, width), bf16), shape((groups, sensors, LANES), f32)]
        + [shape((groups, sensors, LANES), bf16)] * CORES,
        moved=8 * 2**20,
    )(place, prior_rows, *came, *data)

    for j in range(1, CORES):
        cut = pl.pallas_call(
            cut_kernel,
            grid_spec=pltpu.PrefetchScalarGridSpec(
                num_scalar_prefetch=1,
                grid=(pairs, quads),
                in_specs=[
                    pl.BlockSpec((1, 1, 1, halves * sensors, cells), lambda p, q, place: (p, j, q, 0, 0)),
                    ANY,
                ],
                out_specs=pl.BlockSpec((1, 1, 1, halves * sensors, cells), lambda p, q, place: (p, 0, q, 0, 0)),
            ),
            out_shape=shape((pairs, 1, quads, halves * sensors, cells), bf16),
        )(place, whole, data[1])
        arrived.append(to_chips(cut.reshape(pairs * quads, halves * sensors, cells)))

    def over_sides(partial):
        if count == 2:
            return [partial, swap(partial, "side", 1)]
        return [lax.psum(partial, "side")]

    wide, narrow = shape((groups, sensors, LANES), f32), shape((groups, sensors, LANES), bf16)
    sides_scratch = pltpu.VMEM((groups, LANES, halves * sensors), bf16)
    duals, posts = [], []
    for j in range(CORES):
        scale = prior_scale[(CORES * pair + j) * quads + quad].reshape(1)
        mine = arrived[j].reshape(pairs, quads, halves * sensors, cells)
        mine = call(bring_kernel, [ANY], [shape(mine.shape, bf16)], [pltpu.SemaphoreType.DMA], moved=4 * 2**20)(mine)[0]
        maps = [mine, swap(mine, "core", 1)]

        def step(stage, preds):
            operands = [scale, *maps, prior, streams[j], noise] + preds
            return call(
                functools.partial(step_kernel, stage, len(preds)),
                [SMEM] + [VMEM] * (len(operands) - 1),
                [wide, narrow] if stage > 0 else [narrow],
                [sides_scratch],
                flops=2**31,
                moved=8 * 2**20,
            )(*operands)

        preds = over_sides(step(0, [])[0])
        held, partial = step(1, preds)
        preds = over_sides(partial)
        final, out = call(
            functools.partial(last_kernel, len(preds)),
            [SMEM] + [VMEM] * (3 + len(preds)),
            [narrow, shape((groups, quads, sensors, LANES), bf16)],
            moved=2 * 2**20,
        )(place, noise, streams[j], held, *preds)
        out = out.reshape(frequencies, sensors, LANES)
        out = lax.all_to_all(out, ("pair", "core", "quad"), split_axis=0, concat_axis=0, tiled=True)
        duals.append(out.reshape(pairs, CORES, quads, sensors, LANES))
        posts.append(
            call(
                post_kernel,
                [SMEM] + [VMEM] * 4,
                [shape((quads, cells, LANES), bf16)],
                [sides_scratch],
                flops=2**30,
                moved=8 * 2**20,
            )(scale, *maps, prior, final)[0]
        )
    piece = shape((quads, cells, LANES), bf16)
    mine, give = call(part_kernel, [SMEM, VMEM, VMEM], [piece, piece], moved=2**20)(place, *posts)
    posts = call(
        merge_kernel,
        [SMEM, VMEM, VMEM],
        [shape((cells, 2 * LANES), bf16)] * quads,
        moved=2**20,
    )(place, mine, swap(give, "core", 1))
    posts = [posts[0]] + [swap(posts[d], "quad", d) for d in range(1, quads)]
    dual, posterior = call(
        functools.partial(end_kernel, pairs, quads),
        [SMEM] + [VMEM] * (CORES + quads),
        [shape((frequencies, halves, sensors, LANES), f32), shape((quads, cells * 2, LANES), f32)],
        [
            pltpu.VMEM((frequencies, halves, sensors, LANES), f32),
            pltpu.VMEM((quads, cells * 2, LANES), f32),
            pltpu.SemaphoreType.DMA((quads + frequencies,)),
        ],
        [ANY, ANY],
        moved=8 * 2**20,
    )(place, *duals, *posts)
    return dual, posterior.reshape(quads, cells, 2, LANES)


def solution(mesh):
    groups, space = mesh.devices.shape

    def run(forward_map, observed, noise_var, prior_rows, prior_scale):
        quads = forward_map.shape[0] // groups
        split = Mesh(
            mesh.devices.reshape(groups // CORES, CORES, space // quads, quads), ("pair", "core", "side", "quad")
        )
        return jax.shard_map(
            on_device,
            mesh=split,
            in_specs=(
                P(None, None, ("pair", "core"), ("side", "quad")),
                P(None, None, ("pair", "core"), None),
                P(("pair", "core")),
                P(("side", "quad"), None),
                P(),
            ),
            out_specs=(P(None, None, ("pair", "core"), None), P(("pair", "core"), ("side", "quad"), None, None)),
            check_vma=False,
        )(forward_map, observed, noise_var, prior_rows, prior_scale)

    return run
```

```python
import functools

import jax
import jax.numpy as jnp
from jax import lax
from jax.experimental import pallas as pl
from jax.experimental.pallas import tpu as pltpu
from jax.sharding import Mesh, PartitionSpec as P

ITERS = 2
relax_step = 0.25
STREAMS = 2
CORES = 2
LANES = 128
HALF = LANES // 2
VMEM_LIMIT = 16 * 2**20
VMEM = pl.BlockSpec(memory_space=pltpu.VMEM)
SMEM = pl.BlockSpec(memory_space=pltpu.SMEM)
ANY = pl.BlockSpec(memory_space=pl.ANY)
bf16, f32 = jnp.bfloat16, jnp.float32


def shape(dims, dtype):
    return jax.ShapeDtypeStruct(dims, dtype)


def call(kernel, in_specs, out_shape, scratch=(), out_specs=None, flops=0, moved=0, aliases=None):
    return pl.pallas_call(
        kernel,
        input_output_aliases=aliases or {},
        in_specs=in_specs,
        out_specs=out_specs or [VMEM] * len(out_shape),
        out_shape=out_shape,
        scratch_shapes=list(scratch),
        cost_estimate=pl.CostEstimate(flops=flops, bytes_accessed=moved, transcendentals=0),
        compiler_params=pltpu.CompilerParams(vmem_limit_bytes=VMEM_LIMIT),
    )


def swap(x, axes, distance):
    count = lax.axis_size(axes)
    return lax.ppermute(x, axes, [(i, i ^ distance) for i in range(count)])


def dot(a, b):
    return jnp.dot(a, b, preferred_element_type=f32)


def dot_nt(a, b):
    return lax.dot_general(a, b, (((1,), (1,)), ((), ())), preferred_element_type=f32)


def data_kernel(groups, quads, place_ref, obs_ref, noise_ref, *refs):
    outs, (held, sems) = refs[:groups], refs[groups:]
    sensors = obs_ref.shape[2]
    copies = []
    for d in range(groups):
        freq = ((place_ref[0] * CORES + place_ref[2]) ^ d) * quads + place_ref[1]
        copies.append(pltpu.make_async_copy(obs_ref.at[freq], held.at[d], sems.at[d]))
        copies[-1].start()
    noise = noise_ref[...]
    high = noise.astype(bf16)
    low = (noise - high.astype(f32)).astype(bf16)
    tail = jnp.concatenate([jnp.broadcast_to(high, (8, sensors)), jnp.broadcast_to(low, (8, sensors))], 0)
    for d in range(groups):
        copies[d].wait()
        re, im = held[d, 0], held[d, 1]
        for s in range(STREAMS):
            part = slice(s * HALF, (s + 1) * HALF)
            outs[d][:sensors, s * LANES:(s + 1) * LANES] = jnp.concatenate([re[:, part], im[:, part]], 1).astype(bf16)
        outs[d][sensors:, :] = tail


def prior_kernel(place_ref, own_ref, after_ref, full_ref, diagonal_ref):
    cells = own_ref.shape[0]
    full_ref[...] = own_ref[...]
    diagonal_ref[...] = own_ref[:, pl.ds(pl.multiple_of((place_ref[1] & 1) * cells, cells), cells)]


def gather_kernel(groups, quads, place_ref, own_ref, *refs):
    came, data = refs[:quads - 1], refs[quads - 1:quads - 1 + groups]
    prior_ref, noise_ref, *streams = refs[quads + groups:]
    me, quad = place_ref[0] * CORES + place_ref[2], place_ref[1]
    sensors, cells = streams[0].shape[1], own_ref.shape[0]
    on, off = (pl.ds(pl.multiple_of(p * cells, cells), cells) for p in (quad & 1, 1 - (quad & 1)))
    for d in range(0, quads, 2):
        rows = own_ref if d == 0 else came[d - 1]
        prior_ref[quad ^ d] = rows[...]
        prior_ref[quad ^ d ^ 1, :, on] = rows[:, off].T
        prior_ref[quad ^ d ^ 1, :, off] = came[d][...]
    row = lax.broadcasted_iota(jnp.int32, (sensors, sensors), 0)
    col = lax.broadcasted_iota(jnp.int32, (sensors, sensors), 1)
    for d in range(groups):
        for s in range(STREAMS):
            streams[s][me ^ d] = data[d][:sensors, s * LANES:(s + 1) * LANES]
        both = data[d][sensors:, :].astype(f32)
        noise_row = both[0:1, :] + both[8:9, :]
        noise = jnp.sum(jnp.where(row == col, noise_row, 0.0), 1, keepdims=True)
        noise_ref[me ^ d] = jnp.broadcast_to(noise, (sensors, LANES))


def source(map_ref, sides_ref, prior_ref, scale):
    groups, quads, _, cells = map_ref.shape
    per_block = prior_ref.shape[2] // cells
    out = []
    for block in range(quads // per_block):
        members = range(block * per_block, (block + 1) * per_block)
        parts = []
        for q in members:
            u = jnp.zeros((sides_ref.shape[1], cells), f32)
            for g in range(groups):
                u += dot(sides_ref[g], map_ref[g, q])
            parts.append(u.astype(bf16))
        ub = jnp.concatenate(parts, 1)
        out += [(dot_nt(prior_ref[q], ub) * scale).astype(bf16) for q in members]
    return out


def sides(z):
    half = z.shape[1] // 2
    return jnp.concatenate([z, jnp.concatenate([z[:, half:], -z[:, :half]], 1)], 0).T


def bring_kernel(map_ref, out_ref, sem):
    copy = pltpu.make_async_copy(map_ref, out_ref, sem)
    copy.start()
    copy.wait()


def step_kernel(stage, n_pred, n_after, scale_ref, map_ref, prior_ref, obs_ref, noise_ref, *refs):
    groups, quads, double, _ = map_ref.shape
    sensors = double // 2
    preds, refs = refs[:n_pred], refs[n_pred + n_after:]
    if stage > 0:
        next_ref, refs = refs[0], refs[1:]
    out_ref, sides_ref = refs
    for g in range(groups):
        obs = obs_ref[g].astype(f32)
        now = relax_step * obs
        if stage > 0:
            predicted = sum(p[g].astype(f32) for p in preds)
            now = now + relax_step * (obs - predicted - noise_ref[g] * now)
            next_ref[g] = now
        sides_ref[g] = sides(now.astype(bf16))
    sources = source(map_ref, sides_ref, prior_ref, scale_ref[0])
    turned = [jnp.concatenate([-v[:, HALF:], v[:, :HALF]], 1) for v in sources]
    for g in range(groups):
        total = jnp.zeros((sensors, LANES), f32)
        for q in range(quads):
            total += dot(map_ref[g, q, :sensors, :], sources[q]) + dot(map_ref[g, q, sensors:, :], turned[q])
        out_ref[g] = total.astype(bf16)


def last_kernel(n_pred, place_ref, noise_ref, *refs):
    obs, held, refs = refs[:STREAMS], refs[STREAMS:2 * STREAMS], refs[2 * STREAMS:]
    preds, (keep_ref, give_ref) = refs[:STREAMS * n_pred], refs[STREAMS * n_pred:]
    for e in range(keep_ref.shape[0]):
        for out, core in ((give_ref, 1 - place_ref[2]), (keep_ref, place_ref[2])):
            g = CORES * (place_ref[0] ^ e) + core
            parts = []
            for s in range(STREAMS):
                now = held[s][g]
                predicted = sum(p[g].astype(f32) for p in preds[s * n_pred:(s + 1) * n_pred])
                parts.append(now + relax_step * (obs[s][g].astype(f32) - predicted - noise_ref[g] * now))
            out[e] = join(parts).astype(bf16)


def join(streams):
    return jnp.concatenate([x[:, :HALF] for x in streams] + [x[:, HALF:] for x in streams], 1)


def send_kernel(e, place_ref, keep_ref, got_ref, *refs):
    posts, outs = refs[:len(refs) // 2], refs[len(refs) // 2:]
    for i, out in enumerate(outs):
        out[place_ref[2]] = keep_ref[e]
        out[1 - place_ref[2]] = got_ref[e]
        if posts:
            out[CORES] = posts[i][...]


def post_kernel(place_ref, scale_ref, map_ref, prior_ref, keep_ref, give_ref, *refs):
    outs, (sides_ref, held_ref) = refs[:-2], refs[-2:]
    for e in range(keep_ref.shape[0]):
        first = CORES * (place_ref[0] ^ e)
        sides_ref[first + place_ref[2]] = sides(keep_ref[e])
        sides_ref[first + 1 - place_ref[2]] = sides(give_ref[e])
    for q, v in enumerate(source(map_ref, sides_ref, prior_ref, scale_ref[0])):
        held_ref[q] = v
    for d, out in enumerate(outs):
        out[...] = held_ref[place_ref[1] ^ d]


def end_kernel(chips, quads, place_ref, *refs):
    came, (dual_out, post_out, dual_ref, post_ref, sems) = refs[:chips], refs[chips:]
    pair, quad = place_ref[0], place_ref[1]
    cells = post_ref.shape[1] // 2
    sends = []
    for chip in reversed(range(chips)):
        e, d = divmod(chip, quads)
        for core in range(CORES):
            freq = (CORES * (pair ^ e) + core) * quads + (quad ^ d)
            for part in range(2):
                dual_ref[chip, core, part] = came[chip][core, :, part * LANES:(part + 1) * LANES].astype(f32)
            sends.append(pltpu.make_async_copy(dual_ref.at[chip, core], dual_out.at[freq], sems.at[chip, core]))
            sends[-1].start()
        if e == 0:
            post_ref[d, pl.ds(0, cells, stride=2), :] = came[chip][CORES, :, :LANES].astype(f32)
            post_ref[d, pl.ds(1, cells, stride=2), :] = came[chip][CORES, :, LANES:].astype(f32)
            sends.append(pltpu.make_async_copy(post_ref.at[d], post_out.at[quad ^ d], sems.at[chip, CORES]))
            sends[-1].start()
    for copy in sends:
        copy.wait()


def on_device(forward_map, observed, noise_var, prior_rows, prior_scale):
    frequencies, halves, sensors, cells = forward_map.shape
    groups, quads, sides = (lax.axis_size(a) for a in ("sensor", "quad", "side"))
    width = prior_rows.shape[1]
    me, quad = lax.axis_index("sensor"), lax.axis_index("quad")
    place = jnp.stack([me // CORES, quad, me % CORES]).astype(jnp.int32)
    scale = lax.dynamic_slice_in_dim(prior_scale, me * quads + quad, 1, 0)
    both = ("sensor", "quad")

    held = lax.all_to_all(
        forward_map.reshape(frequencies, halves * sensors, cells), both, split_axis=0, concat_axis=0, tiled=True
    ).reshape(groups, quads, halves * sensors, cells)

    data = call(
        functools.partial(data_kernel, groups, quads),
        [SMEM, ANY, VMEM],
        [shape((sensors + 16, STREAMS * LANES), bf16)] * groups,
        [pltpu.VMEM((groups, halves, sensors, LANES), f32), pltpu.SemaphoreType.DMA((groups,))],
        moved=groups * sensors * LANES * 12,
    )(place, observed, noise_var.reshape(1, sensors))
    data = [data[0]] + [swap(data[d], "sensor", d) for d in range(1, groups)]
    rows, diagonal = call(
        prior_kernel,
        [SMEM, VMEM, ANY],
        [shape((cells, width), bf16), shape((cells, cells), bf16)],
    )(place, prior_rows, data[1])
    came = [swap(diagonal if d % 2 else rows, "quad", d) for d in range(1, quads)]
    near = call(bring_kernel, [ANY], [shape(held.shape, bf16)], [pltpu.SemaphoreType.DMA], moved=8 * 2**20)(held)[0]

    prior, noise, *streams = call(
        functools.partial(gather_kernel, groups, quads),
        [SMEM] + [VMEM] * (quads + groups) + [ANY],
        [shape((quads, cells, width), bf16), shape((groups, sensors, LANES), f32)]
        + [shape((groups, sensors, LANES), bf16)] * STREAMS,
        moved=8 * 2**20,
    )(place, prior_rows, *came, *data, near)

    def over_sides(partial):
        if sides == 2:
            return [partial, swap(partial, "side", 1)]
        return [lax.psum(partial, "side")]

    wide, narrow = shape((groups, sensors, LANES), f32), shape((groups, sensors, LANES), bf16)

    def step(stage, obs, preds, after=()):
        operands = [scale, near, prior, obs, noise] + preds
        return call(
            functools.partial(step_kernel, stage, len(preds), len(after)),
            [SMEM] + [VMEM] * (len(operands) - 1) + [ANY] * len(after),
            [wide, narrow] if stage > 0 else [narrow],
            [pltpu.VMEM((groups, LANES, halves * sensors), bf16)],
            flops=2**31,
            moved=8 * 2**20,
        )(*operands, *after)

    partials = [step(0, streams[s], [])[0] for s in range(STREAMS)]
    preds = [over_sides(x) for x in partials]
    steps = [step(1, streams[s], preds[s], partials[s + 1:]) for s in range(STREAMS)]
    preds = [over_sides(x) for _, x in steps]
    pairs, count = groups // CORES, len(preds[0])
    part = shape((pairs, sensors, 2 * LANES), bf16)
    keep, give = call(
        functools.partial(last_kernel, count),
        [SMEM] + [VMEM] * (1 + STREAMS * (2 + count)),
        [part, part],
        moved=2 * 2**20,
    )(place, noise, *streams, *[held for held, _ in steps], *[p for both_sides in preds for p in both_sides])
    got = swap(give, "sensor", 1)
    posts = call(
        post_kernel,
        [SMEM, SMEM] + [VMEM] * 4,
        [shape((cells, 2 * LANES), bf16)] * quads,
        [pltpu.VMEM((groups, 2 * LANES, halves * sensors), bf16), pltpu.VMEM((quads, cells, 2 * LANES), bf16)],
        flops=2**31,
        moved=8 * 2**20,
    )(place, scale, near, prior, keep, give)
    duals = {}
    for e in reversed(range(pairs)):
        extra = list(posts) if e == 0 else []
        messages = call(
            functools.partial(send_kernel, e),
            [SMEM] + [VMEM] * (2 + len(extra)),
            [shape((CORES + (e == 0), sensors, 2 * LANES), bf16)] * (len(extra) or 1),
            moved=2**20,
        )(place, keep, got, *extra)
        for d in reversed(range(quads)):
            message = messages[d] if e == 0 else messages[0]
            duals[e * quads + d] = swap(message, both, CORES * e * quads + d) if e + d else message
    dual, posterior = call(
        functools.partial(end_kernel, pairs * quads, quads),
        [SMEM] + [VMEM] * (pairs * quads),
        [shape((frequencies, halves, sensors, LANES), f32), shape((quads, cells * 2, LANES), f32)],
        [
            pltpu.VMEM((pairs * quads, CORES, halves, sensors, LANES), f32),
            pltpu.VMEM((quads, cells * 2, LANES), f32),
            pltpu.SemaphoreType.DMA((pairs * quads, CORES + 1)),
        ],
        [ANY, ANY],
        moved=8 * 2**20,
    )(place, *[duals[i] for i in range(pairs * quads)])
    return dual, posterior.reshape(quads, cells, 2, LANES)


def solution(mesh):
    groups, space = mesh.devices.shape

    def run(forward_map, observed, noise_var, prior_rows, prior_scale):
        quads = forward_map.shape[0] // groups
        split = Mesh(mesh.devices.reshape(groups, space // quads, quads), ("sensor", "side", "quad"))
        return jax.shard_map(
            on_device,
            mesh=split,
            in_specs=(
                P(None, None, "sensor", ("side", "quad")),
                P(None, None, "sensor", None),
                P("sensor"),
                P(("side", "quad"), None),
                P(),
            ),
            out_specs=(P(None, None, "sensor", None), P("sensor", ("side", "quad"), None, None)),
            check_vma=False,
        )(forward_map, observed, noise_var, prior_rows, prior_scale)

    return run
```

```python
import functools

import jax
import jax.numpy as jnp
from jax import lax
from jax.experimental import pallas as pl
from jax.experimental.pallas import tpu as pltpu
from jax.sharding import Mesh, PartitionSpec as P

ITERS = 2
relax_step = 0.25
STREAMS = 2
CORES = 2
LANES = 128
HALF = LANES // 2
VMEM_LIMIT = 16 * 2**20
VMEM = pl.BlockSpec(memory_space=pltpu.VMEM)
SMEM = pl.BlockSpec(memory_space=pltpu.SMEM)
ANY = pl.BlockSpec(memory_space=pl.ANY)
bf16, f32 = jnp.bfloat16, jnp.float32


def shape(dims, dtype):
    return jax.ShapeDtypeStruct(dims, dtype)


def call(kernel, in_specs, out_shape, scratch=(), out_specs=None, flops=0, moved=0, aliases=None):
    return pl.pallas_call(
        kernel,
        input_output_aliases=aliases or {},
        in_specs=in_specs,
        out_specs=out_specs or [VMEM] * len(out_shape),
        out_shape=out_shape,
        scratch_shapes=list(scratch),
        cost_estimate=pl.CostEstimate(flops=flops, bytes_accessed=moved, transcendentals=0),
        compiler_params=pltpu.CompilerParams(vmem_limit_bytes=VMEM_LIMIT),
    )


def swap(x, axes, distance):
    count = lax.axis_size(axes)
    return lax.ppermute(x, axes, [(i, i ^ distance) for i in range(count)])


def dot(a, b):
    return jnp.dot(a, b, preferred_element_type=f32)


def dot_nt(a, b):
    return lax.dot_general(a, b, (((1,), (1,)), ((), ())), preferred_element_type=f32)


def my_place():
    me = lax.axis_index("sensor")
    return me // CORES, lax.axis_index("quad"), me % CORES


def data_kernel(groups, quads, obs_ref, noise_ref, *refs):
    outs, (held, sems) = refs[:groups], refs[groups:]
    sensors = obs_ref.shape[2]
    copies = []
    for d in range(groups):
        freq = ((my_place()[0] * CORES + my_place()[2]) ^ d) * quads + my_place()[1]
        copies.append(pltpu.make_async_copy(obs_ref.at[freq], held.at[d], sems.at[d]))
        copies[-1].start()
    noise = noise_ref[...]
    high = noise.astype(bf16)
    low = (noise - high.astype(f32)).astype(bf16)
    tail = jnp.concatenate([jnp.broadcast_to(high, (8, sensors)), jnp.broadcast_to(low, (8, sensors))], 0)
    for d in range(groups):
        copies[d].wait()
        re, im = held[d, 0], held[d, 1]
        for s in range(STREAMS):
            part = slice(s * HALF, (s + 1) * HALF)
            outs[d][:sensors, s * LANES:(s + 1) * LANES] = jnp.concatenate([re[:, part], im[:, part]], 1).astype(bf16)
        outs[d][sensors:, :] = tail


def prior_kernel(scale_ref, own_ref, after_ref, full_ref, diagonal_ref, wide_ref):
    cells = own_ref.shape[0]
    full_ref[...] = own_ref[...]
    wide_ref[...] = jnp.full(wide_ref.shape, scale_ref[0], f32)
    diagonal_ref[...] = own_ref[:, pl.ds(pl.multiple_of((my_place()[1] & 1) * cells, cells), cells)]


def gather_kernel(groups, quads, own_ref, *refs):
    came, data = refs[:quads - 1], refs[quads - 1:quads - 1 + groups]
    prior_ref, noise_ref, *streams = refs[quads + groups:]
    me, quad = my_place()[0] * CORES + my_place()[2], my_place()[1]
    sensors, cells = streams[0].shape[1], own_ref.shape[0]
    on, off = (pl.ds(pl.multiple_of(p * cells, cells), cells) for p in (quad & 1, 1 - (quad & 1)))
    for d in range(0, quads, 2):
        rows = own_ref if d == 0 else came[d - 1]
        prior_ref[quad ^ d] = rows[...]
        prior_ref[quad ^ d ^ 1, :, on] = rows[:, off].T
        prior_ref[quad ^ d ^ 1, :, off] = came[d][...]
    row = lax.broadcasted_iota(jnp.int32, (sensors, sensors), 0)
    col = lax.broadcasted_iota(jnp.int32, (sensors, sensors), 1)
    for d in range(groups):
        for s in range(STREAMS):
            streams[s][me ^ d] = data[d][:sensors, s * LANES:(s + 1) * LANES]
        both = data[d][sensors:, :].astype(f32)
        noise_row = both[0:1, :] + both[8:9, :]
        noise = jnp.sum(jnp.where(row == col, noise_row, 0.0), 1, keepdims=True)
        noise_ref[me ^ d] = jnp.broadcast_to(noise, (sensors, LANES))


def source(map_ref, sides_ref, prior_ref, scale):
    groups, quads, _, cells = map_ref.shape
    per_block = prior_ref.shape[2] // cells
    out = []
    for block in range(quads // per_block):
        members = range(block * per_block, (block + 1) * per_block)
        parts = []
        for q in members:
            u = jnp.zeros((sides_ref.shape[1], cells), f32)
            for g in range(groups):
                u += dot(sides_ref[g], map_ref[g, q])
            parts.append(u.astype(bf16))
        ub = jnp.concatenate(parts, 1)
        out += [(dot_nt(prior_ref[q], ub) * scale).astype(bf16) for q in members]
    return out


def sides(z):
    half = z.shape[1] // 2
    return jnp.concatenate([z, jnp.concatenate([z[:, half:], -z[:, :half]], 1)], 0).T


def bring_kernel(map_ref, out_ref, sem):
    copy = pltpu.make_async_copy(map_ref, out_ref, sem)
    copy.start()
    copy.wait()


def step_kernel(stage, n_pred, n_after, scale_ref, map_ref, prior_ref, obs_ref, noise_ref, *refs):
    groups, quads, double, _ = map_ref.shape
    sensors = double // 2
    preds, refs = refs[:n_pred], refs[n_pred + n_after:]
    if stage > 0:
        outs, (sides_ref, now_ref, partial_ref) = refs[:4], refs[4:]
    else:
        out_ref, sides_ref = refs
    for g in range(groups):
        obs = obs_ref[g].astype(f32)
        now = relax_step * obs
        if stage > 0:
            predicted = sum(p[g].astype(f32) for p in preds)
            now = now + relax_step * (obs - predicted - noise_ref[g] * now)
            now_ref[g] = now + relax_step * (obs - noise_ref[g] * now)
        sides_ref[g] = sides(now.astype(bf16))
    sources = source(map_ref, sides_ref, prior_ref, scale_ref[0:1, 0:1])
    turned = [jnp.concatenate([-v[:, HALF:], v[:, :HALF]], 1) for v in sources]
    for g in range(groups):
        total = jnp.zeros((sensors, LANES), f32)
        for q in range(quads):
            total += dot(map_ref[g, q, :sensors, :], sources[q]) + dot(map_ref[g, q, sensors:, :], turned[q])
        if stage == 0:
            out_ref[g] = total.astype(bf16)
        else:
            now_ref[g] -= relax_step * total
            partial_ref[g] = total.astype(bf16)
    if stage > 0:
        for e in range(groups // CORES):
            for parity, core in ((0, my_place()[2]), (1, 1 - my_place()[2])):
                g = CORES * (my_place()[0] ^ e) + core
                outs[parity][e] = partial_ref[g]
                outs[2 + parity][e] = now_ref[g].astype(outs[2 + parity].dtype)


def last_kernel(pairs, *refs):
    mine, theirs, keeps, gots = (refs[i * STREAMS:(i + 1) * STREAMS] for i in range(4))
    *outs, give_ref = refs[4 * STREAMS:]
    core = my_place()[2]
    for e in range(pairs):
        own = join([keeps[s][e] - relax_step * mine[s][e].astype(f32) for s in range(STREAMS)])
        other = join([gots[s][e].astype(f32) - relax_step * theirs[s][e].astype(f32) for s in range(STREAMS)])
        outs[e][core] = own.astype(bf16)
        outs[e][1 - core] = other.astype(bf16)
        give_ref[e] = other.astype(bf16)


def join(streams):
    return jnp.concatenate([x[:, :HALF] for x in streams] + [x[:, HALF:] for x in streams], 1)


def send_kernel(dual_ref, *refs):
    posts, outs = refs[:len(refs) // 2], refs[len(refs) // 2:]
    for post, out in zip(posts, outs):
        out[:CORES] = dual_ref[...]
        out[CORES] = post[...]


def post_kernel(pairs, scale_ref, map_ref, prior_ref, *refs):
    duals, got_ref, refs = refs[:pairs], refs[pairs], refs[pairs + 1:]
    outs, (sides_ref, held_ref) = refs[:-2], refs[-2:]
    core = my_place()[2]
    for e in range(pairs):
        first = CORES * (my_place()[0] ^ e)
        sides_ref[first + core] = sides(duals[e][core])
        sides_ref[first + 1 - core] = sides(got_ref[e])
    for q, v in enumerate(source(map_ref, sides_ref, prior_ref, scale_ref[0:1, 0:1])):
        held_ref[q] = v
    for d, out in enumerate(outs):
        out[...] = held_ref[my_place()[1] ^ d]


def end_kernel(chips, quads, *refs):
    came, (dual_out, post_out, dual_ref, post_ref, sems) = refs[:chips], refs[chips:]
    pair, quad = my_place()[0], my_place()[1]
    cells = post_ref.shape[1] // 2
    sends = []
    for chip in reversed(range(chips)):
        e, d = divmod(chip, quads)
        for core in range(CORES):
            freq = (CORES * (pair ^ e) + core) * quads + (quad ^ d)
            for part in range(2):
                dual_ref[chip, core, part] = came[chip][core, :, part * LANES:(part + 1) * LANES].astype(f32)
            sends.append(pltpu.make_async_copy(dual_ref.at[chip, core], dual_out.at[freq], sems.at[chip, core]))
            sends[-1].start()
        if e == 0:
            post_ref[d, pl.ds(0, cells, stride=2), :] = came[chip][CORES, :, :LANES].astype(f32)
            post_ref[d, pl.ds(1, cells, stride=2), :] = came[chip][CORES, :, LANES:].astype(f32)
            sends.append(pltpu.make_async_copy(post_ref.at[d], post_out.at[quad ^ d], sems.at[chip, CORES]))
            sends[-1].start()
    for copy in sends:
        copy.wait()


def on_device(forward_map, observed, noise_var, prior_rows, prior_scale):
    frequencies, halves, sensors, cells = forward_map.shape
    groups, quads, count = (lax.axis_size(a) for a in ("sensor", "quad", "side"))
    width = prior_rows.shape[1]
    me, quad = lax.axis_index("sensor"), lax.axis_index("quad")
    scale = lax.dynamic_slice_in_dim(prior_scale, me * quads + quad, 1, 0)
    both = ("sensor", "quad")

    held = lax.all_to_all(
        forward_map.reshape(frequencies, halves * sensors, cells), both, split_axis=0, concat_axis=0, tiled=True
    ).reshape(groups, quads, halves * sensors, cells)

    data = call(
        functools.partial(data_kernel, groups, quads),
        [ANY, VMEM],
        [shape((sensors + 16, STREAMS * LANES), bf16)] * groups,
        [pltpu.VMEM((groups, halves, sensors, LANES), f32), pltpu.SemaphoreType.DMA((groups,))],
        moved=groups * sensors * LANES * 12,
    )(observed, noise_var.reshape(1, sensors))
    data = [data[0]] + [swap(data[d], "sensor", d) for d in range(1, groups)]
    rows, diagonal, scale = call(
        prior_kernel,
        [SMEM, VMEM, ANY],
        [shape((cells, width), bf16), shape((cells, cells), bf16), shape((8, LANES), f32)],
    )(scale, prior_rows, data[1])
    came = [swap(diagonal if d % 2 else rows, "quad", d) for d in range(1, quads)]
    near = call(bring_kernel, [ANY], [shape(held.shape, bf16)], [pltpu.SemaphoreType.DMA], moved=8 * 2**20)(held)[0]

    prior, noise, *streams = call(
        functools.partial(gather_kernel, groups, quads),
        [VMEM] * (quads + groups) + [ANY],
        [shape((quads, cells, width), bf16), shape((groups, sensors, LANES), f32)]
        + [shape((groups, sensors, LANES), bf16)] * STREAMS,
        moved=8 * 2**20,
    )(prior_rows, *came, *data, near)

    def over_sides(partial):
        if count == 2:
            return [partial, swap(partial, "side", 1)]
        return [lax.psum(partial, "side")]

    wide, narrow = shape((groups, sensors, LANES), f32), shape((groups, sensors, LANES), bf16)

    def step(stage, obs, preds, after=()):
        operands = [scale, near, prior, obs, noise] + preds
        scratch = [pltpu.VMEM((groups, LANES, halves * sensors), bf16)]
        if stage > 0:
            scratch += [pltpu.VMEM((groups, sensors, LANES), f32), pltpu.VMEM((groups, sensors, LANES), bf16)]
        return call(
            functools.partial(step_kernel, stage, len(preds), len(after)),
            [VMEM] * len(operands) + [ANY] * len(after),
            [part, part, shape(part.shape, f32), part] if stage > 0 else [narrow],
            scratch,
            flops=2**31,
            moved=8 * 2**20,
        )(*operands, *after)

    pairs = groups // CORES
    part = shape((pairs, sensors, LANES), bf16)
    partials = [step(0, streams[s], [])[0] for s in range(STREAMS)]
    preds = [over_sides(x) for x in partials]
    steps = [step(1, streams[s], preds[s], partials[s + 1:]) for s in range(STREAMS)]

    def to_other_sides(x, cross):
        if count == 2:
            return lax.ppermute(
                x, ("sensor", "side"), [(i, i ^ (1 + CORES * cross)) for i in range(groups * count)]
            )
        rest = lax.psum(x.astype(f32), "side") - x.astype(f32)
        return (swap(rest, "sensor", 1) if cross else rest).astype(bf16)

    mine = [to_other_sides(x[0], 0) for x in steps]
    theirs = [to_other_sides(x[1], 1) for x in steps]
    keeps, gots = [x[2] for x in steps], [swap(x[3], "sensor", 1) for x in steps]
    message = shape((CORES, sensors, 2 * LANES), bf16)
    *finals, give = call(
        functools.partial(last_kernel, pairs),
        [VMEM] * (4 * STREAMS),
        [message] * pairs + [shape((pairs, sensors, 2 * LANES), bf16)],
        moved=2 * 2**20,
    )(*mine, *theirs, *keeps, *gots)
    got = swap(give, "sensor", 1)
    posts = call(
        functools.partial(post_kernel, pairs),
        [VMEM] * (4 + pairs),
        [shape((cells, 2 * LANES), bf16)] * quads,
        [pltpu.VMEM((groups, 2 * LANES, halves * sensors), bf16), pltpu.VMEM((quads, cells, 2 * LANES), bf16)],
        flops=2**31,
        moved=8 * 2**20,
    )(scale, near, prior, *finals, got)
    near_ones = call(
        send_kernel,
        [VMEM] * (1 + quads),
        [shape((CORES + 1, sensors, 2 * LANES), bf16)] * quads,
        moved=2**20,
    )(finals[0], *posts)
    duals = {}
    for e in reversed(range(pairs)):
        for d in reversed(range(quads)):
            out = near_ones[d] if e == 0 else finals[e]
            duals[e * quads + d] = swap(out, both, CORES * e * quads + d) if e + d else out
    dual, posterior = call(
        functools.partial(end_kernel, pairs * quads, quads),
        [VMEM] * (pairs * quads),
        [shape((frequencies, halves, sensors, LANES), f32), shape((quads, cells * 2, LANES), f32)],
        [
            pltpu.VMEM((pairs * quads, CORES, halves, sensors, LANES), f32),
            pltpu.VMEM((quads, cells * 2, LANES), f32),
            pltpu.SemaphoreType.DMA((pairs * quads, CORES + 1)),
        ],
        [ANY, ANY],
        moved=8 * 2**20,
    )(*[duals[i] for i in range(pairs * quads)])
    return dual, posterior.reshape(quads, cells, 2, LANES)


def solution(mesh):
    groups, space = mesh.devices.shape

    def run(forward_map, observed, noise_var, prior_rows, prior_scale):
        quads = forward_map.shape[0] // groups
        split = Mesh(mesh.devices.reshape(groups, space // quads, quads), ("sensor", "side", "quad"))
        return jax.shard_map(
            on_device,
            mesh=split,
            in_specs=(
                P(None, None, "sensor", ("side", "quad")),
                P(None, None, "sensor", None),
                P("sensor"),
                P(("side", "quad"), None),
                P(),
            ),
            out_specs=(P(None, None, "sensor", None), P("sensor", ("side", "quad"), None, None)),
            check_vma=False,
        )(forward_map, observed, noise_var, prior_rows, prior_scale)

    return run
```

```python
import functools

import jax
import jax.numpy as jnp
from jax import lax
from jax.experimental import pallas as pl
from jax.experimental.pallas import tpu as pltpu
from jax.sharding import Mesh, PartitionSpec as P

ITERS = 2
relax_step = 0.25
STREAMS = 2
CORES = 2
LANES = 128
HALF = LANES // 2
VMEM_LIMIT = 16 * 2**20
VMEM = pl.BlockSpec(memory_space=pltpu.VMEM)
SMEM = pl.BlockSpec(memory_space=pltpu.SMEM)
ANY = pl.BlockSpec(memory_space=pl.ANY)
bf16, f32 = jnp.bfloat16, jnp.float32


def shape(dims, dtype):
    return jax.ShapeDtypeStruct(dims, dtype)


def call(kernel, in_specs, out_shape, scratch=(), out_specs=None, flops=0, moved=0, aliases=None):
    return pl.pallas_call(
        kernel,
        input_output_aliases=aliases or {},
        in_specs=in_specs,
        out_specs=out_specs or [VMEM] * len(out_shape),
        out_shape=out_shape,
        scratch_shapes=list(scratch),
        cost_estimate=pl.CostEstimate(flops=flops, bytes_accessed=moved, transcendentals=0),
        compiler_params=pltpu.CompilerParams(vmem_limit_bytes=VMEM_LIMIT),
    )


def swap(x, axes, distance):
    count = lax.axis_size(axes)
    return lax.ppermute(x, axes, [(i, i ^ distance) for i in range(count)])


def dot(a, b):
    return jnp.dot(a, b, preferred_element_type=f32)


def dot_nt(a, b):
    return lax.dot_general(a, b, (((1,), (1,)), ((), ())), preferred_element_type=f32)


def my_place():
    me = lax.axis_index("sensor")
    return me // CORES, lax.axis_index("quad"), me % CORES


def data_kernel(groups, quads, obs_ref, noise_ref, *refs):
    outs, (held, sems) = refs[:groups], refs[groups:]
    sensors = obs_ref.shape[2]
    copies = []
    for d in range(groups):
        freq = ((my_place()[0] * CORES + my_place()[2]) ^ d) * quads + my_place()[1]
        copies.append(pltpu.make_async_copy(obs_ref.at[freq], held.at[d], sems.at[d]))
        copies[-1].start()
    noise = noise_ref[...]
    high = noise.astype(bf16)
    low = (noise - high.astype(f32)).astype(bf16)
    tail = jnp.concatenate([jnp.broadcast_to(high, (8, sensors)), jnp.broadcast_to(low, (8, sensors))], 0)
    for d in range(groups):
        copies[d].wait()
        re, im = held[d, 0], held[d, 1]
        for s in range(STREAMS):
            part = slice(s * HALF, (s + 1) * HALF)
            outs[d][:sensors, s * LANES:(s + 1) * LANES] = jnp.concatenate([re[:, part], im[:, part]], 1).astype(bf16)
        outs[d][sensors:, :] = tail


def pack_diagonal(block, out_ref, at):
    half = block.shape[0] // 2
    out_ref[at:at + half, :] = block[:half]
    corner = block[half:, half:]
    out_ref[at + half:at + half + half // 2, :] = jnp.concatenate([corner[:half // 2], corner[half // 2:]], 1)


def unpack_diagonal(came_ref, at):
    half = came_ref.shape[1] // 2
    upper = came_ref[at:at + half, :]
    corner = came_ref[at + half:at + half + half // 2, :]
    corner = jnp.concatenate([corner[:, :half], corner[:, half:]], 0)
    return jnp.concatenate([upper, jnp.concatenate([upper[:, half:].T, corner], 1)], 0)


def prior_kernel(scale_ref, own_ref, after_ref, full_ref, diagonal_ref, wide_ref):
    cells = own_ref.shape[0]
    quad = my_place()[1]
    on, off = (pl.ds(pl.multiple_of(p * cells, cells), cells) for p in (quad & 1, 1 - (quad & 1)))
    diagonal = own_ref[:, on]
    pack_diagonal(diagonal, diagonal_ref, 0)
    full_ref[:cells, :] = own_ref[:, off]
    pack_diagonal(diagonal, full_ref, cells)
    wide_ref[...] = jnp.full(wide_ref.shape, scale_ref[0], f32)


def gather_kernel(groups, quads, own_ref, *refs):
    came, data = refs[:quads - 1], refs[quads - 1:quads - 1 + groups]
    prior_ref, noise_ref, *streams = refs[quads + groups:]
    me, quad = lax.axis_index("sensor"), my_place()[1]
    sensors, cells = streams[0].shape[1], own_ref.shape[0]
    on, off = (pl.ds(pl.multiple_of(p * cells, cells), cells) for p in (quad & 1, 1 - (quad & 1)))
    for d in range(0, quads, 2):
        diagonal = own_ref[:, on] if d == 0 else unpack_diagonal(came[d - 1], cells)
        beside = own_ref[:, off] if d == 0 else came[d - 1][:cells, :]
        prior_ref[quad ^ d, :, on] = diagonal
        prior_ref[quad ^ d, :, off] = beside
        prior_ref[quad ^ d ^ 1, :, on] = beside.T
        prior_ref[quad ^ d ^ 1, :, off] = unpack_diagonal(came[d], 0)
    row = lax.broadcasted_iota(jnp.int32, (sensors, sensors), 0)
    col = lax.broadcasted_iota(jnp.int32, (sensors, sensors), 1)
    for d in range(groups):
        for s in range(STREAMS):
            streams[s][me ^ d] = data[d][:sensors, s * LANES:(s + 1) * LANES]
        both = data[d][sensors:, :].astype(f32)
        noise_row = both[0:1, :] + both[8:9, :]
        noise = jnp.sum(jnp.where(row == col, noise_row, 0.0), 1, keepdims=True)
        noise_ref[me ^ d] = jnp.broadcast_to(noise, (sensors, LANES))


def source(map_ref, sides_ref, prior_ref, scale):
    groups, quads, _, cells = map_ref.shape
    per_block = prior_ref.shape[2] // cells
    out = []
    for block in range(quads // per_block):
        members = range(block * per_block, (block + 1) * per_block)
        parts = []
        for q in members:
            u = jnp.zeros((sides_ref.shape[1], cells), f32)
            for g in range(groups):
                u += dot(sides_ref[g], map_ref[g, q])
            parts.append(u.astype(bf16))
        ub = jnp.concatenate(parts, 1)
        out += [(dot_nt(prior_ref[q], ub) * scale).astype(bf16) for q in members]
    return out


def sides(z):
    half = z.shape[1] // 2
    return jnp.concatenate([z, jnp.concatenate([z[:, half:], -z[:, :half]], 1)], 0).T


def bring_kernel(map_ref, out_ref, sem):
    copy = pltpu.make_async_copy(map_ref, out_ref, sem)
    copy.start()
    copy.wait()


def step_kernel(stage, n_pred, n_after, scale_ref, map_ref, prior_ref, obs_ref, noise_ref, *refs):
    groups, quads, double, _ = map_ref.shape
    sensors = double // 2
    preds, refs = refs[:n_pred], refs[n_pred + n_after:]
    if stage > 0:
        outs, (sides_ref, now_ref, partial_ref) = refs[:4], refs[4:]
    else:
        out_ref, sides_ref = refs
    for g in range(groups):
        obs = obs_ref[g].astype(f32)
        now = relax_step * obs
        if stage > 0:
            predicted = sum(p[g].astype(f32) for p in preds)
            now = now + relax_step * (obs - predicted - noise_ref[g] * now)
            now_ref[g] = now + relax_step * (obs - noise_ref[g] * now)
        sides_ref[g] = sides(now.astype(bf16))
    sources = source(map_ref, sides_ref, prior_ref, scale_ref[0:1, 0:1])
    turned = [jnp.concatenate([-v[:, HALF:], v[:, :HALF]], 1) for v in sources]
    for g in range(groups):
        total = jnp.zeros((sensors, LANES), f32)
        for q in range(quads):
            total += dot(map_ref[g, q, :sensors, :], sources[q]) + dot(map_ref[g, q, sensors:, :], turned[q])
        if stage == 0:
            out_ref[g] = total.astype(bf16)
        else:
            now_ref[g] -= relax_step * total
            partial_ref[g] = total.astype(bf16)
    if stage > 0:
        for e in range(groups // CORES):
            for parity, core in ((0, my_place()[2]), (1, 1 - my_place()[2])):
                g = CORES * (my_place()[0] ^ e) + core
                outs[parity][e] = partial_ref[g]
                outs[2 + parity][e] = now_ref[g].astype(outs[2 + parity].dtype)


def last_kernel(pairs, *refs):
    mine, theirs, keeps, gots = (refs[i * STREAMS:(i + 1) * STREAMS] for i in range(4))
    *outs, give_ref = refs[4 * STREAMS:]
    core = my_place()[2]
    for e in range(pairs):
        own = join([keeps[s][e] - relax_step * mine[s][e].astype(f32) for s in range(STREAMS)])
        other = join([gots[s][e].astype(f32) - relax_step * theirs[s][e].astype(f32) for s in range(STREAMS)])
        outs[e][core] = own.astype(bf16)
        outs[e][1 - core] = other.astype(bf16)
        give_ref[e] = other.astype(bf16)


def join(streams):
    return jnp.concatenate([x[:, :HALF] for x in streams] + [x[:, HALF:] for x in streams], 1)


def send_kernel(dual_ref, *refs):
    posts, outs = refs[:len(refs) // 2], refs[len(refs) // 2:]
    for post, out in zip(posts, outs):
        out[:CORES] = dual_ref[...]
        out[CORES] = post[...]


def post_kernel(pairs, scale_ref, map_ref, prior_ref, *refs):
    duals, got_ref, refs = refs[:pairs], refs[pairs], refs[pairs + 1:]
    outs, (sides_ref, held_ref) = refs[:-2], refs[-2:]
    core = my_place()[2]
    for e in range(pairs):
        first = CORES * (my_place()[0] ^ e)
        sides_ref[first + core] = sides(duals[e][core])
        sides_ref[first + 1 - core] = sides(got_ref[e])
    for q, v in enumerate(source(map_ref, sides_ref, prior_ref, scale_ref[0:1, 0:1])):
        held_ref[q] = v
    for d, out in enumerate(outs):
        out[...] = held_ref[my_place()[1] ^ d]


def end_kernel(e, quads, follows, *refs):
    came, refs = refs[:quads], refs[quads + follows:]
    count = 1 + (e == 0)
    outs, (dual_ref, sems, *post) = refs[:count], refs[count:]
    pair, quad, _ = my_place()
    sends = []
    for d in range(quads):
        for core in range(CORES):
            freq = (CORES * (pair ^ e) + core) * quads + (quad ^ d)
            for part in range(2):
                dual_ref[d, core, part] = came[d][core, :, part * LANES:(part + 1) * LANES].astype(f32)
            sends.append(pltpu.make_async_copy(dual_ref.at[d, core], outs[0].at[freq], sems.at[d, core]))
            sends[-1].start()
        if e == 0:
            post_ref = post[0]
            cells = post_ref.shape[1] // 2
            post_ref[d, pl.ds(0, cells, stride=2), :] = came[d][CORES, :, :LANES].astype(f32)
            post_ref[d, pl.ds(1, cells, stride=2), :] = came[d][CORES, :, LANES:].astype(f32)
            sends.append(pltpu.make_async_copy(post_ref.at[d], outs[1].at[quad ^ d], sems.at[d, CORES]))
            sends[-1].start()
    for copy in sends:
        copy.wait()


def on_device(forward_map, observed, noise_var, prior_rows, prior_scale):
    frequencies, halves, sensors, cells = forward_map.shape
    groups, quads, count = (lax.axis_size(a) for a in ("sensor", "quad", "side"))
    width = prior_rows.shape[1]
    me, quad = lax.axis_index("sensor"), lax.axis_index("quad")
    scale = lax.dynamic_slice_in_dim(prior_scale, me * quads + quad, 1, 0)
    both = ("sensor", "quad")

    held = lax.all_to_all(
        forward_map.reshape(frequencies, halves * sensors, cells), both, split_axis=0, concat_axis=0, tiled=True
    ).reshape(groups, quads, halves * sensors, cells)

    data = call(
        functools.partial(data_kernel, groups, quads),
        [ANY, VMEM],
        [shape((sensors + 16, STREAMS * LANES), bf16)] * groups,
        [pltpu.VMEM((groups, halves, sensors, LANES), f32), pltpu.SemaphoreType.DMA((groups,))],
        moved=groups * sensors * LANES * 12,
    )(observed, noise_var.reshape(1, sensors))
    data = [data[0]] + [swap(data[d], "sensor", d) for d in range(1, groups)]
    packed = cells // 2 + cells // 4
    rows, diagonal, scale = call(
        prior_kernel,
        [SMEM, VMEM, ANY],
        [shape((cells + packed, cells), bf16), shape((packed, cells), bf16), shape((8, LANES), f32)],
    )(scale, prior_rows, data[1])
    came = [swap(diagonal if d % 2 else rows, "quad", d) for d in range(1, quads)]
    near = call(bring_kernel, [ANY], [shape(held.shape, bf16)], [pltpu.SemaphoreType.DMA], moved=8 * 2**20)(held)[0]

    prior, noise, *streams = call(
        functools.partial(gather_kernel, groups, quads),
        [VMEM] * (quads + groups) + [ANY],
        [shape((quads, cells, width), bf16), shape((groups, sensors, LANES), f32)]
        + [shape((groups, sensors, LANES), bf16)] * STREAMS,
        moved=8 * 2**20,
    )(prior_rows, *came, *data, near)

    def over_sides(partial):
        if count == 2:
            return [partial, swap(partial, "side", 1)]
        return [lax.psum(partial, "side")]

    wide, narrow = shape((groups, sensors, LANES), f32), shape((groups, sensors, LANES), bf16)

    def step(stage, obs, preds, after=()):
        operands = [scale, near, prior, obs, noise] + preds
        scratch = [pltpu.VMEM((groups, LANES, halves * sensors), bf16)]
        if stage > 0:
            scratch += [pltpu.VMEM((groups, sensors, LANES), f32), pltpu.VMEM((groups, sensors, LANES), bf16)]
        return call(
            functools.partial(step_kernel, stage, len(preds), len(after)),
            [VMEM] * len(operands) + [ANY] * len(after),
            [part, part, shape(part.shape, f32), part] if stage > 0 else [narrow],
            scratch,
            flops=2**31,
            moved=8 * 2**20,
        )(*operands, *after)

    pairs = groups // CORES
    part = shape((pairs, sensors, LANES), bf16)
    partials = [step(0, streams[s], [])[0] for s in range(STREAMS)]
    preds = [over_sides(x) for x in partials]
    steps = [step(1, streams[s], preds[s], partials[s + 1:]) for s in range(STREAMS)]

    def to_other_sides(x, cross):
        if count == 2:
            return lax.ppermute(
                x, ("sensor", "side"), [(i, i ^ (1 + CORES * cross)) for i in range(groups * count)]
            )
        rest = lax.psum(x.astype(f32), "side") - x.astype(f32)
        return (swap(rest, "sensor", 1) if cross else rest).astype(bf16)

    mine = [to_other_sides(x[0], 0) for x in steps]
    theirs = [to_other_sides(x[1], 1) for x in steps]
    keeps, gots = [x[2] for x in steps], [swap(x[3], "sensor", 1) for x in steps]
    message = shape((CORES, sensors, 2 * LANES), bf16)
    *finals, give = call(
        functools.partial(last_kernel, pairs),
        [VMEM] * (4 * STREAMS),
        [message] * pairs + [shape((pairs, sensors, 2 * LANES), bf16)],
        moved=2 * 2**20,
    )(*mine, *theirs, *keeps, *gots)
    got = swap(give, "sensor", 1)
    posts = call(
        functools.partial(post_kernel, pairs),
        [VMEM] * (4 + pairs),
        [shape((cells, 2 * LANES), bf16)] * quads,
        [pltpu.VMEM((groups, 2 * LANES, halves * sensors), bf16), pltpu.VMEM((quads, cells, 2 * LANES), bf16)],
        flops=2**31,
        moved=8 * 2**20,
    )(scale, near, prior, *finals, got)
    near_ones = call(
        send_kernel,
        [VMEM] * (1 + quads),
        [shape((CORES + 1, sensors, 2 * LANES), bf16)] * quads,
        moved=2**20,
    )(finals[0], *posts)
    duals = {}
    for e in reversed(range(pairs)):
        for d in reversed(range(quads)):
            out = near_ones[d] if e == 0 else finals[e]
            duals[e * quads + d] = swap(out, both, CORES * e * quads + d) if e + d else out
    dual, posterior = [], []
    for e in reversed(range(pairs)):
        out = [shape((frequencies, halves, sensors, LANES), f32)]
        scratch = [
            pltpu.VMEM((quads, CORES, halves, sensors, LANES), f32),
            pltpu.SemaphoreType.DMA((quads, CORES + 1)),
        ]
        if e == 0:
            out.append(shape((quads, cells * 2, LANES), f32))
            scratch.append(pltpu.VMEM((quads, cells * 2, LANES), f32))
        *dual, last = call(
            functools.partial(end_kernel, e, quads, len(dual)),
            [VMEM] * quads + [ANY] * len(dual),
            out,
            scratch,
            [ANY] * len(out),
            moved=4 * 2**20,
            aliases={quads: 0} if dual else None,
        )(*[duals[e * quads + d] for d in range(quads)], *dual)
        if e:
            dual = [last]
    return dual[0], last.reshape(quads, cells, 2, LANES)


def solution(mesh):
    groups, space = mesh.devices.shape

    def run(forward_map, observed, noise_var, prior_rows, prior_scale):
        quads = forward_map.shape[0] // groups
        split = Mesh(mesh.devices.reshape(groups, space // quads, quads), ("sensor", "side", "quad"))
        return jax.shard_map(
            on_device,
            mesh=split,
            in_specs=(
                P(None, None, "sensor", ("side", "quad")),
                P(None, None, "sensor", None),
                P("sensor"),
                P(("side", "quad"), None),
                P(),
            ),
            out_specs=(P(None, None, "sensor", None), P("sensor", ("side", "quad"), None, None)),
            check_vma=False,
        )(forward_map, observed, noise_var, prior_rows, prior_scale)

    return run
```

```python
import functools

import jax
import jax.numpy as jnp
from jax import lax
from jax.experimental import pallas as pl
from jax.experimental.pallas import tpu as pltpu
from jax.sharding import Mesh, PartitionSpec as P

ITERS = 2
relax_step = 0.25
STREAMS = 2
CORES = 2
LANES = 128
HALF = LANES // 2
VMEM_LIMIT = 16 * 2**20
VMEM = pl.BlockSpec(memory_space=pltpu.VMEM)
SMEM = pl.BlockSpec(memory_space=pltpu.SMEM)
ANY = pl.BlockSpec(memory_space=pl.ANY)
bf16, f32 = jnp.bfloat16, jnp.float32


def shape(dims, dtype):
    return jax.ShapeDtypeStruct(dims, dtype)


def call(kernel, in_specs, out_shape, scratch=(), out_specs=None, flops=0, moved=0, aliases=None):
    return pl.pallas_call(
        kernel,
        input_output_aliases=aliases or {},
        in_specs=in_specs,
        out_specs=out_specs or [VMEM] * len(out_shape),
        out_shape=out_shape,
        scratch_shapes=list(scratch),
        cost_estimate=pl.CostEstimate(flops=flops, bytes_accessed=moved, transcendentals=0),
        compiler_params=pltpu.CompilerParams(vmem_limit_bytes=VMEM_LIMIT),
    )


def swap(x, axes, distance):
    count = lax.axis_size(axes)
    return lax.ppermute(x, axes, [(i, i ^ distance) for i in range(count)])


def dot(a, b):
    return jnp.dot(a, b, preferred_element_type=f32)


def dot_nt(a, b):
    return lax.dot_general(a, b, (((1,), (1,)), ((), ())), preferred_element_type=f32)


def my_place():
    me = lax.axis_index("sensor")
    return me // CORES, lax.axis_index("quad"), me % CORES


def data_kernel(groups, quads, obs_ref, noise_ref, *refs):
    outs, (held, sems) = refs[:groups], refs[groups:]
    sensors = obs_ref.shape[2]
    copies = []
    for d in range(groups):
        freq = ((my_place()[0] * CORES + my_place()[2]) ^ d) * quads + my_place()[1]
        copies.append(pltpu.make_async_copy(obs_ref.at[freq], held.at[d], sems.at[d]))
        copies[-1].start()
    noise = noise_ref[...]
    high = noise.astype(bf16)
    low = (noise - high.astype(f32)).astype(bf16)
    tail = jnp.concatenate([jnp.broadcast_to(high, (8, sensors)), jnp.broadcast_to(low, (8, sensors))], 0)
    for d in range(groups):
        copies[d].wait()
        re, im = held[d, 0], held[d, 1]
        for s in range(STREAMS):
            part = slice(s * HALF, (s + 1) * HALF)
            outs[d][:sensors, s * LANES:(s + 1) * LANES] = jnp.concatenate([re[:, part], im[:, part]], 1).astype(bf16)
        outs[d][sensors:, :] = tail


def pack_diagonal(block, out_ref, at):
    half = block.shape[0] // 2
    out_ref[at:at + half, :] = block[:half]
    corner = block[half:, half:]
    out_ref[at + half:at + half + half // 2, :] = jnp.concatenate([corner[:half // 2], corner[half // 2:]], 1)


def unpack_diagonal(came_ref, at):
    half = came_ref.shape[1] // 2
    upper = came_ref[at:at + half, :]
    corner = came_ref[at + half:at + half + half // 2, :]
    corner = jnp.concatenate([corner[:, :half], corner[:, half:]], 0)
    return jnp.concatenate([upper, jnp.concatenate([upper[:, half:].T, corner], 1)], 0)


def prior_kernel(scale_ref, own_ref, after_ref, full_ref, diagonal_ref, wide_ref):
    cells = own_ref.shape[0]
    quad = my_place()[1]
    on, off = (pl.ds(pl.multiple_of(p * cells, cells), cells) for p in (quad & 1, 1 - (quad & 1)))
    diagonal = own_ref[:, on]
    pack_diagonal(diagonal, diagonal_ref, 0)
    full_ref[:cells, :] = own_ref[:, off]
    pack_diagonal(diagonal, full_ref, cells)
    wide_ref[...] = jnp.full(wide_ref.shape, scale_ref[0], f32)


def gather_kernel(groups, quads, own_ref, *refs):
    came, data = refs[:quads - 1], refs[quads - 1:quads - 1 + groups]
    prior_ref, noise_ref, *streams = refs[quads + groups:]
    me, quad = lax.axis_index("sensor"), my_place()[1]
    sensors, cells = streams[0].shape[1], own_ref.shape[0]
    on, off = (pl.ds(pl.multiple_of(p * cells, cells), cells) for p in (quad & 1, 1 - (quad & 1)))
    for d in range(0, quads, 2):
        diagonal = own_ref[:, on] if d == 0 else unpack_diagonal(came[d - 1], cells)
        beside = own_ref[:, off] if d == 0 else came[d - 1][:cells, :]
        prior_ref[quad ^ d, :, on] = diagonal
        prior_ref[quad ^ d, :, off] = beside
        prior_ref[quad ^ d ^ 1, :, on] = beside.T
        prior_ref[quad ^ d ^ 1, :, off] = unpack_diagonal(came[d], 0)
    row = lax.broadcasted_iota(jnp.int32, (sensors, sensors), 0)
    col = lax.broadcasted_iota(jnp.int32, (sensors, sensors), 1)
    for d in range(groups):
        for s in range(STREAMS):
            streams[s][me ^ d] = data[d][:sensors, s * LANES:(s + 1) * LANES]
        both = data[d][sensors:, :].astype(f32)
        noise_row = both[0:1, :] + both[8:9, :]
        noise = jnp.sum(jnp.where(row == col, noise_row, 0.0), 1, keepdims=True)
        noise_ref[me ^ d] = jnp.broadcast_to(noise, (sensors, LANES))


def source(map_ref, sides_ref, prior_ref, scale):
    groups, quads, _, cells = map_ref.shape
    per_block = prior_ref.shape[2] // cells
    out = []
    for block in range(quads // per_block):
        members = range(block * per_block, (block + 1) * per_block)
        parts = []
        for q in members:
            u = jnp.zeros((sides_ref.shape[1], cells), f32)
            for g in range(groups):
                u += dot(sides_ref[g], map_ref[g, q])
            parts.append(u.astype(bf16))
        ub = jnp.concatenate(parts, 1)
        out += [(dot_nt(prior_ref[q], ub) * scale).astype(bf16) for q in members]
    return out


def sides(z):
    half = z.shape[1] // 2
    return jnp.concatenate([z, jnp.concatenate([z[:, half:], -z[:, :half]], 1)], 0).T


def bring_kernel(map_ref, out_ref, sem):
    copy = pltpu.make_async_copy(map_ref, out_ref, sem)
    copy.start()
    copy.wait()


def step_kernel(stage, n_pred, n_after, scale_ref, map_ref, prior_ref, obs_ref, noise_ref, *refs):
    groups, quads, double, _ = map_ref.shape
    sensors = double // 2
    preds, refs = refs[:n_pred], refs[n_pred + n_after:]
    if stage > 0:
        outs, (sides_ref, now_ref, partial_ref) = refs[:4], refs[4:]
    else:
        out_ref, sides_ref = refs
    for g in range(groups):
        obs = obs_ref[g].astype(f32)
        now = relax_step * obs
        if stage > 0:
            predicted = sum(p[g].astype(f32) for p in preds)
            now = now + relax_step * (obs - predicted - noise_ref[g] * now)
            now_ref[g] = now + relax_step * (obs - noise_ref[g] * now)
        sides_ref[g] = sides(now.astype(bf16))
    sources = source(map_ref, sides_ref, prior_ref, scale_ref[0:1, 0:1])
    turned = [jnp.concatenate([-v[:, HALF:], v[:, :HALF]], 1) for v in sources]
    for g in range(groups):
        total = jnp.zeros((sensors, LANES), f32)
        for q in range(quads):
            total += dot(map_ref[g, q, :sensors, :], sources[q]) + dot(map_ref[g, q, sensors:, :], turned[q])
        if stage == 0:
            out_ref[g] = total.astype(bf16)
        else:
            now_ref[g] -= relax_step * total
            partial_ref[g] = total.astype(bf16)
    if stage > 0:
        for e in range(groups // CORES):
            for parity, core in ((0, my_place()[2]), (1, 1 - my_place()[2])):
                g = CORES * (my_place()[0] ^ e) + core
                outs[parity][e] = partial_ref[g]
                outs[2 + parity][e] = now_ref[g].astype(outs[2 + parity].dtype)


def last_kernel(pairs, *refs):
    mine, theirs, keeps, gots = (refs[i * STREAMS:(i + 1) * STREAMS] for i in range(4))
    *outs, give_ref = refs[4 * STREAMS:]
    core = my_place()[2]
    for e in range(pairs):
        own = join([keeps[s][e] - relax_step * mine[s][e].astype(f32) for s in range(STREAMS)])
        other = join([gots[s][e].astype(f32) - relax_step * theirs[s][e].astype(f32) for s in range(STREAMS)])
        outs[e][core] = own.astype(bf16)
        outs[e][1 - core] = other.astype(bf16)
        give_ref[e] = other.astype(bf16)


def join(streams):
    return jnp.concatenate([x[:, :HALF] for x in streams] + [x[:, HALF:] for x in streams], 1)


def send_kernel(dual_ref, *refs):
    posts, outs = refs[:len(refs) // 2], refs[len(refs) // 2:]
    for post, out in zip(posts, outs):
        out[:CORES] = dual_ref[...]
        out[CORES] = post[...]


def post_kernel(pairs, scale_ref, map_ref, prior_ref, *refs):
    duals, got_ref, refs = refs[:pairs], refs[pairs], refs[pairs + 1:]
    outs, (sides_ref, held_ref) = refs[:-2], refs[-2:]
    core = my_place()[2]
    for e in range(pairs):
        first = CORES * (my_place()[0] ^ e)
        sides_ref[first + core] = sides(duals[e][core])
        sides_ref[first + 1 - core] = sides(got_ref[e])
    for q, v in enumerate(source(map_ref, sides_ref, prior_ref, scale_ref[0:1, 0:1])):
        held_ref[q] = v
    for d, out in enumerate(outs):
        out[...] = held_ref[my_place()[1] ^ d]


def end_kernel(e, quads, members, follows, *refs):
    came, refs = refs[:len(members)], refs[len(members) + follows:]
    count = 1 + (e == 0)
    outs, (dual_ref, sems, *post) = refs[:count], refs[count:]
    pair, quad, _ = my_place()
    sends = []
    for i, d in enumerate(members):
        for core in range(CORES):
            freq = (CORES * (pair ^ e) + core) * quads + (quad ^ d)
            for part in range(2):
                dual_ref[i, core, part] = came[i][core, :, part * LANES:(part + 1) * LANES].astype(f32)
            sends.append(pltpu.make_async_copy(dual_ref.at[i, core], outs[0].at[freq], sems.at[i, core]))
            sends[-1].start()
        if e == 0:
            post_ref = post[0]
            cells = post_ref.shape[1] // 2
            post_ref[i, pl.ds(0, cells, stride=2), :] = came[i][CORES, :, :LANES].astype(f32)
            post_ref[i, pl.ds(1, cells, stride=2), :] = came[i][CORES, :, LANES:].astype(f32)
            sends.append(pltpu.make_async_copy(post_ref.at[i], outs[1].at[quad ^ d], sems.at[i, CORES]))
            sends[-1].start()
    for copy in sends:
        copy.wait()


def on_device(forward_map, observed, noise_var, prior_rows, prior_scale):
    frequencies, halves, sensors, cells = forward_map.shape
    groups, quads, count = (lax.axis_size(a) for a in ("sensor", "quad", "side"))
    width = prior_rows.shape[1]
    me, quad = lax.axis_index("sensor"), lax.axis_index("quad")
    scale = lax.dynamic_slice_in_dim(prior_scale, me * quads + quad, 1, 0)
    both = ("sensor", "quad")

    held = lax.all_to_all(
        forward_map.reshape(frequencies, halves * sensors, cells), both, split_axis=0, concat_axis=0, tiled=True
    ).reshape(groups, quads, halves * sensors, cells)

    data = call(
        functools.partial(data_kernel, groups, quads),
        [ANY, VMEM],
        [shape((sensors + 16, STREAMS * LANES), bf16)] * groups,
        [pltpu.VMEM((groups, halves, sensors, LANES), f32), pltpu.SemaphoreType.DMA((groups,))],
        moved=groups * sensors * LANES * 12,
    )(observed, noise_var.reshape(1, sensors))
    data = [data[0]] + [swap(data[d], "sensor", d) for d in range(1, groups)]
    packed = cells // 2 + cells // 4
    rows, diagonal, scale = call(
        prior_kernel,
        [SMEM, VMEM, ANY],
        [shape((cells + packed, cells), bf16), shape((packed, cells), bf16), shape((8, LANES), f32)],
    )(scale, prior_rows, data[1])
    came = [swap(diagonal if d % 2 else rows, "quad", d) for d in range(1, quads)]
    near = call(bring_kernel, [ANY], [shape(held.shape, bf16)], [pltpu.SemaphoreType.DMA], moved=8 * 2**20)(held)[0]

    prior, noise, *streams = call(
        functools.partial(gather_kernel, groups, quads),
        [VMEM] * (quads + groups) + [ANY],
        [shape((quads, cells, width), bf16), shape((groups, sensors, LANES), f32)]
        + [shape((groups, sensors, LANES), bf16)] * STREAMS,
        moved=8 * 2**20,
    )(prior_rows, *came, *data, near)

    def over_sides(partial):
        if count == 2:
            return [partial, swap(partial, "side", 1)]
        return [lax.psum(partial, "side")]

    wide, narrow = shape((groups, sensors, LANES), f32), shape((groups, sensors, LANES), bf16)

    def step(stage, obs, preds, after=()):
        operands = [scale, near, prior, obs, noise] + preds
        scratch = [pltpu.VMEM((groups, LANES, halves * sensors), bf16)]
        if stage > 0:
            scratch += [pltpu.VMEM((groups, sensors, LANES), f32), pltpu.VMEM((groups, sensors, LANES), bf16)]
        return call(
            functools.partial(step_kernel, stage, len(preds), len(after)),
            [VMEM] * len(operands) + [ANY] * len(after),
            [part, part, shape(part.shape, f32), part] if stage > 0 else [narrow],
            scratch,
            flops=2**31,
            moved=8 * 2**20,
        )(*operands, *after)

    pairs = groups // CORES
    part = shape((pairs, sensors, LANES), bf16)
    partials = [step(0, streams[s], [])[0] for s in range(STREAMS)]
    preds = [over_sides(x) for x in partials]
    steps = [step(1, streams[s], preds[s], partials[s + 1:]) for s in range(STREAMS)]

    def to_other_sides(x, cross):
        if count == 2:
            return lax.ppermute(
                x, ("sensor", "side"), [(i, i ^ (1 + CORES * cross)) for i in range(groups * count)]
            )
        rest = lax.psum(x.astype(f32), "side") - x.astype(f32)
        return (swap(rest, "sensor", 1) if cross else rest).astype(bf16)

    mine = [to_other_sides(x[0], 0) for x in steps]
    theirs = [to_other_sides(x[1], 1) for x in steps]
    keeps, gots = [x[2] for x in steps], [swap(x[3], "sensor", 1) for x in steps]
    message = shape((CORES, sensors, 2 * LANES), bf16)
    *finals, give = call(
        functools.partial(last_kernel, pairs),
        [VMEM] * (4 * STREAMS),
        [message] * pairs + [shape((pairs, sensors, 2 * LANES), bf16)],
        moved=2 * 2**20,
    )(*mine, *theirs, *keeps, *gots)
    got = swap(give, "sensor", 1)
    posts = call(
        functools.partial(post_kernel, pairs),
        [VMEM] * (4 + pairs),
        [shape((cells, 2 * LANES), bf16)] * quads,
        [pltpu.VMEM((groups, 2 * LANES, halves * sensors), bf16), pltpu.VMEM((quads, cells, 2 * LANES), bf16)],
        flops=2**31,
        moved=8 * 2**20,
    )(scale, near, prior, *finals, got)
    near_ones = call(
        send_kernel,
        [VMEM] * (1 + quads),
        [shape((CORES + 1, sensors, 2 * LANES), bf16)] * quads,
        moved=2**20,
    )(finals[0], *posts)
    duals = {}
    for e in reversed(range(pairs)):
        for d in reversed(range(quads)):
            out = near_ones[d] if e == 0 else finals[e]
            duals[e * quads + d] = swap(out, both, CORES * e * quads + d) if e + d else out
    far = [(e, list(range(quads))) for e in reversed(range(1, pairs))]
    done = []
    for e, members in far + [(0, list(range(0, quads, 2))), (0, list(range(1, quads, 2)))]:
        count = len(members)
        out = [shape((frequencies, halves, sensors, LANES), f32)]
        scratch = [
            pltpu.VMEM((count, CORES, halves, sensors, LANES), f32),
            pltpu.SemaphoreType.DMA((count, CORES + 1)),
        ]
        if e == 0:
            out.append(shape((quads, cells * 2, LANES), f32))
            scratch.append(pltpu.VMEM((count, cells * 2, LANES), f32))
        done = call(
            functools.partial(end_kernel, e, quads, members, len(done)),
            [VMEM] * count + [ANY] * len(done),
            out,
            scratch,
            [ANY] * len(out),
            moved=4 * 2**20,
            aliases={count + i: i for i in range(len(done))},
        )(*[duals[e * quads + d] for d in members], *done)
    dual, posterior = done
    return dual, posterior.reshape(quads, cells, 2, LANES)


def solution(mesh):
    groups, space = mesh.devices.shape

    def run(forward_map, observed, noise_var, prior_rows, prior_scale):
        quads = forward_map.shape[0] // groups
        split = Mesh(mesh.devices.reshape(groups, space // quads, quads), ("sensor", "side", "quad"))
        return jax.shard_map(
            on_device,
            mesh=split,
            in_specs=(
                P(None, None, "sensor", ("side", "quad")),
                P(None, None, "sensor", None),
                P("sensor"),
                P(("side", "quad"), None),
                P(),
            ),
            out_specs=(P(None, None, "sensor", None), P("sensor", ("side", "quad"), None, None)),
            check_vma=False,
        )(forward_map, observed, noise_var, prior_rows, prior_scale)

    return run
```

```python
import functools

import jax
import jax.numpy as jnp
from jax import lax
from jax.experimental import pallas as pl
from jax.experimental.pallas import tpu as pltpu
from jax.sharding import Mesh, PartitionSpec as P

ITERS = 2
relax_step = 0.25
STREAMS = 2
CORES = 2
LANES = 128
HALF = LANES // 2
VMEM_LIMIT = 16 * 2**20
VMEM = pl.BlockSpec(memory_space=pltpu.VMEM)
SMEM = pl.BlockSpec(memory_space=pltpu.SMEM)
ANY = pl.BlockSpec(memory_space=pl.ANY)
bf16, f32 = jnp.bfloat16, jnp.float32


def shape(dims, dtype):
    return jax.ShapeDtypeStruct(dims, dtype)


def call(kernel, in_specs, out_shape, scratch=(), out_specs=None, flops=0, moved=0, aliases=None):
    return pl.pallas_call(
        kernel,
        input_output_aliases=aliases or {},
        in_specs=in_specs,
        out_specs=out_specs or [VMEM] * len(out_shape),
        out_shape=out_shape,
        scratch_shapes=list(scratch),
        cost_estimate=pl.CostEstimate(flops=flops, bytes_accessed=moved, transcendentals=0),
        compiler_params=pltpu.CompilerParams(vmem_limit_bytes=VMEM_LIMIT),
    )


def swap(x, axes, distance):
    count = lax.axis_size(axes)
    return lax.ppermute(x, axes, [(i, i ^ distance) for i in range(count)])


def dot(a, b):
    return jnp.dot(a, b, preferred_element_type=f32)


def dot_nt(a, b):
    return lax.dot_general(a, b, (((1,), (1,)), ((), ())), preferred_element_type=f32)


def my_place():
    me = lax.axis_index("sensor")
    return me // CORES, lax.axis_index("quad"), me % CORES


def data_kernel(groups, quads, obs_ref, noise_ref, *refs):
    outs, (held, sems) = refs[:groups], refs[groups:]
    sensors = obs_ref.shape[2]
    copies = []
    for d in range(groups):
        freq = ((my_place()[0] * CORES + my_place()[2]) ^ d) * quads + my_place()[1]
        copies.append(pltpu.make_async_copy(obs_ref.at[freq], held.at[d], sems.at[d]))
        copies[-1].start()
    noise = noise_ref[...]
    high = noise.astype(bf16)
    low = (noise - high.astype(f32)).astype(bf16)
    tail = jnp.concatenate([jnp.broadcast_to(high, (8, sensors)), jnp.broadcast_to(low, (8, sensors))], 0)
    for d in range(groups):
        copies[d].wait()
        re, im = held[d, 0], held[d, 1]
        for s in range(STREAMS):
            part = slice(s * HALF, (s + 1) * HALF)
            outs[d][:sensors, s * LANES:(s + 1) * LANES] = jnp.concatenate([re[:, part], im[:, part]], 1).astype(bf16)
        outs[d][sensors:, :] = tail


def pack_diagonal(block, out_ref, at):
    half = block.shape[0] // 2
    out_ref[at:at + half, :] = block[:half]
    corner = block[half:, half:]
    out_ref[at + half:at + half + half // 2, :] = jnp.concatenate([corner[:half // 2], corner[half // 2:]], 1)


def unpack_diagonal(came_ref, at):
    half = came_ref.shape[1] // 2
    upper = came_ref[at:at + half, :]
    corner = came_ref[at + half:at + half + half // 2, :]
    corner = jnp.concatenate([corner[:, :half], corner[:, half:]], 0)
    return jnp.concatenate([upper, jnp.concatenate([upper[:, half:].T, corner], 1)], 0)


def prior_kernel(scale_ref, own_ref, after_ref, full_ref, diagonal_ref, wide_ref):
    cells = own_ref.shape[0]
    quad = my_place()[1]
    on, off = (pl.ds(pl.multiple_of(p * cells, cells), cells) for p in (quad & 1, 1 - (quad & 1)))
    diagonal = own_ref[:, on]
    pack_diagonal(diagonal, diagonal_ref, 0)
    full_ref[:cells, :] = own_ref[:, off]
    pack_diagonal(diagonal, full_ref, cells)
    wide_ref[...] = jnp.full(wide_ref.shape, scale_ref[0], f32)


def gather_kernel(groups, quads, own_ref, *refs):
    came, data = refs[:quads - 1], refs[quads - 1:quads - 1 + groups]
    prior_ref, noise_ref, *streams = refs[quads + groups:]
    me, quad = lax.axis_index("sensor"), my_place()[1]
    sensors, cells = streams[0].shape[1], own_ref.shape[0]
    on, off = (pl.ds(pl.multiple_of(p * cells, cells), cells) for p in (quad & 1, 1 - (quad & 1)))
    for d in range(0, quads, 2):
        diagonal = own_ref[:, on] if d == 0 else unpack_diagonal(came[d - 1], cells)
        beside = own_ref[:, off] if d == 0 else came[d - 1][:cells, :]
        prior_ref[quad ^ d, :, on] = diagonal
        prior_ref[quad ^ d, :, off] = beside
        prior_ref[quad ^ d ^ 1, :, on] = beside.T
        prior_ref[quad ^ d ^ 1, :, off] = unpack_diagonal(came[d], 0)
    row = lax.broadcasted_iota(jnp.int32, (sensors, sensors), 0)
    col = lax.broadcasted_iota(jnp.int32, (sensors, sensors), 1)
    for d in range(groups):
        for s in range(STREAMS):
            streams[s][me ^ d] = data[d][:sensors, s * LANES:(s + 1) * LANES]
        both = data[d][sensors:, :].astype(f32)
        noise_row = both[0:1, :] + both[8:9, :]
        noise = jnp.sum(jnp.where(row == col, noise_row, 0.0), 1, keepdims=True)
        noise_ref[me ^ d] = jnp.broadcast_to(noise, (sensors, LANES))


def source(map_ref, sides_ref, prior_ref, scale):
    groups, quads, _, cells = map_ref.shape
    per_block = prior_ref.shape[2] // cells
    out = []
    for block in range(quads // per_block):
        members = range(block * per_block, (block + 1) * per_block)
        parts = []
        for q in members:
            u = jnp.zeros((sides_ref.shape[1], cells), f32)
            for g in range(groups):
                u += dot(sides_ref[g], map_ref[g, q])
            parts.append(u.astype(bf16))
        ub = jnp.concatenate(parts, 1)
        out += [(dot_nt(prior_ref[q], ub) * scale).astype(bf16) for q in members]
    return out


def sides(z):
    half = z.shape[1] // 2
    return jnp.concatenate([z, jnp.concatenate([z[:, half:], -z[:, :half]], 1)], 0).T


def bring_kernel(map_ref, out_ref, sem):
    copy = pltpu.make_async_copy(map_ref, out_ref, sem)
    copy.start()
    copy.wait()


def step_kernel(stage, n_pred, n_after, scale_ref, map_ref, prior_ref, obs_ref, noise_ref, *refs):
    groups, quads, double, _ = map_ref.shape
    sensors = double // 2
    preds, refs = refs[:n_pred], refs[n_pred + n_after:]
    if stage > 0:
        outs, (sides_ref, now_ref, partial_ref) = refs[:4], refs[4:]
    else:
        out_ref, sides_ref = refs
    for g in range(groups):
        obs = obs_ref[g].astype(f32)
        now = relax_step * obs
        if stage > 0:
            predicted = sum(p[g].astype(f32) for p in preds)
            now = now + relax_step * (obs - predicted - noise_ref[g] * now)
            now_ref[g] = now + relax_step * (obs - noise_ref[g] * now)
        sides_ref[g] = sides(now.astype(bf16))
    sources = source(map_ref, sides_ref, prior_ref, scale_ref[0:1, 0:1])
    turned = [jnp.concatenate([-v[:, HALF:], v[:, :HALF]], 1) for v in sources]
    for g in range(groups):
        total = jnp.zeros((sensors, LANES), f32)
        for q in range(quads):
            total += dot(map_ref[g, q, :sensors, :], sources[q]) + dot(map_ref[g, q, sensors:, :], turned[q])
        if stage == 0:
            out_ref[g] = total.astype(bf16)
        else:
            now_ref[g] -= relax_step * total
            partial_ref[g] = total.astype(bf16)
    if stage > 0:
        for e in range(groups // CORES):
            for parity, core in ((0, my_place()[2]), (1, 1 - my_place()[2])):
                g = CORES * (my_place()[0] ^ e) + core
                outs[parity][e] = partial_ref[g]
                outs[2 + parity][e] = now_ref[g].astype(outs[2 + parity].dtype)


def last_kernel(pairs, *refs):
    mine, theirs, keeps, gots = (refs[i * STREAMS:(i + 1) * STREAMS] for i in range(4))
    *outs, give_ref = refs[4 * STREAMS:]
    core = my_place()[2]
    for e in range(pairs):
        own = join([keeps[s][e] - relax_step * mine[s][e].astype(f32) for s in range(STREAMS)])
        other = join([gots[s][e].astype(f32) - relax_step * theirs[s][e].astype(f32) for s in range(STREAMS)])
        outs[e][core] = own.astype(bf16)
        outs[e][1 - core] = other.astype(bf16)
        give_ref[e] = other.astype(bf16)


def join(streams):
    return jnp.concatenate([x[:, :HALF] for x in streams] + [x[:, HALF:] for x in streams], 1)


def post_kernel(pairs, scale_ref, map_ref, prior_ref, *refs):
    duals, got_ref, refs = refs[:pairs], refs[pairs], refs[pairs + 1:]
    outs, (sides_ref, held_ref) = refs[:-2], refs[-2:]
    core = my_place()[2]
    for e in range(pairs):
        first = CORES * (my_place()[0] ^ e)
        sides_ref[first + core] = sides(duals[e][core])
        sides_ref[first + 1 - core] = sides(got_ref[e])
    for q, v in enumerate(source(map_ref, sides_ref, prior_ref, scale_ref[0:1, 0:1])):
        held_ref[q] = v
    for d, out in enumerate(outs):
        out[...] = held_ref[my_place()[1] ^ d]


def end_kernel(e, quads, members, follows, *refs):
    count = 1 + (e == 0)
    came, refs = refs[:len(members) * count], refs[len(members) * count + follows:]
    outs, (dual_ref, sems, *post) = refs[:count], refs[count:]
    pair, quad, _ = my_place()
    sends = []
    for i, d in enumerate(members):
        for core in range(CORES):
            freq = (CORES * (pair ^ e) + core) * quads + (quad ^ d)
            for part in range(2):
                dual_ref[i, core, part] = came[i][core, :, part * LANES:(part + 1) * LANES].astype(f32)
            sends.append(pltpu.make_async_copy(dual_ref.at[i, core], outs[0].at[freq], sems.at[i, core]))
            sends[-1].start()
        if e == 0:
            post_ref = post[0]
            cells = post_ref.shape[1] // 2
            post_ref[i, pl.ds(0, cells, stride=2), :] = came[len(members) + i][:, :LANES].astype(f32)
            post_ref[i, pl.ds(1, cells, stride=2), :] = came[len(members) + i][:, LANES:].astype(f32)
            sends.append(pltpu.make_async_copy(post_ref.at[i], outs[1].at[quad ^ d], sems.at[i, CORES]))
            sends[-1].start()
    for copy in sends:
        copy.wait()


def on_device(forward_map, observed, noise_var, prior_rows, prior_scale):
    frequencies, halves, sensors, cells = forward_map.shape
    groups, quads, count = (lax.axis_size(a) for a in ("sensor", "quad", "side"))
    width = prior_rows.shape[1]
    me, quad = lax.axis_index("sensor"), lax.axis_index("quad")
    scale = lax.dynamic_slice_in_dim(prior_scale, me * quads + quad, 1, 0)
    both = ("sensor", "quad")

    held = lax.all_to_all(
        forward_map.reshape(frequencies, halves * sensors, cells), both, split_axis=0, concat_axis=0, tiled=True
    ).reshape(groups, quads, halves * sensors, cells)

    data = call(
        functools.partial(data_kernel, groups, quads),
        [ANY, VMEM],
        [shape((sensors + 16, STREAMS * LANES), bf16)] * groups,
        [pltpu.VMEM((groups, halves, sensors, LANES), f32), pltpu.SemaphoreType.DMA((groups,))],
        moved=groups * sensors * LANES * 12,
    )(observed, noise_var.reshape(1, sensors))
    data = [data[0]] + [swap(data[d], "sensor", d) for d in range(1, groups)]
    packed = cells // 2 + cells // 4
    rows, diagonal, scale = call(
        prior_kernel,
        [SMEM, VMEM, ANY],
        [shape((cells + packed, cells), bf16), shape((packed, cells), bf16), shape((8, LANES), f32)],
    )(scale, prior_rows, data[1])
    came = [swap(diagonal if d % 2 else rows, "quad", d) for d in range(1, quads)]
    near = call(bring_kernel, [ANY], [shape(held.shape, bf16)], [pltpu.SemaphoreType.DMA], moved=8 * 2**20)(held)[0]

    prior, noise, *streams = call(
        functools.partial(gather_kernel, groups, quads),
        [VMEM] * (quads + groups) + [ANY],
        [shape((quads, cells, width), bf16), shape((groups, sensors, LANES), f32)]
        + [shape((groups, sensors, LANES), bf16)] * STREAMS,
        moved=8 * 2**20,
    )(prior_rows, *came, *data, near)

    def over_sides(partial):
        if count == 2:
            return [partial, swap(partial, "side", 1)]
        return [lax.psum(partial, "side")]

    wide, narrow = shape((groups, sensors, LANES), f32), shape((groups, sensors, LANES), bf16)

    def step(stage, obs, preds, after=()):
        operands = [scale, near, prior, obs, noise] + preds
        scratch = [pltpu.VMEM((groups, LANES, halves * sensors), bf16)]
        if stage > 0:
            scratch += [pltpu.VMEM((groups, sensors, LANES), f32), pltpu.VMEM((groups, sensors, LANES), bf16)]
        return call(
            functools.partial(step_kernel, stage, len(preds), len(after)),
            [VMEM] * len(operands) + [ANY] * len(after),
            [part, part, shape(part.shape, f32), part] if stage > 0 else [narrow],
            scratch,
            flops=2**31,
            moved=8 * 2**20,
        )(*operands, *after)

    pairs = groups // CORES
    part = shape((pairs, sensors, LANES), bf16)
    partials = [step(0, streams[s], [])[0] for s in range(STREAMS)]
    preds = [over_sides(x) for x in partials]
    steps = [step(1, streams[s], preds[s], partials[s + 1:]) for s in range(STREAMS)]

    def to_other_sides(x, cross):
        if count == 2:
            return lax.ppermute(
                x, ("sensor", "side"), [(i, i ^ (1 + CORES * cross)) for i in range(groups * count)]
            )
        rest = lax.psum(x.astype(f32), "side") - x.astype(f32)
        return (swap(rest, "sensor", 1) if cross else rest).astype(bf16)

    mine = [to_other_sides(x[0], 0) for x in steps]
    theirs = [to_other_sides(x[1], 1) for x in steps]
    keeps, gots = [x[2] for x in steps], [swap(x[3], "sensor", 1) for x in steps]
    message = shape((CORES, sensors, 2 * LANES), bf16)
    *finals, give = call(
        functools.partial(last_kernel, pairs),
        [VMEM] * (4 * STREAMS),
        [message] * pairs + [shape((pairs, sensors, 2 * LANES), bf16)],
        moved=2 * 2**20,
    )(*mine, *theirs, *keeps, *gots)
    got = swap(give, "sensor", 1)
    posts = call(
        functools.partial(post_kernel, pairs),
        [VMEM] * (4 + pairs),
        [shape((cells, 2 * LANES), bf16)] * quads,
        [pltpu.VMEM((groups, 2 * LANES, halves * sensors), bf16), pltpu.VMEM((quads, cells, 2 * LANES), bf16)],
        flops=2**31,
        moved=8 * 2**20,
    )(scale, near, prior, *finals, got)
    duals = {}
    for e in reversed(range(pairs)):
        for d in range(quads):
            low, high = d & 1, d & ~1
            if low and high:
                first, second = (high, low) if e == 0 else (low, high)
                duals[e * quads + d] = swap(duals[e * quads + first], "quad", second)
            else:
                duals[e * quads + d] = swap(finals[e], both, CORES * e * quads + d) if e + d else finals[e]
    posts = [posts[0]] + [swap(posts[d], "quad", d) for d in range(1, quads)]
    far = [(e, list(range(quads))) for e in reversed(range(1, pairs))]
    done = []
    for e, members in far + [(0, list(range(quads - 1))), (0, [quads - 1])]:
        count = len(members)
        out = [shape((frequencies, halves, sensors, LANES), f32)]
        scratch = [
            pltpu.VMEM((count, CORES, halves, sensors, LANES), f32),
            pltpu.SemaphoreType.DMA((count, CORES + 1)),
        ]
        if e == 0:
            out.append(shape((quads, cells * 2, LANES), f32))
            scratch.append(pltpu.VMEM((count, cells * 2, LANES), f32))
        done = call(
            functools.partial(end_kernel, e, quads, members, len(done)),
            [VMEM] * (count * len(out)) + [ANY] * len(done),
            out,
            scratch,
            [ANY] * len(out),
            moved=4 * 2**20,
            aliases={count * len(out) + i: i for i in range(len(done))},
        )(*[duals[e * quads + d] for d in members], *[posts[d] for d in members if e == 0], *done)
    dual, posterior = done
    return dual, posterior.reshape(quads, cells, 2, LANES)


def solution(mesh):
    groups, space = mesh.devices.shape

    def run(forward_map, observed, noise_var, prior_rows, prior_scale):
        quads = forward_map.shape[0] // groups
        split = Mesh(mesh.devices.reshape(groups, space // quads, quads), ("sensor", "side", "quad"))
        return jax.shard_map(
            on_device,
            mesh=split,
            in_specs=(
                P(None, None, "sensor", ("side", "quad")),
                P(None, None, "sensor", None),
                P("sensor"),
                P(("side", "quad"), None),
                P(),
            ),
            out_specs=(P(None, None, "sensor", None), P("sensor", ("side", "quad"), None, None)),
            check_vma=False,
        )(forward_map, observed, noise_var, prior_rows, prior_scale)

    return run
```

```python
import functools

import jax
import jax.numpy as jnp
from jax import lax
from jax.experimental import pallas as pl
from jax.experimental.pallas import tpu as pltpu
from jax.sharding import Mesh, PartitionSpec as P

ITERS = 2
relax_step = 0.25
STREAMS = 2
CORES = 2
LANES = 128
HALF = LANES // 2
VMEM_LIMIT = 16 * 2**20
VMEM = pl.BlockSpec(memory_space=pltpu.VMEM)
SMEM = pl.BlockSpec(memory_space=pltpu.SMEM)
ANY = pl.BlockSpec(memory_space=pl.ANY)
bf16, f32 = jnp.bfloat16, jnp.float32


def shape(dims, dtype):
    return jax.ShapeDtypeStruct(dims, dtype)


def call(kernel, in_specs, out_shape, scratch=(), out_specs=None, flops=0, moved=0, aliases=None):
    return pl.pallas_call(
        kernel,
        input_output_aliases=aliases or {},
        in_specs=in_specs,
        out_specs=out_specs or [VMEM] * len(out_shape),
        out_shape=out_shape,
        scratch_shapes=list(scratch),
        cost_estimate=pl.CostEstimate(flops=flops, bytes_accessed=moved, transcendentals=0),
        compiler_params=pltpu.CompilerParams(vmem_limit_bytes=VMEM_LIMIT),
    )


def swap(x, axes, distance):
    count = lax.axis_size(axes)
    return lax.ppermute(x, axes, [(i, i ^ distance) for i in range(count)])


def dot(a, b):
    return jnp.dot(a, b, preferred_element_type=f32)


def dot_nt(a, b):
    return lax.dot_general(a, b, (((1,), (1,)), ((), ())), preferred_element_type=f32)


def my_place():
    me = lax.axis_index("sensor")
    return me // CORES, lax.axis_index("quad"), me % CORES


def data_kernel(groups, quads, obs_ref, noise_ref, *refs):
    outs, (held, sems) = refs[:groups], refs[groups:]
    sensors = obs_ref.shape[2]
    copies = []
    for d in range(groups):
        freq = ((my_place()[0] * CORES + my_place()[2]) ^ d) * quads + my_place()[1]
        copies.append(pltpu.make_async_copy(obs_ref.at[freq], held.at[d], sems.at[d]))
        copies[-1].start()
    noise = noise_ref[...]
    high = noise.astype(bf16)
    low = (noise - high.astype(f32)).astype(bf16)
    tail = jnp.concatenate([jnp.broadcast_to(high, (8, sensors)), jnp.broadcast_to(low, (8, sensors))], 0)
    for d in range(groups):
        copies[d].wait()
        re, im = held[d, 0], held[d, 1]
        for s in range(STREAMS):
            part = slice(s * HALF, (s + 1) * HALF)
            outs[d][:sensors, s * LANES:(s + 1) * LANES] = jnp.concatenate([re[:, part], im[:, part]], 1).astype(bf16)
        outs[d][sensors:, :] = tail


def pack_diagonal(block, out_ref, at):
    half = block.shape[0] // 2
    out_ref[at:at + half, :] = block[:half]
    corner = block[half:, half:]
    out_ref[at + half:at + half + half // 2, :] = jnp.concatenate([corner[:half // 2], corner[half // 2:]], 1)


def unpack_diagonal(came_ref, at):
    half = came_ref.shape[1] // 2
    upper = came_ref[at:at + half, :]
    corner = came_ref[at + half:at + half + half // 2, :]
    corner = jnp.concatenate([corner[:, :half], corner[:, half:]], 0)
    return jnp.concatenate([upper, jnp.concatenate([upper[:, half:].T, corner], 1)], 0)


def prior_kernel(scale_ref, own_ref, after_ref, full_ref, diagonal_ref, wide_ref):
    cells = own_ref.shape[0]
    quad = my_place()[1]
    on, off = (pl.ds(pl.multiple_of(p * cells, cells), cells) for p in (quad & 1, 1 - (quad & 1)))
    diagonal = own_ref[:, on]
    pack_diagonal(diagonal, diagonal_ref, 0)
    full_ref[:cells, :] = own_ref[:, off]
    pack_diagonal(diagonal, full_ref, cells)
    wide_ref[...] = jnp.full(wide_ref.shape, scale_ref[0], f32)


def gather_kernel(groups, quads, own_ref, *refs):
    came, data = refs[:quads - 1], refs[quads - 1:quads - 1 + groups]
    prior_ref, noise_ref, *streams = refs[quads + groups:]
    me, quad = lax.axis_index("sensor"), my_place()[1]
    sensors, cells = streams[0].shape[1], own_ref.shape[0]
    on, off = (pl.ds(pl.multiple_of(p * cells, cells), cells) for p in (quad & 1, 1 - (quad & 1)))
    for d in range(0, quads, 2):
        diagonal = own_ref[:, on] if d == 0 else unpack_diagonal(came[d - 1], cells)
        beside = own_ref[:, off] if d == 0 else came[d - 1][:cells, :]
        prior_ref[quad ^ d, :, on] = diagonal
        prior_ref[quad ^ d, :, off] = beside
        prior_ref[quad ^ d ^ 1, :, on] = beside.T
        prior_ref[quad ^ d ^ 1, :, off] = unpack_diagonal(came[d], 0)
    row = lax.broadcasted_iota(jnp.int32, (sensors, sensors), 0)
    col = lax.broadcasted_iota(jnp.int32, (sensors, sensors), 1)
    for d in range(groups):
        for s in range(STREAMS):
            streams[s][me ^ d] = data[d][:sensors, s * LANES:(s + 1) * LANES]
        both = data[d][sensors:, :].astype(f32)
        noise_row = both[0:1, :] + both[8:9, :]
        noise = jnp.sum(jnp.where(row == col, noise_row, 0.0), 1, keepdims=True)
        noise_ref[me ^ d] = jnp.broadcast_to(noise, (sensors, LANES))


def source(map_ref, sides_ref, prior_ref, scale):
    groups, quads, _, cells = map_ref.shape
    per_block = prior_ref.shape[2] // cells
    out = []
    for block in range(quads // per_block):
        members = range(block * per_block, (block + 1) * per_block)
        parts = []
        for q in members:
            u = jnp.zeros((sides_ref.shape[1], cells), f32)
            for g in range(groups):
                u += dot(sides_ref[g], map_ref[g, q])
            parts.append(u.astype(bf16))
        ub = jnp.concatenate(parts, 1)
        out += [(dot_nt(prior_ref[q], ub) * scale).astype(bf16) for q in members]
    return out


def sides(z):
    half = z.shape[1] // 2
    return jnp.concatenate([z, jnp.concatenate([z[:, half:], -z[:, :half]], 1)], 0).T


def bring_kernel(map_ref, out_ref, sem):
    copy = pltpu.make_async_copy(map_ref, out_ref, sem)
    copy.start()
    copy.wait()


def step_kernel(stage, n_pred, n_after, scale_ref, map_ref, prior_ref, obs_ref, noise_ref, *refs):
    groups, quads, double, _ = map_ref.shape
    sensors = double // 2
    preds, refs = refs[:n_pred], refs[n_pred + n_after:]
    if stage > 0:
        outs, (sides_ref, now_ref, partial_ref) = refs[:4], refs[4:]
    else:
        out_ref, sides_ref = refs
    for g in range(groups):
        obs = obs_ref[g].astype(f32)
        now = relax_step * obs
        if stage > 0:
            predicted = sum(p[g].astype(f32) for p in preds)
            now = now + relax_step * (obs - predicted - noise_ref[g] * now)
            now_ref[g] = now + relax_step * (obs - noise_ref[g] * now)
        sides_ref[g] = sides(now.astype(bf16))
    sources = source(map_ref, sides_ref, prior_ref, scale_ref[0:1, 0:1])
    turned = [jnp.concatenate([-v[:, HALF:], v[:, :HALF]], 1) for v in sources]
    for g in range(groups):
        total = jnp.zeros((sensors, LANES), f32)
        for q in range(quads):
            total += dot(map_ref[g, q, :sensors, :], sources[q]) + dot(map_ref[g, q, sensors:, :], turned[q])
        if stage == 0:
            out_ref[g] = total.astype(bf16)
        else:
            now_ref[g] -= relax_step * total
            partial_ref[g] = total.astype(bf16)
    if stage > 0:
        for e in range(groups // CORES):
            for parity, core in ((0, my_place()[2]), (1, 1 - my_place()[2])):
                g = CORES * (my_place()[0] ^ e) + core
                outs[parity][e] = partial_ref[g]
                outs[2 + parity][e] = now_ref[g].astype(outs[2 + parity].dtype)


def last_kernel(pairs, *refs):
    mine, theirs, keeps, gots = (refs[i * STREAMS:(i + 1) * STREAMS] for i in range(4))
    *outs, give_ref = refs[4 * STREAMS:]
    core = my_place()[2]
    for e in range(pairs):
        own = join([keeps[s][e] - relax_step * mine[s][e].astype(f32) for s in range(STREAMS)])
        other = join([gots[s][e].astype(f32) - relax_step * theirs[s][e].astype(f32) for s in range(STREAMS)])
        outs[e][core] = own.astype(bf16)
        outs[e][1 - core] = other.astype(bf16)
        give_ref[e] = other.astype(bf16)


def join(streams):
    return jnp.concatenate([x[:, :HALF] for x in streams] + [x[:, HALF:] for x in streams], 1)


def post_kernel(pairs, scale_ref, map_ref, prior_ref, *refs):
    duals, got_ref, refs = refs[:pairs], refs[pairs], refs[pairs + 1:]
    outs, (sides_ref, held_ref) = refs[:-2], refs[-2:]
    core = my_place()[2]
    for e in range(pairs):
        first = CORES * (my_place()[0] ^ e)
        sides_ref[first + core] = sides(duals[e][core])
        sides_ref[first + 1 - core] = sides(got_ref[e])
    for q, v in enumerate(source(map_ref, sides_ref, prior_ref, scale_ref[0:1, 0:1])):
        held_ref[q] = v
    for d, out in enumerate(outs):
        out[...] = held_ref[my_place()[1] ^ d]


def end_kernel(e, quads, members, follows, *refs):
    count = 1 + (e == 0)
    came, refs = refs[:len(members) * count], refs[len(members) * count + follows:]
    outs, (dual_ref, sems, *post) = refs[:count], refs[count:]
    pair, quad, _ = my_place()
    sends = []
    for i, d in enumerate(members):
        for core in range(CORES):
            freq = (CORES * (pair ^ e) + core) * quads + (quad ^ d)
            for part in range(2):
                dual_ref[i, core, part] = came[i][core, :, part * LANES:(part + 1) * LANES].astype(f32)
            sends.append(pltpu.make_async_copy(dual_ref.at[i, core], outs[0].at[freq], sems.at[i, core]))
            sends[-1].start()
        if e == 0:
            post_ref = post[0]
            cells = post_ref.shape[1] // 2
            post_ref[i, pl.ds(0, cells, stride=2), :] = came[len(members) + i][:, :LANES].astype(f32)
            post_ref[i, pl.ds(1, cells, stride=2), :] = came[len(members) + i][:, LANES:].astype(f32)
            sends.append(pltpu.make_async_copy(post_ref.at[i], outs[1].at[quad ^ d], sems.at[i, CORES]))
            sends[-1].start()
    for copy in sends:
        copy.wait()


def on_device(forward_map, observed, noise_var, prior_rows, prior_scale):
    frequencies, halves, sensors, cells = forward_map.shape
    groups, quads, count = (lax.axis_size(a) for a in ("sensor", "quad", "side"))
    width = prior_rows.shape[1]
    me, quad = lax.axis_index("sensor"), lax.axis_index("quad")
    scale = lax.dynamic_slice_in_dim(prior_scale, me * quads + quad, 1, 0)
    both = ("sensor", "quad")

    held = lax.all_to_all(
        forward_map.reshape(frequencies, halves * sensors, cells), both, split_axis=0, concat_axis=0, tiled=True
    ).reshape(groups, quads, halves * sensors, cells)

    data = call(
        functools.partial(data_kernel, groups, quads),
        [ANY, VMEM],
        [shape((sensors + 16, STREAMS * LANES), bf16)] * groups,
        [pltpu.VMEM((groups, halves, sensors, LANES), f32), pltpu.SemaphoreType.DMA((groups,))],
        moved=groups * sensors * LANES * 12,
    )(observed, noise_var.reshape(1, sensors))
    data = [data[0]] + [swap(data[d], "sensor", d) for d in range(1, groups)]
    packed = cells // 2 + cells // 4
    rows, diagonal, scale = call(
        prior_kernel,
        [SMEM, VMEM, ANY],
        [shape((cells + packed, cells), bf16), shape((packed, cells), bf16), shape((8, LANES), f32)],
    )(scale, prior_rows, data[1])
    came = [swap(diagonal if d % 2 else rows, "quad", d) for d in range(1, quads)]
    near = call(bring_kernel, [ANY], [shape(held.shape, bf16)], [pltpu.SemaphoreType.DMA], moved=8 * 2**20)(held)[0]

    prior, noise, *streams = call(
        functools.partial(gather_kernel, groups, quads),
        [VMEM] * (quads + groups) + [ANY],
        [shape((quads, cells, width), bf16), shape((groups, sensors, LANES), f32)]
        + [shape((groups, sensors, LANES), bf16)] * STREAMS,
        moved=8 * 2**20,
    )(prior_rows, *came, *data, near)

    def over_sides(partial):
        if count == 2:
            return [partial, swap(partial, "side", 1)]
        return [lax.psum(partial, "side")]

    wide, narrow = shape((groups, sensors, LANES), f32), shape((groups, sensors, LANES), bf16)

    def step(stage, obs, preds, after=()):
        operands = [scale, near, prior, obs, noise] + preds
        scratch = [pltpu.VMEM((groups, LANES, halves * sensors), bf16)]
        if stage > 0:
            scratch += [pltpu.VMEM((groups, sensors, LANES), f32), pltpu.VMEM((groups, sensors, LANES), bf16)]
        return call(
            functools.partial(step_kernel, stage, len(preds), len(after)),
            [VMEM] * len(operands) + [ANY] * len(after),
            [part, part, shape(part.shape, f32), part] if stage > 0 else [narrow],
            scratch,
            flops=2**31,
            moved=8 * 2**20,
        )(*operands, *after)

    pairs = groups // CORES
    part = shape((pairs, sensors, LANES), bf16)
    partials = [step(0, streams[s], [])[0] for s in range(STREAMS)]
    preds = [over_sides(x) for x in partials]
    steps = [step(1, streams[s], preds[s], partials[s + 1:]) for s in range(STREAMS)]

    def to_other_sides(x, cross):
        if count == 2:
            return lax.ppermute(
                x, ("sensor", "side"), [(i, i ^ (1 + CORES * cross)) for i in range(groups * count)]
            )
        rest = lax.psum(x.astype(f32), "side") - x.astype(f32)
        return (swap(rest, "sensor", 1) if cross else rest).astype(bf16)

    mine = [to_other_sides(x[0], 0) for x in steps]
    theirs = [to_other_sides(x[1], 1) for x in steps]
    keeps, gots = [x[2] for x in steps], [swap(x[3], "sensor", 1) for x in steps]
    message = shape((CORES, sensors, 2 * LANES), bf16)
    *finals, give = call(
        functools.partial(last_kernel, pairs),
        [VMEM] * (4 * STREAMS),
        [message] * pairs + [shape((pairs, sensors, 2 * LANES), bf16)],
        moved=2 * 2**20,
    )(*mine, *theirs, *keeps, *gots)
    got = swap(give, "sensor", 1)
    posts = call(
        functools.partial(post_kernel, pairs),
        [VMEM] * (4 + pairs),
        [shape((cells, 2 * LANES), bf16)] * quads,
        [pltpu.VMEM((groups, 2 * LANES, halves * sensors), bf16), pltpu.VMEM((quads, cells, 2 * LANES), bf16)],
        flops=2**31,
        moved=8 * 2**20,
    )(scale, near, prior, *finals, got)
    duals = {}
    for e in range(pairs):
        for d in range(quads):
            low, high = d & 1, d & ~1
            if low and high:
                first, second = (high, low) if e == 0 else (low, high)
                duals[e * quads + d] = swap(duals[e * quads + first], "quad", second)
            else:
                duals[e * quads + d] = swap(finals[e], both, CORES * e * quads + d) if e + d else finals[e]
    posts = [posts[0]] + [swap(posts[d], "quad", d) for d in range(1, quads)]
    far = [(e, list(range(quads))) for e in reversed(range(1, pairs))]
    done = []
    for e, members in far + [(0, [0, 1]), (0, list(range(2, quads)))]:
        count = len(members)
        out = [shape((frequencies, halves, sensors, LANES), f32)]
        scratch = [
            pltpu.VMEM((count, CORES, halves, sensors, LANES), f32),
            pltpu.SemaphoreType.DMA((count, CORES + 1)),
        ]
        if e == 0:
            out.append(shape((quads, cells * 2, LANES), f32))
            scratch.append(pltpu.VMEM((count, cells * 2, LANES), f32))
        done = call(
            functools.partial(end_kernel, e, quads, members, len(done)),
            [VMEM] * (count * len(out)) + [ANY] * len(done),
            out,
            scratch,
            [ANY] * len(out),
            moved=4 * 2**20,
            aliases={count * len(out) + i: i for i in range(len(done))},
        )(*[duals[e * quads + d] for d in members], *[posts[d] for d in members if e == 0], *done)
    dual, posterior = done
    return dual, posterior.reshape(quads, cells, 2, LANES)


def solution(mesh):
    groups, space = mesh.devices.shape

    def run(forward_map, observed, noise_var, prior_rows, prior_scale):
        quads = forward_map.shape[0] // groups
        split = Mesh(mesh.devices.reshape(groups, space // quads, quads), ("sensor", "side", "quad"))
        return jax.shard_map(
            on_device,
            mesh=split,
            in_specs=(
                P(None, None, "sensor", ("side", "quad")),
                P(None, None, "sensor", None),
                P("sensor"),
                P(("side", "quad"), None),
                P(),
            ),
            out_specs=(P(None, None, "sensor", None), P("sensor", ("side", "quad"), None, None)),
            check_vma=False,
        )(forward_map, observed, noise_var, prior_rows, prior_scale)

    return run
```
